512 devices in a mesh: member: 8 (over y, core), dp: 32 (over z, x_lo), tensor: 2 (over x_hi).
Axes of the slice: x: 4 (x_hi: 2, x_lo: 2; x = x_hi * 2 + x_lo), y: 4, z: 16, core: 2. Of those that a mesh axis runs over, the one named last changes fastest.
Arguments:
- context: bfloat16 [8, 32, 128, 2560], P('member', 'dp', None, 'tensor')
- out_weight: bfloat16 [8, 5120, 2560], P('member', 'dp', 'tensor')
- first_moment: float32 [8, 5120, 2560], P('member', 'dp', 'tensor'), may hold values from -0.75 to 0.75
- second_moment: float32 [8, 5120, 2560], P('member', 'dp', 'tensor'), may hold values from 0.001 to 0.01
- target: bfloat16 [8, 32, 128, 5120], P('member', None, 'tensor', 'dp'), may hold values from -6 to 6
- token_ids: int32 [8, 32, 128], P('member'), may hold values from 0 to 31999, as said below
- base_lr: float32 [8], replicated, may hold values from 0.02 to 0.2
- perturb_index: int32 [8], replicated, may hold values from 0 to 8
- partner: int32 [8, 32], P(None, 'dp'), may hold values from 0 to 7, as said below
Outputs:
- new_weight: bfloat16 [8, 5120, 2560], P('member', 'dp', 'tensor')
- new_first: float32 [8, 5120, 2560], P('member', 'dp', 'tensor')
- new_second: float32 [8, 5120, 2560], P('member', 'dp', 'tensor')
The draws below stay inside these ranges and needn't reach their ends.
Inputs may be any that keep to these rules, and one draw needn't show every extreme that they name: `token_ids`: 0 marks padding; in each window of 128 tokens the padding, if any, is the final run and covers at most half of the window; the largest id occurs. `partner`: in each slab s, every member names itself except the losers of that slab; each loser names a different member, and a named member names itself.
All inputs are finite; a program needn't handle non-finite values.
Results may differ from the reference program's by a relative error of at most 0.0021.
Values may be sent and summed in bfloat16 or wider, within the bound.
A program may use at most 128 MiB of HBM per device.

```python
import math
import jax
import jax.numpy as jnp
from jax import lax

D = 5120
VOCAB = 32000
HW = 2560
TOK_DEV = 128
MEMBERS = 8
SEQS = 32


def draw_context(key, part):
    key = jax.random.fold_in(key, 1)
    first_key, second_key = jax.random.split(key)
    shape = (MEMBERS, SEQS, TOK_DEV, HW)
    base = jax.random.normal(first_key, shape, jnp.float32)
    spread = jax.random.uniform(second_key, (MEMBERS, SEQS, TOK_DEV, 1), jnp.float32, 0.0, math.log(10.0))
    return (base * jnp.exp(spread)).astype(jnp.bfloat16)


def draw_out_weight(key, part):
    key = jax.random.fold_in(key, 2)
    first_key, second_key = jax.random.split(key)
    shape = (MEMBERS, D, HW)
    base = 0.4 * jax.random.normal(first_key, shape, jnp.float32)
    column_scale = 10.0 ** (jnp.arange(D, dtype=jnp.float32) / D)
    rough = jax.random.uniform(second_key, (MEMBERS, D, 1), jnp.float32, 1.0, 2.0)
    return (base * column_scale[None, :, None] * rough).astype(jnp.bfloat16)


def draw_token_ids(key, part):
    key = jax.random.fold_in(key, 3)
    first_key, second_key = jax.random.split(key)
    words = jax.random.randint(first_key, (MEMBERS, SEQS, TOK_DEV), 1, VOCAB)
    words = words.at[0, 0, 0].set(VOCAB - 1)
    padding = jax.random.randint(second_key, (MEMBERS, SEQS, 1), 0, TOK_DEV // 2 + 1)
    position = jnp.arange(TOK_DEV)[None, None, :]
    return jnp.where(position < TOK_DEV - padding, words, 0).astype(jnp.int32)


def slab_matching(key):
    order = jax.random.permutation(key, MEMBERS).astype(jnp.int32)
    count = max(MEMBERS // 4, 1)
    itself = jnp.arange(MEMBERS, dtype=jnp.int32)
    return itself.at[order[MEMBERS - count:]].set(order[:count])


def draw_partner(key, part):
    key = jax.random.fold_in(key, 4)
    slab_keys = jax.random.split(key, SEQS)
    columns = jax.vmap(slab_matching)(slab_keys)
    return columns.T.astype(jnp.int32)


def with_ends(drawn, stream_key, least, high):
    longest = drawn.shape.index(max(drawn.shape))
    spots = []
    for shift in (0, 1):
        where = [jax.random.randint(jax.random.fold_in(stream_key, axis), (), 0, length) for axis, length in enumerate(drawn.shape)]
        where[longest] = (where[longest] + shift) % drawn.shape[longest]
        spots.append(tuple(where))
    return drawn.at[spots[0]].set(least).at[spots[1]].set(high)


def block_scale(own_key, dims, pieces, low, largest):
    loudness, own = 1.0, jax.random.fold_in(own_key, 6)
    for axis_at, blocks in pieces:
        steps = jnp.exp(jax.random.uniform(jax.random.fold_in(own, axis_at), (blocks,), jnp.float32, low / len(pieces), largest / len(pieces)))
        loudness = loudness * jnp.repeat(steps, dims[axis_at] // blocks).reshape([-1 if axis == axis_at else 1 for axis in range(len(dims))])
    return loudness


def gaussian(key, extent, deviation, bound, shards=(), held_as=jnp.bfloat16):
    gain = block_scale(key, extent, shards, -0.22, 0.18) if shards else 1.0
    values = jax.random.normal(key, extent, jnp.float32) * deviation * gain
    return jnp.minimum(jnp.maximum(values, -bound), bound).astype(held_as)


def setup_inputs(seed: int = 0) -> dict:
    streams_of = jax.random.split(jax.random.key(seed), 10)
    context = draw_context(jax.random.fold_in(streams_of[9], 71), 0)
    out_weight = draw_out_weight(jax.random.fold_in(streams_of[9], 71), 0)
    first_moment = gaussian(streams_of[2], (MEMBERS, D, HW), 0.05, 0.75, ((0, 8), (1, 32), (2, 2)), jnp.float32)
    second_moment = jnp.clip(jnp.exp(math.log(0.01) - 2.30258502 * jax.random.uniform(streams_of[3], (MEMBERS, D, HW), jnp.float32) ** block_scale(streams_of[3], (MEMBERS, D, HW), ((0, 8), (1, 32), (2, 2)), -0.2, 0.2)), 0.001, 0.01)
    target = gaussian(streams_of[4], (MEMBERS, SEQS, TOK_DEV, D), 1.0, 6.0, ((0, 8), (2, 2), (3, 32)))
    token_ids = draw_token_ids(jax.random.fold_in(streams_of[9], 71), 0)
    base_lr = jnp.clip(jnp.exp(jax.random.uniform(streams_of[6], (MEMBERS,), jnp.float32, math.log(0.02), math.log(0.2))), 0.02, 0.2)
    perturb_index = with_ends(jax.random.randint(streams_of[7], (MEMBERS,), 0, 9), jax.random.fold_in(streams_of[7], 1), 0, 8).astype(jnp.int32)
    partner = draw_partner(jax.random.fold_in(streams_of[9], 71), 0)
    return dict(context=context, out_weight=out_weight, first_moment=first_moment, second_moment=second_moment, target=target, token_ids=token_ids, base_lr=base_lr, perturb_index=perturb_index, partner=partner)


beta_one = 0.9
beta_two = 0.95
norm_eps = 1e-05
adam_eps = 1e-08

def member_moments(inputs):
    context, weight, first, second, target, token_ids = inputs
    scaling = 1.0 / math.sqrt(HW)
    matrix = context.reshape(-1, HW)
    goal = target.reshape(-1, D).astype(jnp.float32)
    loss_mask = (token_ids.reshape(-1) != 0).astype(jnp.float32)
    outputs = jnp.dot(matrix, weight.T, preferred_element_type=jnp.float32) * scaling
    squares = lax.optimization_barrier(jnp.sum(outputs * outputs, axis=1))
    cross_sums = lax.optimization_barrier(jnp.sum(goal * outputs, axis=1))
    inverse = lax.rsqrt(squares / D + norm_eps)
    projection = loss_mask * (inverse * inverse * squares - inverse * cross_sums) / D
    normed = outputs * inverse[:, None]
    hidden_grad = loss_mask[:, None] * (normed - goal)
    grad_out = (inverse[:, None] * (hidden_grad - normed * projection[:, None])).astype(jnp.bfloat16)
    gradient = jnp.dot(grad_out.T, matrix, preferred_element_type=jnp.float32) * scaling
    first_new = beta_one * first + (1.0 - beta_one) * gradient
    second_new = beta_two * second + (1.0 - beta_two) * gradient * gradient
    return (first_new, second_new)

def slab_pick(values, partner):
    shaped = values.reshape(MEMBERS, SEQS, D // SEQS, HW)
    picked = jnp.take_along_axis(shaped, partner[:, :, None, None].astype(jnp.int32), axis=0)
    return picked.reshape(MEMBERS, D, HW)

def reference(context, out_weight, first_moment, second_moment, target, token_ids, base_lr, perturb_index, partner):
    first_new, second_new = lax.map(member_moments, (context, out_weight, first_moment, second_moment, target, token_ids))
    step_sizes = base_lr * 2.0 ** ((perturb_index.astype(jnp.float32) - 4.0) / 4.0)
    stepped = (out_weight.astype(jnp.float32) - step_sizes[:, None, None] * first_new / (jnp.sqrt(second_new) + adam_eps)).astype(jnp.bfloat16)
    return (slab_pick(stepped, partner), slab_pick(first_new, partner), slab_pick(second_new, partner))
```

```python
import math

import jax
import jax.numpy as jnp
from jax import lax
from jax.experimental import pallas as pl
from jax.experimental.pallas import tpu as pltpu
from jax.sharding import PartitionSpec as P

D = 5120
HW = 2560
MEMBERS = 8
ZN = 16
YN = 4
ROWS = 160
COLS = 1280
HALF = 80
TOK = 64
SLOTS = 8
CB = 256
NB = COLS // CB
SCALING = 1.0 / math.sqrt(HW)

beta_one = 0.9
beta_two = 0.95
norm_eps = 1e-05
adam_eps = 1e-08

MESH = pl.DeviceIdType.MESH
F32 = jnp.float32
BF16 = jnp.bfloat16


def remote(src, dst, send_sem, recv_sem, device):
    return pltpu.make_async_remote_copy(
        src_ref=src,
        dst_ref=dst,
        send_sem=send_sem,
        recv_sem=recv_sem,
        device_id=device,
        device_id_type=MESH,
    )


def gradient_kernel(
    ctx,
    w,
    m,
    v,
    tgt,
    ids,
    gall,
    wall,
    mall,
    vall,
    xbuf,
    wbuf,
    tbuf,
    eye,
    yt,
    gt,
    dyt,
    stat,
    early,
    late_out,
    late,
    tot,
    pbuf,
    r1,
    r2,
    rout,
    loc,
    in_s,
    in_r,
    z_s,
    z_r,
    e_s,
    e_r,
    l_s,
    l_r,
    st_s,
    st_r,
    x_s,
    x_r,
    y_s,
    y_r,
    y_l,
):
    mem = lax.axis_index("member")
    dp = lax.axis_index("dp")
    ten = lax.axis_index("tensor")
    yy, core = mem // 2, mem % 2
    zz, xl = dp // 2, dp % 2

    def at_z(k):
        return (mem, lax.rem(zz + k, ZN) * 2 + xl, ten)

    def member_at(k):
        return lax.rem(yy + k, YN) * 2 + core

    right, left = at_z(1), at_z(ZN - 1)
    dev_a = (mem, zz * 2 + 1 - xl, ten)
    dev_b = (mem, zz * 2 + 1 - xl, 1 - ten)
    dev_c = (mem, dp, 1 - ten)
    up_m, down_m, far_m = member_at(1), member_at(YN - 1), member_at(2)
    sib_m = yy * 2 + 1 - core
    up, down, sib = (up_m, dp, ten), (down_m, dp, ten), (sib_m, dp, ten)

    own_rows = ctx.at[pl.ds(pl.multiple_of(ten * TOK, TOK), TOK)]
    other_rows = ctx.at[pl.ds(pl.multiple_of((1 - ten) * TOK, TOK), TOK)]

    locals_ = [
        pltpu.make_async_copy(own_rows, xbuf.at[0, 0, 0], loc.at[0]),
        pltpu.make_async_copy(w, wbuf.at[0, 0], loc.at[1]),
        pltpu.make_async_copy(tgt.at[:, xl], tbuf.at[0], loc.at[2]),
        pltpu.make_async_copy(w, wall.at[mem], loc.at[3]),
        pltpu.make_async_copy(m, mall.at[mem], loc.at[4]),
        pltpu.make_async_copy(v, vall.at[mem], loc.at[5]),
    ]
    for copy in locals_:
        copy.start()

    barrier = pltpu.get_barrier_semaphore()

    def greet(k, _):
        pl.semaphore_signal(barrier, inc=1, device_id=at_z(k), device_id_type=MESH)
        return 0

    lax.fori_loop(1, ZN, greet, 0)
    for device in (dev_a, dev_b, dev_c, up, down, sib):
        pl.semaphore_signal(barrier, inc=1, device_id=device, device_id_type=MESH)
    pl.semaphore_wait(barrier, ZN - 1 + 6)

    swap = remote(other_rows, xbuf.at[1, 0, 0], in_s.at[0], in_r.at[0], dev_c)
    swap.start()

    def ring(h, s, d):
        dst = xbuf.at[h, lax.rem(s + 1, SLOTS), d if d else s // (SLOTS - 1)]
        return remote(
            xbuf.at[h, s, d],
            dst,
            z_s.at[d, h, s],
            z_r.at[d, h, lax.rem(s + 1, SLOTS)],
            left if d else right,
        )

    def first(h, d, src):
        return remote(
            src, xbuf.at[h, 1, d], z_s.at[d, h, 0], z_r.at[d, h, 1], left if d else right
        )

    for d in (0, 1):
        first(0, d, own_rows).start()
    inputs = [
        remote(w, wbuf.at[0, 1], in_s.at[1], in_r.at[1], dev_a),
        remote(w, wbuf.at[1, 1], in_s.at[2], in_r.at[2], dev_b),
        remote(w, wbuf.at[1, 0], in_s.at[3], in_r.at[3], dev_c),
        remote(tgt.at[:, 1 - xl], tbuf.at[1], in_s.at[4], in_r.at[4], dev_a),
    ]
    for copy in inputs:
        copy.start()

    state = [(w, wall), (m, mall), (v, vall)]

    def state_first(i, src, dst):
        return [
            remote(src, dst.at[mem], st_s.at[i, 0], st_r.at[i, 0], up),
            remote(src, dst.at[mem], st_s.at[i, 1], st_r.at[i, 1], down),
            remote(src, dst.at[mem], st_s.at[i, 2], st_r.at[i, 2], sib),
        ]

    def state_on(i, dst):
        low, high = pl.ds(0, HALF), pl.ds(HALF, HALF)
        return [
            remote(dst.at[down_m, low], dst.at[down_m, low], st_s.at[i, 3], st_r.at[i, 3], up),
            remote(dst.at[up_m, high], dst.at[up_m, high], st_s.at[i, 4], st_r.at[i, 4], down),
            remote(dst.at[down_m], dst.at[down_m], st_s.at[i, 5], st_r.at[i, 5], sib),
            remote(dst.at[up_m], dst.at[up_m], st_s.at[i, 6], st_r.at[i, 6], sib),
        ]

    def state_last(i, dst):
        return remote(dst.at[far_m], dst.at[far_m], st_s.at[i, 7], st_r.at[i, 7], sib)

    for i, (src, dst) in enumerate(state):
        for copy in state_first(i, src, dst):
            copy.start()

    eye[...] = (
        lax.broadcasted_iota(jnp.int32, (ROWS, ROWS), 0)
        == lax.broadcasted_iota(jnp.int32, (ROWS, ROWS), 1)
    ).astype(BF16)
    stat[...] = jnp.zeros_like(stat)
    lane = lax.broadcasted_iota(jnp.int32, (1, 2 * TOK), 1)
    low_lanes = lane < TOK

    swap.wait_recv()
    for d in (0, 1):
        first(1, d, xbuf.at[1, 0, 0]).start()
    for copy in locals_:
        copy.wait()

    def chunks_of(s):
        one = lax.rem(zz - s + ZN, ZN)
        two = lax.rem(zz + jnp.where(s == 0, SLOTS, s), ZN)
        return one, two

    def project(s):
        one, two = chunks_of(s)
        total = None
        for h in (0, 1):
            part = lax.dot_general(
                wbuf[h].reshape(2 * ROWS, COLS),
                xbuf[h, s].reshape(2 * TOK, COLS),
                (((1,), (1,)), ((), ())),
                preferred_element_type=F32,
            )
            total = part if total is None else total + part
        out = total * SCALING
        yt[s] = out
        goal = jnp.concatenate(
            [
                lax.dot_general(
                    eye[...],
                    jnp.concatenate([tbuf[side, one], tbuf[side, two]], axis=0),
                    (((1,), (1,)), ((), ())),
                    preferred_element_type=F32,
                )
                for side in (0, 1)
            ],
            axis=0,
        )
        gt[s] = goal
        squares = jnp.sum(out * out, axis=0, keepdims=True)
        crosses = jnp.sum(goal * out, axis=0, keepdims=True)
        row_one = jnp.where(low_lanes, squares, pltpu.roll(crosses, TOK, 1))
        row_two = jnp.where(low_lanes, pltpu.roll(squares, TOK, 1), crosses)
        return one, two, row_one, row_two

    def project_early(s, _):
        one, two, row_one, row_two = project(s)
        stat[pl.ds(one, 1), :] = row_one
        stat[pl.ds(two, 1), :] = row_two
        return 0

    def done_by(s):
        return jnp.minimum(jnp.maximum(2 * (s - 3), 0), SLOTS - 1)

    def gather_step(s, _):
        for h in (0, 1):
            for d in (0, 1):
                remote(
                    xbuf.at[h, s, d], xbuf.at[h, s, d], z_s.at[d, h, s], z_r.at[d, h, s], right
                ).wait_recv()
                if d == h:
                    ring(h, s, d).start()
                else:

                    @pl.when(s < SLOTS - 1)
                    def _():
                        ring(h, s, d).start()

        @pl.when(s == 4)
        def _():
            for copy in inputs:
                copy.wait_recv()

        lax.fori_loop(done_by(s - 1) + 1, done_by(s) + 1, project_early, 0)
        return 0

    lax.fori_loop(1, SLOTS, gather_step, 0)

    def early_copy(k):
        return remote(stat, early.at[zz], e_s.at[k], e_r.at[zz], at_z(k))

    def late_copy(k):
        return remote(late_out, late.at[zz], l_s.at[k], l_r.at[zz], at_z(k))

    def send_early(k, _):
        early_copy(k).start()
        return 0

    lax.fori_loop(1, ZN, send_early, 0)
    early[zz] = stat[...]

    for h in (0, 1):
        remote(
            xbuf.at[h, 0, 1], xbuf.at[h, 0, 1], z_s.at[h, h, 0], z_r.at[h, h, 0], right
        ).wait_recv()
    _, _, row_one, row_two = project(0)
    late_out[pl.ds(0, 1), :] = row_one
    late_out[pl.ds(1, 1), :] = row_two

    def send_late(k, _):
        late_copy(k).start()
        return 0

    lax.fori_loop(1, ZN, send_late, 0)
    late[zz] = late_out[...]

    for i, (src, dst) in enumerate(state):
        for copy in state_first(i, src, dst):
            copy.wait_recv()
        for copy in state_on(i, dst):
            copy.start()

    def take_early(k, total):
        src = lax.rem(zz + k, ZN)
        remote(stat, early.at[src], e_s.at[k], e_r.at[src], right).wait_recv()
        return total + early[src]

    tot[...] = lax.fori_loop(1, ZN, take_early, stat[...])

    def take_late(k, _):
        src = lax.rem(zz + k, ZN)
        remote(late_out, late.at[src], l_s.at[k], l_r.at[src], right).wait_recv()
        return 0

    lax.fori_loop(1, ZN, take_late, 0)

    def add_late(c, _):
        opposite = lax.rem(c + SLOTS, ZN)
        tot[pl.ds(c, 1), :] = (
            tot[pl.ds(c, 1), :] + late[c, pl.ds(0, 1), :] + late[opposite, pl.ds(1, 1), :]
        )
        return 0

    lax.fori_loop(0, ZN, add_late, 0)

    def window_mask(c):
        row = ids[pl.ds(2 * c + xl, 1), :]
        return jnp.where(row != 0, 1.0, 0.0)

    def out_gradient(s, _):
        one, two = chunks_of(s)
        row_one, row_two = tot[pl.ds(one, 1), :], tot[pl.ds(two, 1), :]
        squares = jnp.where(low_lanes, row_one, pltpu.roll(row_two, TOK, 1))
        crosses = jnp.where(low_lanes, pltpu.roll(row_one, TOK, 1), row_two)
        mask_one, mask_two = window_mask(one), window_mask(two)
        first_half = jnp.where(low_lanes, mask_one, pltpu.roll(mask_two, TOK, 1))
        second_half = jnp.where(low_lanes, pltpu.roll(mask_one, TOK, 1), mask_two)
        mask = jnp.where(ten == 0, first_half, second_half)
        inverse = lax.rsqrt(squares / D + norm_eps)
        projection = mask * (inverse * inverse * squares - inverse * crosses) / D
        normed = yt[s] * inverse
        hidden = mask * (normed - gt[s])
        grad_out = inverse * (hidden - normed * projection)
        dyt[:, pl.ds(pl.multiple_of(s * 2 * TOK, 2 * TOK), 2 * TOK)] = grad_out.astype(BF16)
        return 0

    lax.fori_loop(0, SLOTS, out_gradient, 0)

    low, high = pl.ds(0, HALF), pl.ds(HALF, HALF)

    def hop_one(j):
        return [
            remote(pbuf.at[j, 1, 0, low], r1.at[0, j], x_s.at[0, j], x_r.at[0, j], dev_a),
            remote(pbuf.at[j, 1, 0, high], r1.at[1, j], x_s.at[1, j], x_r.at[1, j], dev_b),
        ]

    def hop_two(j):
        return [
            remote(pbuf.at[j, 0, 1], r2.at[0, j], x_s.at[2, j], x_r.at[2, j], dev_a),
            remote(pbuf.at[j, 1, 1], r2.at[1, j], x_s.at[3, j], x_r.at[3, j], dev_b),
        ]

    def y_local(j):
        return pltpu.make_async_copy(rout.at[j], gall.at[mem, j], y_l.at[j])

    def y_first(j):
        return [
            remote(rout.at[j], gall.at[mem, j], y_s.at[0, j], y_r.at[0, j], up),
            remote(rout.at[j], gall.at[mem, j], y_s.at[1, j], y_r.at[1, j], down),
            remote(rout.at[j], gall.at[mem, j], y_s.at[2, j], y_r.at[2, j], sib),
        ]

    def y_on(j):
        one, two = gall.at[down_m, j], gall.at[up_m, j]
        return [
            remote(one.at[low], one.at[low], y_s.at[3, j], y_r.at[3, j], up),
            remote(two.at[high], two.at[high], y_s.at[4, j], y_r.at[4, j], down),
            remote(one, one, y_s.at[5, j], y_r.at[5, j], sib),
            remote(two, two, y_s.at[6, j], y_r.at[6, j], sib),
        ]

    def y_last(j):
        return remote(gall.at[far_m, j], gall.at[far_m, j], y_s.at[7, j], y_r.at[7, j], sib)

    def far_halves(ref, sems):
        return [
            remote(ref.at[low], ref.at[low], sems[0], sems[1], up),
            remote(ref.at[high], ref.at[high], sems[2], sems[3], up),
        ]

    def stage(step, behind, run):
        j = step - behind

        @pl.when(jnp.logical_and(j >= 0, j < NB))
        def _():
            run(j)

    def multiply(j):
        cols = pl.ds(pl.multiple_of(j * CB, CB), CB)
        for h in (1, 0):
            part = jnp.dot(
                dyt[...],
                xbuf[h, :, :, :, cols].reshape(2 * SLOTS * TOK, CB),
                preferred_element_type=F32,
            )
            pbuf[j, h] = (part * SCALING).reshape(2, ROWS, CB)
        for copy in hop_one(j):
            copy.start()

    def add_one(j):
        for copy in hop_one(j):
            copy.wait_recv()
        pbuf[j, 1, 1, low] = pbuf[j, 1, 1, low] + r1[0, j]
        pbuf[j, 0, 1, high] = pbuf[j, 0, 1, high] + r1[1, j]
        for copy in hop_two(j):
            copy.start()

    def add_two(j):
        for copy in hop_two(j):
            copy.wait_recv()
        rout[j] = pbuf[j, 0, 0] + r2[0, j] + r2[1, j]
        y_local(j).start()
        for copy in y_first(j):
            copy.start()

    def pass_on(j):
        for copy in y_first(j):
            copy.wait_recv()
        for copy in y_on(j):
            copy.start()

    def pass_last(j):
        for copy in y_on(j):
            copy.wait_recv()
        y_last(j).start()

    def finish(j):
        y_last(j).wait_recv()
        y_local(j).wait()
        for copy in hop_one(j) + hop_two(j) + y_first(j) + y_on(j) + [y_last(j)]:
            copy.wait_send()

    def pipeline_step(step, _):
        for behind, run in enumerate((multiply, add_one, add_two, pass_on, pass_last, finish)):
            stage(step, behind, run)
        return 0

    lax.fori_loop(0, NB + 5, pipeline_step, 0)

    for i, (src, dst) in enumerate(state):
        for copy in state_on(i, dst):
            copy.wait_recv()
        state_last(i, dst).start()
    for i, (src, dst) in enumerate(state):
        state_last(i, dst).wait_recv()
        for copy in state_first(i, src, dst) + state_on(i, dst) + [state_last(i, dst)]:
            copy.wait_send()
    swap.wait_send()
    for copy in inputs:
        copy.wait_send()
    for d in (0, 1):
        first(0, d, own_rows).wait_send()
        first(1, d, xbuf.at[1, 0, 0]).wait_send()

    def drain_ring(s, _):
        for h in (0, 1):
            for d in (0, 1):
                if d == h:
                    ring(h, s, d).wait_send()
                else:

                    @pl.when(s < SLOTS - 1)
                    def _():
                        ring(h, s, d).wait_send()

        return 0

    lax.fori_loop(1, SLOTS, drain_ring, 0)

    def drain_stats(k, _):
        early_copy(k).wait_send()
        late_copy(k).wait_send()
        return 0

    lax.fori_loop(1, ZN, drain_stats, 0)


def gather_gradients(ctx, w, m, v, tgt, ids):
    anywhere = pl.BlockSpec(memory_space=pl.ANY)
    dma = pltpu.SemaphoreType.DMA
    vmem = pltpu.VMEM
    return pl.pallas_call(
        gradient_kernel,
        out_shape=(
            jax.ShapeDtypeStruct((MEMBERS, NB, ROWS, CB), F32),
            jax.ShapeDtypeStruct((MEMBERS, ROWS, COLS), BF16),
            jax.ShapeDtypeStruct((MEMBERS, ROWS, COLS), F32),
            jax.ShapeDtypeStruct((MEMBERS, ROWS, COLS), F32),
        ),
        in_specs=[anywhere] * 5 + [pl.BlockSpec(memory_space=pltpu.VMEM)],
        out_specs=(anywhere,) * 4,
        scratch_shapes=[
            vmem((2, SLOTS, 2, TOK, COLS), BF16),
            vmem((2, 2, ROWS, COLS), BF16),
            vmem((2, ZN, TOK, ROWS), BF16),
            vmem((ROWS, ROWS), BF16),
            vmem((SLOTS, 2 * ROWS, 2 * TOK), F32),
            vmem((SLOTS, 2 * ROWS, 2 * TOK), F32),
            vmem((2 * ROWS, SLOTS * 2 * TOK), BF16),
            vmem((ZN, 2 * TOK), F32),
            vmem((ZN, ZN, 2 * TOK), F32),
            vmem((2, 2 * TOK), F32),
            vmem((ZN, 2, 2 * TOK), F32),
            vmem((ZN, 2 * TOK), F32),
            vmem((NB, 2, 2, ROWS, CB), F32),
            vmem((2, NB, HALF, CB), F32),
            vmem((2, NB, ROWS, CB), F32),
            vmem((NB, ROWS, CB), F32),
            dma((6,)),
            dma((5,)),
            dma((5,)),
            dma((2, 2, SLOTS)),
            dma((2, 2, SLOTS)),
            dma((ZN,)),
            dma((ZN,)),
            dma((ZN,)),
            dma((ZN,)),
            dma((3, 8)),
            dma((3, 8)),
            dma((4, NB)),
            dma((4, NB)),
            dma((8, NB)),
            dma((8, NB)),
            dma((NB,)),
        ],
        compiler_params=pltpu.CompilerParams(
            collective_id=0, has_side_effects=True, vmem_limit_bytes=56 * 1024 * 1024
        ),
        cost_estimate=pl.CostEstimate(
            flops=4 * 1024 * HW * 2 * ROWS, bytes_accessed=20_000_000, transcendentals=0
        ),
    )(ctx, w, m, v, tgt, ids)


def update_kernel(pick, rate_of, level_of, g, w, m, v, new_w, new_m, new_v):
    p = pick[0]
    level = jnp.full((8, CB), level_of[p].astype(F32), F32)
    step_size = (rate_of[p] * 2.0 ** ((level - 4.0) / 4.0))[:1]
    gradient = g[0, 0]
    first = beta_one * m[0] + (1.0 - beta_one) * gradient
    second = beta_two * v[0] + (1.0 - beta_two) * gradient * gradient
    new_w[...] = (w[0].astype(F32) - step_size * first / (jnp.sqrt(second) + adam_eps)).astype(BF16)
    new_m[...] = first
    new_v[...] = second


def update(pick, base_lr, perturb_index, gall, wall, mall, vall):
    def member_block(j, pick, rate, level):
        return (pick[0], 0, j)

    def own_block(j, pick, rate, level):
        return (0, j)

    return pl.pallas_call(
        update_kernel,
        out_shape=(
            jax.ShapeDtypeStruct((ROWS, COLS), BF16),
            jax.ShapeDtypeStruct((ROWS, COLS), F32),
            jax.ShapeDtypeStruct((ROWS, COLS), F32),
        ),
        grid_spec=pltpu.PrefetchScalarGridSpec(
            num_scalar_prefetch=3,
            grid=(NB,),
            in_specs=[
                pl.BlockSpec((1, 1, ROWS, CB), lambda j, pick, rate, level: (pick[0], j, 0, 0)),
                pl.BlockSpec((1, ROWS, CB), member_block),
                pl.BlockSpec((1, ROWS, CB), member_block),
                pl.BlockSpec((1, ROWS, CB), member_block),
            ],
            out_specs=(
                pl.BlockSpec((ROWS, CB), own_block),
                pl.BlockSpec((ROWS, CB), own_block),
                pl.BlockSpec((ROWS, CB), own_block),
            ),
        ),
    )(pick, base_lr, perturb_index, gall, wall, mall, vall)


def body(
    context,
    out_weight,
    first_moment,
    second_moment,
    target,
    token_ids,
    base_lr,
    perturb_index,
    partner,
):
    gall, wall, mall, vall = gather_gradients(
        context[0, 0],
        out_weight[0],
        first_moment[0],
        second_moment[0],
        target[0].reshape(ZN, 2, TOK, ROWS),
        token_ids[0],
    )
    pick = lax.dynamic_slice(partner[:, 0], (lax.axis_index("member"),), (1,))
    new_weight, new_first, new_second = update(pick, base_lr, perturb_index, gall, wall, mall, vall)
    return (new_weight[None], new_first[None], new_second[None])


def solution(mesh):
    return jax.shard_map(
        body,
        mesh=mesh,
        in_specs=(
            P("member", "dp", None, "tensor"),
            P("member", "dp", "tensor"),
            P("member", "dp", "tensor"),
            P("member", "dp", "tensor"),
            P("member", None, "tensor", "dp"),
            P("member", None, None),
            P(),
            P(),
            P(None, "dp"),
        ),
        out_specs=(
            P("member", "dp", "tensor"),
            P("member", "dp", "tensor"),
            P("member", "dp", "tensor"),
        ),
        check_vma=False,
    )
```

```python
import math

import jax
import jax.numpy as jnp
from jax import lax
from jax.experimental import pallas as pl
from jax.experimental.pallas import tpu as pltpu
from jax.sharding import PartitionSpec as P

D = 5120
HW = 2560
MEMBERS = 8
ZN = 16
YN = 4
ROWS = 160
COLS = 1280
HALF = 80
TOK = 64
SLOTS = 8
CB = 256
NB = COLS // CB
SCALING = 1.0 / math.sqrt(HW)

beta_one = 0.9
beta_two = 0.95
norm_eps = 1e-05
adam_eps = 1e-08

MESH = pl.DeviceIdType.MESH
F32 = jnp.float32
BF16 = jnp.bfloat16


def remote(src, dst, send_sem, recv_sem, device):
    return pltpu.make_async_remote_copy(
        src_ref=src,
        dst_ref=dst,
        send_sem=send_sem,
        recv_sem=recv_sem,
        device_id=device,
        device_id_type=MESH,
    )


def gradient_kernel(
    ctx,
    w,
    m,
    v,
    tgt,
    ids,
    gall,
    wall,
    mall,
    vall,
    xbuf,
    wbuf,
    tbuf,
    eye,
    yt,
    gt,
    dyt,
    stat,
    early,
    late_out,
    late,
    tot,
    pbuf,
    r1,
    r2,
    rout,
    loc,
    in_s,
    in_r,
    z_s,
    z_r,
    e_s,
    e_r,
    l_s,
    l_r,
    st_s,
    st_r,
    x_s,
    x_r,
    y_s,
    y_r,
    y_l,
):
    mem = lax.axis_index("member")
    dp = lax.axis_index("dp")
    ten = lax.axis_index("tensor")
    yy, core = mem // 2, mem % 2
    zz, xl = dp // 2, dp % 2

    def at_z(k):
        return (mem, lax.rem(zz + k, ZN) * 2 + xl, ten)

    def member_at(k):
        return lax.rem(yy + k, YN) * 2 + core

    right, left = at_z(1), at_z(ZN - 1)
    dev_a = (mem, zz * 2 + 1 - xl, ten)
    dev_b = (mem, zz * 2 + 1 - xl, 1 - ten)
    dev_c = (mem, dp, 1 - ten)
    up_m, down_m, far_m = member_at(1), member_at(YN - 1), member_at(2)
    sib_m = yy * 2 + 1 - core
    up, down, sib = (up_m, dp, ten), (down_m, dp, ten), (sib_m, dp, ten)

    own_rows = ctx.at[pl.ds(pl.multiple_of(ten * TOK, TOK), TOK)]
    other_rows = ctx.at[pl.ds(pl.multiple_of((1 - ten) * TOK, TOK), TOK)]

    locals_ = [
        pltpu.make_async_copy(own_rows, xbuf.at[0, 0, 0], loc.at[0]),
        pltpu.make_async_copy(w, wbuf.at[0, 0], loc.at[1]),
        pltpu.make_async_copy(tgt.at[:, xl], tbuf.at[0], loc.at[2]),
        pltpu.make_async_copy(w, wall.at[mem], loc.at[3]),
        pltpu.make_async_copy(m, mall.at[mem], loc.at[4]),
        pltpu.make_async_copy(v, vall.at[mem], loc.at[5]),
    ]
    for copy in locals_:
        copy.start()

    barrier = pltpu.get_barrier_semaphore()

    def greet(k, _):
        pl.semaphore_signal(barrier, inc=1, device_id=at_z(k), device_id_type=MESH)
        return 0

    with jax.named_scope("entry_barrier"):
        lax.fori_loop(1, ZN, greet, 0)
        for device in (dev_a, dev_b, dev_c, up, down, sib):
            pl.semaphore_signal(barrier, inc=1, device_id=device, device_id_type=MESH)
        pl.semaphore_wait(barrier, ZN - 1 + 6)

    swap = remote(other_rows, xbuf.at[1, 0, 0], in_s.at[0], in_r.at[0], dev_c)
    swap.start()

    def ring(h, s, d):
        dst = xbuf.at[h, lax.rem(s + 1, SLOTS), d if d else s // (SLOTS - 1)]
        return remote(
            xbuf.at[h, s, d],
            dst,
            z_s.at[d, h, s],
            z_r.at[d, h, lax.rem(s + 1, SLOTS)],
            left if d else right,
        )

    def first(h, d, src):
        return remote(
            src, xbuf.at[h, 1, d], z_s.at[d, h, 0], z_r.at[d, h, 1], left if d else right
        )

    for d in (0, 1):
        first(0, d, own_rows).start()
    inputs = [
        remote(w, wbuf.at[0, 1], in_s.at[1], in_r.at[1], dev_a),
        remote(w, wbuf.at[1, 1], in_s.at[2], in_r.at[2], dev_b),
        remote(w, wbuf.at[1, 0], in_s.at[3], in_r.at[3], dev_c),
        remote(tgt.at[:, 1 - xl], tbuf.at[1], in_s.at[4], in_r.at[4], dev_a),
    ]
    for copy in inputs:
        copy.start()

    state = [(w, wall), (m, mall), (v, vall)]

    def state_first(i, src, dst):
        return [
            remote(src, dst.at[mem], st_s.at[i, 0], st_r.at[i, 0], up),
            remote(src, dst.at[mem], st_s.at[i, 1], st_r.at[i, 1], down),
            remote(src, dst.at[mem], st_s.at[i, 2], st_r.at[i, 2], sib),
        ]

    def state_on(i, dst):
        low, high = pl.ds(0, HALF), pl.ds(HALF, HALF)
        return [
            remote(dst.at[down_m, low], dst.at[down_m, low], st_s.at[i, 3], st_r.at[i, 3], up),
            remote(dst.at[up_m, high], dst.at[up_m, high], st_s.at[i, 4], st_r.at[i, 4], down),
            remote(dst.at[down_m], dst.at[down_m], st_s.at[i, 5], st_r.at[i, 5], sib),
            remote(dst.at[up_m], dst.at[up_m], st_s.at[i, 6], st_r.at[i, 6], sib),
        ]

    def state_last(i, dst):
        return remote(dst.at[far_m], dst.at[far_m], st_s.at[i, 7], st_r.at[i, 7], sib)

    for i, (src, dst) in enumerate(state):
        for copy in state_first(i, src, dst):
            copy.start()

    eye[...] = (
        lax.broadcasted_iota(jnp.int32, (ROWS, ROWS), 0)
        == lax.broadcasted_iota(jnp.int32, (ROWS, ROWS), 1)
    ).astype(BF16)
    stat[...] = jnp.zeros_like(stat)
    lane = lax.broadcasted_iota(jnp.int32, (1, 2 * TOK), 1)
    low_lanes = lane < TOK

    with jax.named_scope("swap_wait"):
        swap.wait_recv()
    for d in (0, 1):
        first(1, d, xbuf.at[1, 0, 0]).start()
    with jax.named_scope("local_wait"):
        for copy in locals_:
            copy.wait()

    def chunks_of(s):
        one = lax.rem(zz - s + ZN, ZN)
        two = lax.rem(zz + jnp.where(s == 0, SLOTS, s), ZN)
        return one, two

    def project(s):
        one, two = chunks_of(s)
        total = None
        for h in (0, 1):
            part = lax.dot_general(
                wbuf[h].reshape(2 * ROWS, COLS),
                xbuf[h, s].reshape(2 * TOK, COLS),
                (((1,), (1,)), ((), ())),
                preferred_element_type=F32,
            )
            total = part if total is None else total + part
        out = total * SCALING
        yt[s] = out
        goal = jnp.concatenate(
            [
                lax.dot_general(
                    eye[...],
                    jnp.concatenate([tbuf[side, one], tbuf[side, two]], axis=0),
                    (((1,), (1,)), ((), ())),
                    preferred_element_type=F32,
                )
                for side in (0, 1)
            ],
            axis=0,
        )
        gt[s] = goal
        squares = jnp.sum(out * out, axis=0, keepdims=True)
        crosses = jnp.sum(goal * out, axis=0, keepdims=True)
        row_one = jnp.where(low_lanes, squares, pltpu.roll(crosses, TOK, 1))
        row_two = jnp.where(low_lanes, pltpu.roll(squares, TOK, 1), crosses)
        return one, two, row_one, row_two

    def project_early(s, _):
        one, two, row_one, row_two = project(s)
        stat[pl.ds(one, 1), :] = row_one
        stat[pl.ds(two, 1), :] = row_two
        return 0

    def done_by(s):
        return jnp.minimum(jnp.maximum(2 * (s - 3), 0), SLOTS - 1)

    def gather_step(s, _):
        for h in (0, 1):
            for d in (0, 1):
                with jax.named_scope("ring_wait"):
                    remote(
                        xbuf.at[h, s, d], xbuf.at[h, s, d], z_s.at[d, h, s], z_r.at[d, h, s], right
                    ).wait_recv()
                if d == h:
                    ring(h, s, d).start()
                else:

                    @pl.when(s < SLOTS - 1)
                    def _():
                        ring(h, s, d).start()

        @pl.when(s == 4)
        def _():
            with jax.named_scope("inputs_wait"):
                for copy in inputs:
                    copy.wait_recv()

        with jax.named_scope("project_slots"):
            lax.fori_loop(done_by(s - 1) + 1, done_by(s) + 1, project_early, 0)
        return 0

    lax.fori_loop(1, SLOTS, gather_step, 0)

    def early_copy(k):
        return remote(stat, early.at[zz], e_s.at[k], e_r.at[zz], at_z(k))

    def late_copy(k):
        return remote(late_out, late.at[zz], l_s.at[k], l_r.at[zz], at_z(k))

    def send_early(k, _):
        early_copy(k).start()
        return 0

    lax.fori_loop(1, ZN, send_early, 0)
    early[zz] = stat[...]

    with jax.named_scope("ring_last_wait"):
        for h in (0, 1):
            remote(
                xbuf.at[h, 0, 1], xbuf.at[h, 0, 1], z_s.at[h, h, 0], z_r.at[h, h, 0], right
            ).wait_recv()
    with jax.named_scope("project_last"):
        _, _, row_one, row_two = project(0)
    late_out[pl.ds(0, 1), :] = row_one
    late_out[pl.ds(1, 1), :] = row_two

    def send_late(k, _):
        late_copy(k).start()
        return 0

    lax.fori_loop(1, ZN, send_late, 0)
    late[zz] = late_out[...]

    with jax.named_scope("state_first_wait"):
        for i, (src, dst) in enumerate(state):
            for copy in state_first(i, src, dst):
                copy.wait_recv()
            for copy in state_on(i, dst):
                copy.start()

    def take_early(k, total):
        src = lax.rem(zz + k, ZN)
        remote(stat, early.at[src], e_s.at[k], e_r.at[src], right).wait_recv()
        return total + early[src]

    with jax.named_scope("early_sums"):
        tot[...] = lax.fori_loop(1, ZN, take_early, stat[...])

    def take_late(k, _):
        src = lax.rem(zz + k, ZN)
        remote(late_out, late.at[src], l_s.at[k], l_r.at[src], right).wait_recv()
        return 0

    with jax.named_scope("late_sums"):
        lax.fori_loop(1, ZN, take_late, 0)

    def add_late(c, _):
        opposite = lax.rem(c + SLOTS, ZN)
        tot[pl.ds(c, 1), :] = (
            tot[pl.ds(c, 1), :] + late[c, pl.ds(0, 1), :] + late[opposite, pl.ds(1, 1), :]
        )
        return 0

    lax.fori_loop(0, ZN, add_late, 0)

    def window_mask(c):
        row = ids[pl.ds(2 * c + xl, 1), :]
        return jnp.where(row != 0, 1.0, 0.0)

    def out_gradient(s, _):
        one, two = chunks_of(s)
        row_one, row_two = tot[pl.ds(one, 1), :], tot[pl.ds(two, 1), :]
        squares = jnp.where(low_lanes, row_one, pltpu.roll(row_two, TOK, 1))
        crosses = jnp.where(low_lanes, pltpu.roll(row_one, TOK, 1), row_two)
        mask_one, mask_two = window_mask(one), window_mask(two)
        first_half = jnp.where(low_lanes, mask_one, pltpu.roll(mask_two, TOK, 1))
        second_half = jnp.where(low_lanes, pltpu.roll(mask_one, TOK, 1), mask_two)
        mask = jnp.where(ten == 0, first_half, second_half)
        inverse = lax.rsqrt(squares / D + norm_eps)
        projection = mask * (inverse * inverse * squares - inverse * crosses) / D
        normed = yt[s] * inverse
        hidden = mask * (normed - gt[s])
        grad_out = inverse * (hidden - normed * projection)
        dyt[:, pl.ds(pl.multiple_of(s * 2 * TOK, 2 * TOK), 2 * TOK)] = grad_out.astype(BF16)
        return 0

    with jax.named_scope("out_gradient"):
        lax.fori_loop(0, SLOTS, out_gradient, 0)

    low, high = pl.ds(0, HALF), pl.ds(HALF, HALF)

    def hop_one(j):
        return [
            remote(pbuf.at[j, 1, 0, low], r1.at[0, j], x_s.at[0, j], x_r.at[0, j], dev_a),
            remote(pbuf.at[j, 1, 0, high], r1.at[1, j], x_s.at[1, j], x_r.at[1, j], dev_b),
        ]

    def hop_two(j):
        return [
            remote(pbuf.at[j, 0, 1], r2.at[0, j], x_s.at[2, j], x_r.at[2, j], dev_a),
            remote(pbuf.at[j, 1, 1], r2.at[1, j], x_s.at[3, j], x_r.at[3, j], dev_b),
        ]

    def y_local(j):
        return pltpu.make_async_copy(rout.at[j], gall.at[mem, j], y_l.at[j])

    def y_first(j):
        return [
            remote(rout.at[j], gall.at[mem, j], y_s.at[0, j], y_r.at[0, j], up),
            remote(rout.at[j], gall.at[mem, j], y_s.at[1, j], y_r.at[1, j], down),
            remote(rout.at[j], gall.at[mem, j], y_s.at[2, j], y_r.at[2, j], sib),
        ]

    def y_on(j):
        one, two = gall.at[down_m, j], gall.at[up_m, j]
        return [
            remote(one.at[low], one.at[low], y_s.at[3, j], y_r.at[3, j], up),
            remote(two.at[high], two.at[high], y_s.at[4, j], y_r.at[4, j], down),
            remote(one, one, y_s.at[5, j], y_r.at[5, j], sib),
            remote(two, two, y_s.at[6, j], y_r.at[6, j], sib),
        ]

    def y_last(j):
        return remote(gall.at[far_m, j], gall.at[far_m, j], y_s.at[7, j], y_r.at[7, j], sib)

    def stage(step, behind, run):
        j = step - behind

        @pl.when(jnp.logical_and(j >= 0, j < NB))
        def _():
            with jax.named_scope(run.__name__):
                run(j)

    def multiply(j):
        cols = pl.ds(pl.multiple_of(j * CB, CB), CB)
        for h in (1, 0):
            part = jnp.dot(
                dyt[...],
                xbuf[h, :, :, :, cols].reshape(2 * SLOTS * TOK, CB),
                preferred_element_type=F32,
            )
            pbuf[j, h] = (part * SCALING).reshape(2, ROWS, CB)
        for copy in hop_one(j):
            copy.start()

    def add_one(j):
        for copy in hop_one(j):
            copy.wait_recv()
        pbuf[j, 1, 1, low] = pbuf[j, 1, 1, low] + r1[0, j]
        pbuf[j, 0, 1, high] = pbuf[j, 0, 1, high] + r1[1, j]
        for copy in hop_two(j):
            copy.start()

    def add_two(j):
        for copy in hop_two(j):
            copy.wait_recv()
        rout[j] = pbuf[j, 0, 0] + r2[0, j] + r2[1, j]
        y_local(j).start()
        for copy in y_first(j):
            copy.start()

    def pass_on(j):
        for copy in y_first(j):
            copy.wait_recv()
        for copy in y_on(j):
            copy.start()

    def pass_last(j):
        for copy in y_on(j):
            copy.wait_recv()
        y_last(j).start()

    def finish(j):
        y_last(j).wait_recv()
        y_local(j).wait()
        for copy in hop_one(j) + hop_two(j) + y_first(j) + y_on(j) + [y_last(j)]:
            copy.wait_send()

    def pipeline_step(step, _):
        for behind, run in enumerate((multiply, add_one, add_two, pass_on, pass_last, finish)):
            stage(step, behind, run)
        return 0

    lax.fori_loop(0, NB + 5, pipeline_step, 0)

    with jax.named_scope("state_on_wait"):
        for i, (src, dst) in enumerate(state):
            for copy in state_on(i, dst):
                copy.wait_recv()
            state_last(i, dst).start()
    with jax.named_scope("state_last_wait"):
        for i, (src, dst) in enumerate(state):
            state_last(i, dst).wait_recv()
            for copy in state_first(i, src, dst) + state_on(i, dst) + [state_last(i, dst)]:
                copy.wait_send()
    swap.wait_send()
    for copy in inputs:
        copy.wait_send()
    for d in (0, 1):
        first(0, d, own_rows).wait_send()
        first(1, d, xbuf.at[1, 0, 0]).wait_send()

    def drain_ring(s, _):
        for h in (0, 1):
            for d in (0, 1):
                if d == h:
                    ring(h, s, d).wait_send()
                else:

                    @pl.when(s < SLOTS - 1)
                    def _():
                        ring(h, s, d).wait_send()

        return 0

    lax.fori_loop(1, SLOTS, drain_ring, 0)

    def drain_stats(k, _):
        early_copy(k).wait_send()
        late_copy(k).wait_send()
        return 0

    lax.fori_loop(1, ZN, drain_stats, 0)


def gather_gradients(ctx, w, m, v, tgt, ids):
    anywhere = pl.BlockSpec(memory_space=pl.ANY)
    dma = pltpu.SemaphoreType.DMA
    vmem = pltpu.VMEM
    return pl.pallas_call(
        gradient_kernel,
        out_shape=(
            jax.ShapeDtypeStruct((MEMBERS, NB, ROWS, CB), F32),
            jax.ShapeDtypeStruct((MEMBERS, ROWS, COLS), BF16),
            jax.ShapeDtypeStruct((MEMBERS, ROWS, COLS), F32),
            jax.ShapeDtypeStruct((MEMBERS, ROWS, COLS), F32),
        ),
        in_specs=[anywhere] * 5 + [pl.BlockSpec(memory_space=pltpu.VMEM)],
        out_specs=(anywhere,) * 4,
        scratch_shapes=[
            vmem((2, SLOTS, 2, TOK, COLS), BF16),
            vmem((2, 2, ROWS, COLS), BF16),
            vmem((2, ZN, TOK, ROWS), BF16),
            vmem((ROWS, ROWS), BF16),
            vmem((SLOTS, 2 * ROWS, 2 * TOK), F32),
            vmem((SLOTS, 2 * ROWS, 2 * TOK), F32),
            vmem((2 * ROWS, SLOTS * 2 * TOK), BF16),
            vmem((ZN, 2 * TOK), F32),
            vmem((ZN, ZN, 2 * TOK), F32),
            vmem((2, 2 * TOK), F32),
            vmem((ZN, 2, 2 * TOK), F32),
            vmem((ZN, 2 * TOK), F32),
            vmem((NB, 2, 2, ROWS, CB), F32),
            vmem((2, NB, HALF, CB), F32),
            vmem((2, NB, ROWS, CB), F32),
            vmem((NB, ROWS, CB), F32),
            dma((6,)),
            dma((5,)),
            dma((5,)),
            dma((2, 2, SLOTS)),
            dma((2, 2, SLOTS)),
            dma((ZN,)),
            dma((ZN,)),
            dma((ZN,)),
            dma((ZN,)),
            dma((3, 8)),
            dma((3, 8)),
            dma((4, NB)),
            dma((4, NB)),
            dma((8, NB)),
            dma((8, NB)),
            dma((NB,)),
        ],
        compiler_params=pltpu.CompilerParams(
            collective_id=0, has_side_effects=True, vmem_limit_bytes=56 * 1024 * 1024
        ),
        cost_estimate=pl.CostEstimate(
            flops=4 * 1024 * HW * 2 * ROWS, bytes_accessed=20_000_000, transcendentals=0
        ),
    )(ctx, w, m, v, tgt, ids)


def update_kernel(pick, rate_of, level_of, g, w, m, v, new_w, new_m, new_v):
    p = pick[0]
    level = jnp.full((8, CB), level_of[p].astype(F32), F32)
    step_size = (rate_of[p] * 2.0 ** ((level - 4.0) / 4.0))[:1]
    gradient = g[0, 0]
    first = beta_one * m[0] + (1.0 - beta_one) * gradient
    second = beta_two * v[0] + (1.0 - beta_two) * gradient * gradient
    new_w[...] = (w[0].astype(F32) - step_size * first / (jnp.sqrt(second) + adam_eps)).astype(BF16)
    new_m[...] = first
    new_v[...] = second


def update(pick, base_lr, perturb_index, gall, wall, mall, vall):
    def member_block(j, pick, rate, level):
        return (pick[0], 0, j)

    def own_block(j, pick, rate, level):
        return (0, j)

    return pl.pallas_call(
        update_kernel,
        out_shape=(
            jax.ShapeDtypeStruct((ROWS, COLS), BF16),
            jax.ShapeDtypeStruct((ROWS, COLS), F32),
            jax.ShapeDtypeStruct((ROWS, COLS), F32),
        ),
        grid_spec=pltpu.PrefetchScalarGridSpec(
            num_scalar_prefetch=3,
            grid=(NB,),
            in_specs=[
                pl.BlockSpec((1, 1, ROWS, CB), lambda j, pick, rate, level: (pick[0], j, 0, 0)),
                pl.BlockSpec((1, ROWS, CB), member_block),
                pl.BlockSpec((1, ROWS, CB), member_block),
                pl.BlockSpec((1, ROWS, CB), member_block),
            ],
            out_specs=(
                pl.BlockSpec((ROWS, CB), own_block),
                pl.BlockSpec((ROWS, CB), own_block),
                pl.BlockSpec((ROWS, CB), own_block),
            ),
        ),
    )(pick, base_lr, perturb_index, gall, wall, mall, vall)


def body(
    context,
    out_weight,
    first_moment,
    second_moment,
    target,
    token_ids,
    base_lr,
    perturb_index,
    partner,
):
    gall, wall, mall, vall = gather_gradients(
        context[0, 0],
        out_weight[0],
        first_moment[0],
        second_moment[0],
        target[0].reshape(ZN, 2, TOK, ROWS),
        token_ids[0],
    )
    pick = lax.dynamic_slice(partner[:, 0], (lax.axis_index("member"),), (1,))
    new_weight, new_first, new_second = update(pick, base_lr, perturb_index, gall, wall, mall, vall)
    return (new_weight[None], new_first[None], new_second[None])


def solution(mesh):
    return jax.shard_map(
        body,
        mesh=mesh,
        in_specs=(
            P("member", "dp", None, "tensor"),
            P("member", "dp", "tensor"),
            P("member", "dp", "tensor"),
            P("member", "dp", "tensor"),
            P("member", None, "tensor", "dp"),
            P("member", None, None),
            P(),
            P(),
            P(None, "dp"),
        ),
        out_specs=(
            P("member", "dp", "tensor"),
            P("member", "dp", "tensor"),
            P("member", "dp", "tensor"),
        ),
        check_vma=False,
    )
```

```python
import math

import jax
import jax.numpy as jnp
from jax import lax
from jax.experimental import pallas as pl
from jax.experimental.pallas import tpu as pltpu
from jax.sharding import PartitionSpec as P

D = 5120
HW = 2560
MEMBERS = 8
ZN = 16
YN = 4
ROWS = 160
COLS = 1280
HALF = 80
TOK = 64
SLOTS = 8
CB = 256
NB = COLS // CB
PAD = 16
CODED = ROWS + PAD
TOP = 32000.0
LAG = 2
SCALING = 1.0 / math.sqrt(HW)

beta_one = 0.9
beta_two = 0.95
norm_eps = 1e-05
adam_eps = 1e-08

MESH = pl.DeviceIdType.MESH
F32 = jnp.float32
BF16 = jnp.bfloat16


def remote(src, dst, send_sem, recv_sem, device):
    return pltpu.make_async_remote_copy(
        src_ref=src,
        dst_ref=dst,
        send_sem=send_sem,
        recv_sem=recv_sem,
        device_id=device,
        device_id_type=MESH,
    )


def encode(values):
    top = jnp.max(jnp.abs(values), axis=0, keepdims=True)
    power = jnp.clip(jnp.ceil(jnp.log2(jnp.maximum(top, 1e-30))), -100.0, 126.0)
    codes = jnp.round(values * (TOP * jnp.exp2(-power)))
    powers = jnp.broadcast_to(power, (PAD, values.shape[1]))
    return jnp.concatenate([codes, powers], axis=0).astype(jnp.int32).astype(jnp.int16)


def decode(coded):
    wide = coded.astype(jnp.int32).astype(F32)
    rows = wide.shape[0] - PAD
    return wide[:rows] * (jnp.exp2(wide[rows : rows + 1]) * (1.0 / TOP))


def gradient_kernel(
    ctx,
    w,
    m,
    v,
    tgt,
    ids,
    gall,
    wall,
    mall,
    vall,
    xbuf,
    wbuf,
    tbuf,
    eye,
    yt,
    gt,
    dyt,
    stat,
    early,
    late_out,
    late,
    tot,
    pbuf,
    c1,
    r1,
    c2,
    r2,
    rout,
    mbuf,
    vbuf,
    loc,
    in_s,
    in_r,
    z_s,
    z_r,
    e_s,
    e_r,
    l_s,
    l_r,
    st_s,
    st_r,
    x_s,
    x_r,
    y_s,
    y_r,
    y_l,
):
    mem = lax.axis_index("member")
    dp = lax.axis_index("dp")
    ten = lax.axis_index("tensor")
    yy, core = mem // 2, mem % 2
    zz, xl = dp // 2, dp % 2

    def at_z(k):
        return (mem, lax.rem(zz + k, ZN) * 2 + xl, ten)

    def member_at(k):
        return lax.rem(yy + k, YN) * 2 + core

    right, left = at_z(1), at_z(ZN - 1)
    dev_a = (mem, zz * 2 + 1 - xl, ten)
    dev_b = (mem, zz * 2 + 1 - xl, 1 - ten)
    dev_c = (mem, dp, 1 - ten)
    up_m, down_m, far_m = member_at(1), member_at(YN - 1), member_at(2)
    sib_m = yy * 2 + 1 - core
    up, down, sib = (up_m, dp, ten), (down_m, dp, ten), (sib_m, dp, ten)

    own_rows = ctx.at[pl.ds(pl.multiple_of(ten * TOK, TOK), TOK)]
    other_rows = ctx.at[pl.ds(pl.multiple_of((1 - ten) * TOK, TOK), TOK)]

    locals_ = [
        pltpu.make_async_copy(own_rows, xbuf.at[0, 0, 0], loc.at[0]),
        pltpu.make_async_copy(w, wbuf.at[0, 0], loc.at[1]),
        pltpu.make_async_copy(tgt.at[:, xl], tbuf.at[0], loc.at[2]),
        pltpu.make_async_copy(m, mbuf, loc.at[3]),
        pltpu.make_async_copy(v, vbuf, loc.at[4]),
    ]
    kept = [
        pltpu.make_async_copy(wbuf.at[0, 0], wall.at[mem], loc.at[5]),
        pltpu.make_async_copy(mbuf, mall.at[mem], loc.at[6]),
        pltpu.make_async_copy(vbuf, vall.at[mem], loc.at[7]),
    ]
    for copy in locals_:
        copy.start()

    barrier = pltpu.get_barrier_semaphore()

    def greet(k, _):
        pl.semaphore_signal(barrier, inc=1, device_id=at_z(k), device_id_type=MESH)
        return 0

    lax.fori_loop(1, ZN, greet, 0)
    for device in (dev_a, dev_b, dev_c, up, down, sib):
        pl.semaphore_signal(barrier, inc=1, device_id=device, device_id_type=MESH)
    pl.semaphore_wait(barrier, ZN - 1 + 6)

    swap = remote(other_rows, xbuf.at[1, 0, 0], in_s.at[0], in_r.at[0], dev_c)
    swap.start()

    def ring(h, s, d):
        dst = xbuf.at[h, lax.rem(s + 1, SLOTS), d if d else s // (SLOTS - 1)]
        return remote(
            xbuf.at[h, s, d],
            dst,
            z_s.at[d, h, s],
            z_r.at[d, h, lax.rem(s + 1, SLOTS)],
            left if d else right,
        )

    def first(h, d, src):
        return remote(
            src, xbuf.at[h, 1, d], z_s.at[d, h, 0], z_r.at[d, h, 1], left if d else right
        )

    for d in (0, 1):
        first(0, d, own_rows).start()
    inputs = [
        remote(w, wbuf.at[0, 1], in_s.at[1], in_r.at[1], dev_a),
        remote(w, wbuf.at[1, 1], in_s.at[2], in_r.at[2], dev_b),
        remote(w, wbuf.at[1, 0], in_s.at[3], in_r.at[3], dev_c),
        remote(tgt.at[:, 1 - xl], tbuf.at[1], in_s.at[4], in_r.at[4], dev_a),
    ]
    for copy in inputs:
        copy.start()

    state = [(w, wall), (m, mall), (v, vall)]

    def state_first(i, src, dst):
        return [
            remote(src, dst.at[mem], st_s.at[i, 0], st_r.at[i, 0], up),
            remote(src, dst.at[mem], st_s.at[i, 1], st_r.at[i, 1], down),
            remote(src, dst.at[mem], st_s.at[i, 2], st_r.at[i, 2], sib),
        ]

    def state_on(i, dst):
        low, high = pl.ds(0, HALF), pl.ds(HALF, HALF)
        return [
            remote(dst.at[down_m, low], dst.at[down_m, low], st_s.at[i, 3], st_r.at[i, 3], up),
            remote(dst.at[up_m, high], dst.at[up_m, high], st_s.at[i, 4], st_r.at[i, 4], down),
            remote(dst.at[down_m], dst.at[down_m], st_s.at[i, 5], st_r.at[i, 5], sib),
            remote(dst.at[up_m], dst.at[up_m], st_s.at[i, 6], st_r.at[i, 6], sib),
        ]

    def state_last(i, dst):
        return remote(dst.at[far_m], dst.at[far_m], st_s.at[i, 7], st_r.at[i, 7], sib)

    for i, (src, dst) in enumerate(state):
        for copy in state_first(i, src, dst):
            copy.start()

    eye[...] = (
        lax.broadcasted_iota(jnp.int32, (ROWS, ROWS), 0)
        == lax.broadcasted_iota(jnp.int32, (ROWS, ROWS), 1)
    ).astype(BF16)
    stat[...] = jnp.zeros_like(stat)
    lane = lax.broadcasted_iota(jnp.int32, (1, 2 * TOK), 1)
    low_lanes = lane < TOK

    swap.wait_recv()
    for d in (0, 1):
        first(1, d, xbuf.at[1, 0, 0]).start()
    for copy in locals_:
        copy.wait()
    for copy in kept:
        copy.start()

    def chunks_of(s):
        one = lax.rem(zz - s + ZN, ZN)
        two = lax.rem(zz + jnp.where(s == 0, SLOTS, s), ZN)
        return one, two

    def project(s):
        one, two = chunks_of(s)
        total = None
        for h in (0, 1):
            part = lax.dot_general(
                wbuf[h].reshape(2 * ROWS, COLS),
                xbuf[h, s].reshape(2 * TOK, COLS),
                (((1,), (1,)), ((), ())),
                preferred_element_type=F32,
            )
            total = part if total is None else total + part
        out = total * SCALING
        yt[s] = out
        goal = jnp.concatenate(
            [
                lax.dot_general(
                    eye[...],
                    jnp.concatenate([tbuf[side, one], tbuf[side, two]], axis=0),
                    (((1,), (1,)), ((), ())),
                    preferred_element_type=F32,
                )
                for side in (0, 1)
            ],
            axis=0,
        )
        gt[s] = goal
        squares = jnp.sum(out * out, axis=0, keepdims=True)
        crosses = jnp.sum(goal * out, axis=0, keepdims=True)
        row_one = jnp.where(low_lanes, squares, pltpu.roll(crosses, TOK, 1))
        row_two = jnp.where(low_lanes, pltpu.roll(squares, TOK, 1), crosses)
        return one, two, row_one, row_two

    def project_early(s, _):
        one, two, row_one, row_two = project(s)
        stat[pl.ds(one, 1), :] = row_one
        stat[pl.ds(two, 1), :] = row_two
        return 0

    def done_by(s):
        return jnp.minimum(jnp.maximum(2 * (s - 3), 0), SLOTS - 1)

    def gather_step(s, _):
        for h in (0, 1):
            for d in (0, 1):
                remote(
                    xbuf.at[h, s, d], xbuf.at[h, s, d], z_s.at[d, h, s], z_r.at[d, h, s], right
                ).wait_recv()
                if d == h:
                    ring(h, s, d).start()
                else:

                    @pl.when(s < SLOTS - 1)
                    def _():
                        ring(h, s, d).start()

        @pl.when(s == 4)
        def _():
            for copy in inputs:
                copy.wait_recv()

        @pl.when(s == SLOTS - 1)
        def _():
            for i, (src, dst) in enumerate(state):
                for copy in state_first(i, src, dst):
                    copy.wait_recv()
                for copy in state_on(i, dst):
                    copy.start()

        lax.fori_loop(done_by(s - 1) + 1, done_by(s) + 1, project_early, 0)
        return 0

    lax.fori_loop(1, SLOTS, gather_step, 0)

    def early_copy(k):
        return remote(stat, early.at[zz], e_s.at[k], e_r.at[zz], at_z(k))

    def late_copy(k):
        return remote(late_out, late.at[zz], l_s.at[k], l_r.at[zz], at_z(k))

    def send_early(k, _):
        early_copy(k).start()
        return 0

    lax.fori_loop(1, ZN, send_early, 0)
    early[zz] = stat[...]

    for h in (0, 1):
        remote(
            xbuf.at[h, 0, 1], xbuf.at[h, 0, 1], z_s.at[h, h, 0], z_r.at[h, h, 0], right
        ).wait_recv()
    _, _, row_one, row_two = project(0)
    late_out[pl.ds(0, 1), :] = row_one
    late_out[pl.ds(1, 1), :] = row_two

    def send_late(k, _):
        late_copy(k).start()
        return 0

    lax.fori_loop(1, ZN, send_late, 0)
    late[zz] = late_out[...]

    def take_early(k, total):
        src = lax.rem(zz + k, ZN)
        remote(stat, early.at[src], e_s.at[k], e_r.at[src], right).wait_recv()
        return total + early[src]

    tot[...] = lax.fori_loop(1, ZN, take_early, stat[...])

    def take_late(k, _):
        src = lax.rem(zz + k, ZN)
        remote(late_out, late.at[src], l_s.at[k], l_r.at[src], right).wait_recv()
        return 0

    lax.fori_loop(1, ZN, take_late, 0)

    def add_late(c, _):
        opposite = lax.rem(c + SLOTS, ZN)
        tot[pl.ds(c, 1), :] = (
            tot[pl.ds(c, 1), :] + late[c, pl.ds(0, 1), :] + late[opposite, pl.ds(1, 1), :]
        )
        return 0

    lax.fori_loop(0, ZN, add_late, 0)

    def window_mask(c):
        row = ids[pl.ds(2 * c + xl, 1), :]
        return jnp.where(row != 0, 1.0, 0.0)

    def out_gradient(s, _):
        one, two = chunks_of(s)
        row_one, row_two = tot[pl.ds(one, 1), :], tot[pl.ds(two, 1), :]
        squares = jnp.where(low_lanes, row_one, pltpu.roll(row_two, TOK, 1))
        crosses = jnp.where(low_lanes, pltpu.roll(row_one, TOK, 1), row_two)
        mask_one, mask_two = window_mask(one), window_mask(two)
        first_half = jnp.where(low_lanes, mask_one, pltpu.roll(mask_two, TOK, 1))
        second_half = jnp.where(low_lanes, pltpu.roll(mask_one, TOK, 1), mask_two)
        mask = jnp.where(ten == 0, first_half, second_half)
        inverse = lax.rsqrt(squares / D + norm_eps)
        projection = mask * (inverse * inverse * squares - inverse * crosses) / D
        normed = yt[s] * inverse
        hidden = mask * (normed - gt[s])
        grad_out = inverse * (hidden - normed * projection)
        dyt[:, pl.ds(pl.multiple_of(s * 2 * TOK, 2 * TOK), 2 * TOK)] = grad_out.astype(BF16)
        return 0

    lax.fori_loop(0, SLOTS, out_gradient, 0)

    low, high = pl.ds(0, HALF), pl.ds(HALF, CODED - HALF)

    def hop_one(j):
        return [
            remote(c1.at[0, j], r1.at[0, j], x_s.at[0, j], x_r.at[0, j], dev_a),
            remote(c1.at[1, j], r1.at[1, j], x_s.at[1, j], x_r.at[1, j], dev_b),
        ]

    def hop_two(j):
        return [
            remote(c2.at[0, j], r2.at[0, j], x_s.at[2, j], x_r.at[2, j], dev_a),
            remote(c2.at[1, j], r2.at[1, j], x_s.at[3, j], x_r.at[3, j], dev_b),
        ]

    def y_local(j):
        return pltpu.make_async_copy(rout.at[j], gall.at[mem, j], y_l.at[j])

    def y_first(j):
        return [
            remote(rout.at[j], gall.at[mem, j], y_s.at[0, j], y_r.at[0, j], up),
            remote(rout.at[j], gall.at[mem, j], y_s.at[1, j], y_r.at[1, j], down),
            remote(rout.at[j], gall.at[mem, j], y_s.at[2, j], y_r.at[2, j], sib),
        ]

    def y_on(j):
        one, two = gall.at[down_m, j], gall.at[up_m, j]
        return [
            remote(one.at[low], one.at[low], y_s.at[3, j], y_r.at[3, j], up),
            remote(two.at[high], two.at[high], y_s.at[4, j], y_r.at[4, j], down),
            remote(one, one, y_s.at[5, j], y_r.at[5, j], sib),
            remote(two, two, y_s.at[6, j], y_r.at[6, j], sib),
        ]

    def y_last(j):
        return remote(gall.at[far_m, j], gall.at[far_m, j], y_s.at[7, j], y_r.at[7, j], sib)

    def stage(step, behind, run):
        j = step - behind

        @pl.when(jnp.logical_and(j >= 0, j < NB))
        def _():
            run(j)

    def multiply(j):
        cols = pl.ds(pl.multiple_of(j * CB, CB), CB)
        for h in (1, 0):
            part = SCALING * jnp.dot(
                dyt[...],
                xbuf[h, :, :, :, cols].reshape(2 * SLOTS * TOK, CB),
                preferred_element_type=F32,
            )
            pbuf[j, h, 1] = part[ROWS:]
            if h:
                c1[0, j] = encode(part[:HALF])
                c1[1, j] = encode(part[HALF:ROWS])
                for copy in hop_one(j):
                    copy.start()
            else:
                pbuf[j, h, 0] = part[:ROWS]

    def add_one(j):
        for copy in hop_one(j):
            copy.wait_recv()
        pbuf[j, 1, 1, :HALF] = pbuf[j, 1, 1, :HALF] + decode(r1[0, j])
        pbuf[j, 0, 1, HALF:] = pbuf[j, 0, 1, HALF:] + decode(r1[1, j])
        c2[0, j] = encode(pbuf[j, 0, 1])
        c2[1, j] = encode(pbuf[j, 1, 1])
        for copy in hop_two(j):
            copy.start()

    def add_two(j):
        for copy in hop_two(j):
            copy.wait_recv()
        rout[j] = encode(pbuf[j, 0, 0] + decode(r2[0, j]) + decode(r2[1, j]))
        y_local(j).start()
        for copy in y_first(j):
            copy.start()

    def pass_on(j):
        for copy in y_first(j):
            copy.wait_recv()
        for copy in y_on(j):
            copy.start()

    def pass_last(j):
        for copy in y_on(j):
            copy.wait_recv()
        y_last(j).start()

    def finish(j):
        y_last(j).wait_recv()
        y_local(j).wait()
        for copy in hop_one(j) + hop_two(j) + y_first(j) + y_on(j) + [y_last(j)]:
            copy.wait_send()

    def pipeline_step(step, _):
        for behind, run in enumerate((multiply, add_one, add_two, pass_on, pass_last, finish)):
            stage(step, LAG * behind, run)
        return 0

    lax.fori_loop(0, NB + 5 * LAG, pipeline_step, 0)

    for i, (src, dst) in enumerate(state):
        for copy in state_on(i, dst):
            copy.wait_recv()
        state_last(i, dst).start()
    for i, (src, dst) in enumerate(state):
        state_last(i, dst).wait_recv()
        for copy in state_first(i, src, dst) + state_on(i, dst) + [state_last(i, dst)]:
            copy.wait_send()
    for copy in kept:
        copy.wait()
    swap.wait_send()
    for copy in inputs:
        copy.wait_send()
    for d in (0, 1):
        first(0, d, own_rows).wait_send()
        first(1, d, xbuf.at[1, 0, 0]).wait_send()

    def drain_ring(s, _):
        for h in (0, 1):
            for d in (0, 1):
                if d == h:
                    ring(h, s, d).wait_send()
                else:

                    @pl.when(s < SLOTS - 1)
                    def _():
                        ring(h, s, d).wait_send()

        return 0

    lax.fori_loop(1, SLOTS, drain_ring, 0)

    def drain_stats(k, _):
        early_copy(k).wait_send()
        late_copy(k).wait_send()
        return 0

    lax.fori_loop(1, ZN, drain_stats, 0)


def gather_gradients(ctx, w, m, v, tgt, ids):
    anywhere = pl.BlockSpec(memory_space=pl.ANY)
    dma = pltpu.SemaphoreType.DMA
    vmem = pltpu.VMEM
    return pl.pallas_call(
        gradient_kernel,
        out_shape=(
            jax.ShapeDtypeStruct((MEMBERS, NB, CODED, CB), jnp.int16),
            jax.ShapeDtypeStruct((MEMBERS, ROWS, COLS), BF16),
            jax.ShapeDtypeStruct((MEMBERS, ROWS, COLS), F32),
            jax.ShapeDtypeStruct((MEMBERS, ROWS, COLS), F32),
        ),
        in_specs=[anywhere] * 5 + [pl.BlockSpec(memory_space=pltpu.VMEM)],
        out_specs=(anywhere,) * 4,
        scratch_shapes=[
            vmem((2, SLOTS, 2, TOK, COLS), BF16),
            vmem((2, 2, ROWS, COLS), BF16),
            vmem((2, ZN, TOK, ROWS), BF16),
            vmem((ROWS, ROWS), BF16),
            vmem((SLOTS, 2 * ROWS, 2 * TOK), F32),
            vmem((SLOTS, 2 * ROWS, 2 * TOK), F32),
            vmem((2 * ROWS, SLOTS * 2 * TOK), BF16),
            vmem((ZN, 2 * TOK), F32),
            vmem((ZN, ZN, 2 * TOK), F32),
            vmem((2, 2 * TOK), F32),
            vmem((ZN, 2, 2 * TOK), F32),
            vmem((ZN, 2 * TOK), F32),
            vmem((NB, 2, 2, ROWS, CB), F32),
            vmem((2, NB, HALF + PAD, CB), jnp.int16),
            vmem((2, NB, HALF + PAD, CB), jnp.int16),
            vmem((2, NB, CODED, CB), jnp.int16),
            vmem((2, NB, CODED, CB), jnp.int16),
            vmem((NB, CODED, CB), jnp.int16),
            vmem((ROWS, COLS), F32),
            vmem((ROWS, COLS), F32),
            dma((8,)),
            dma((5,)),
            dma((5,)),
            dma((2, 2, SLOTS)),
            dma((2, 2, SLOTS)),
            dma((ZN,)),
            dma((ZN,)),
            dma((ZN,)),
            dma((ZN,)),
            dma((3, 8)),
            dma((3, 8)),
            dma((4, NB)),
            dma((4, NB)),
            dma((8, NB)),
            dma((8, NB)),
            dma((NB,)),
        ],
        compiler_params=pltpu.CompilerParams(
            collective_id=0, has_side_effects=True, vmem_limit_bytes=56 * 1024 * 1024
        ),
        cost_estimate=pl.CostEstimate(
            flops=4 * 1024 * HW * 2 * ROWS, bytes_accessed=20_000_000, transcendentals=0
        ),
    )(ctx, w, m, v, tgt, ids)


def update_kernel(pick, rate_of, level_of, g, w, m, v, new_w, new_m, new_v):
    p = pick[0]
    level = jnp.full((8, CB), level_of[p].astype(F32), F32)
    step_size = (rate_of[p] * 2.0 ** ((level - 4.0) / 4.0))[:1]
    gradient = decode(g[0, 0])
    first = beta_one * m[0] + (1.0 - beta_one) * gradient
    second = beta_two * v[0] + (1.0 - beta_two) * gradient * gradient
    new_w[...] = (w[0].astype(F32) - step_size * first / (jnp.sqrt(second) + adam_eps)).astype(BF16)
    new_m[...] = first
    new_v[...] = second


def update(pick, base_lr, perturb_index, gall, wall, mall, vall):
    def member_block(j, pick, rate, level):
        return (pick[0], 0, j)

    def own_block(j, pick, rate, level):
        return (0, j)

    return pl.pallas_call(
        update_kernel,
        out_shape=(
            jax.ShapeDtypeStruct((ROWS, COLS), BF16),
            jax.ShapeDtypeStruct((ROWS, COLS), F32),
            jax.ShapeDtypeStruct((ROWS, COLS), F32),
        ),
        grid_spec=pltpu.PrefetchScalarGridSpec(
            num_scalar_prefetch=3,
            grid=(NB,),
            in_specs=[
                pl.BlockSpec((1, 1, CODED, CB), lambda j, pick, rate, level: (pick[0], j, 0, 0)),
                pl.BlockSpec((1, ROWS, CB), member_block),
                pl.BlockSpec((1, ROWS, CB), member_block),
                pl.BlockSpec((1, ROWS, CB), member_block),
            ],
            out_specs=(
                pl.BlockSpec((ROWS, CB), own_block),
                pl.BlockSpec((ROWS, CB), own_block),
                pl.BlockSpec((ROWS, CB), own_block),
            ),
        ),
    )(pick, base_lr, perturb_index, gall, wall, mall, vall)


def body(
    context,
    out_weight,
    first_moment,
    second_moment,
    target,
    token_ids,
    base_lr,
    perturb_index,
    partner,
):
    gall, wall, mall, vall = gather_gradients(
        context[0, 0],
        out_weight[0],
        first_moment[0],
        second_moment[0],
        target[0].reshape(ZN, 2, TOK, ROWS),
        token_ids[0],
    )
    pick = lax.dynamic_slice(partner[:, 0], (lax.axis_index("member"),), (1,))
    new_weight, new_first, new_second = update(pick, base_lr, perturb_index, gall, wall, mall, vall)
    return (new_weight[None], new_first[None], new_second[None])


def solution(mesh):
    return jax.shard_map(
        body,
        mesh=mesh,
        in_specs=(
            P("member", "dp", None, "tensor"),
            P("member", "dp", "tensor"),
            P("member", "dp", "tensor"),
            P("member", "dp", "tensor"),
            P("member", None, "tensor", "dp"),
            P("member", None, None),
            P(),
            P(),
            P(None, "dp"),
        ),
        out_specs=(
            P("member", "dp", "tensor"),
            P("member", "dp", "tensor"),
            P("member", "dp", "tensor"),
        ),
        check_vma=False,
    )
```

```python
import math

import jax
import jax.numpy as jnp
from jax import lax
from jax.experimental import pallas as pl
from jax.experimental.pallas import tpu as pltpu
from jax.sharding import PartitionSpec as P

D = 5120
HW = 2560
MEMBERS = 8
ZN = 16
YN = 4
ROWS = 160
COLS = 1280
HALF = 80
TOK = 64
SLOTS = 8
CB = 256
NB = COLS // CB
PAD = 16
CODED = ROWS + PAD
TOP = 32000.0
LAG = 2
SCALING = 1.0 / math.sqrt(HW)

beta_one = 0.9
beta_two = 0.95
norm_eps = 1e-05
adam_eps = 1e-08

MESH = pl.DeviceIdType.MESH
F32 = jnp.float32
BF16 = jnp.bfloat16


def remote(src, dst, send_sem, recv_sem, device):
    return pltpu.make_async_remote_copy(
        src_ref=src,
        dst_ref=dst,
        send_sem=send_sem,
        recv_sem=recv_sem,
        device_id=device,
        device_id_type=MESH,
    )


def encode(values):
    top = jnp.max(jnp.abs(values), axis=0, keepdims=True)
    power = jnp.clip(jnp.ceil(jnp.log2(jnp.maximum(top, 1e-30))), -100.0, 126.0)
    codes = jnp.round(values * (TOP * jnp.exp2(-power)))
    powers = jnp.broadcast_to(power, (PAD, values.shape[1]))
    return jnp.concatenate([codes, powers], axis=0).astype(jnp.int32).astype(jnp.int16)


def decode(coded):
    wide = coded.astype(jnp.int32).astype(F32)
    rows = wide.shape[0] - PAD
    return wide[:rows] * (jnp.exp2(wide[rows : rows + 1]) * (1.0 / TOP))


def gradient_kernel(
    ctx,
    w,
    m,
    v,
    tgt,
    ids,
    gall,
    wall,
    mall,
    vall,
    xbuf,
    wbuf,
    tbuf,
    eye,
    yt,
    gt,
    dyt,
    stat,
    early,
    late_out,
    late,
    tot,
    pbuf,
    c1,
    r1,
    c2,
    r2,
    rout,
    mbuf,
    vbuf,
    mcode,
    vcode,
    idbuf,
    loc,
    in_s,
    in_r,
    z_s,
    z_r,
    e_s,
    e_r,
    l_s,
    l_r,
    st_s,
    st_r,
    x_s,
    x_r,
    y_s,
    y_r,
    y_l,
):
    mem = lax.axis_index("member")
    dp = lax.axis_index("dp")
    ten = lax.axis_index("tensor")
    yy, core = mem // 2, mem % 2
    zz, xl = dp // 2, dp % 2

    def at_z(k):
        return (mem, lax.rem(zz + k, ZN) * 2 + xl, ten)

    def member_at(k):
        return lax.rem(yy + k, YN) * 2 + core

    right, left = at_z(1), at_z(ZN - 1)
    dev_a = (mem, zz * 2 + 1 - xl, ten)
    dev_b = (mem, zz * 2 + 1 - xl, 1 - ten)
    dev_c = (mem, dp, 1 - ten)
    up_m, down_m, far_m = member_at(1), member_at(YN - 1), member_at(2)
    sib_m = yy * 2 + 1 - core
    up, down, sib = (up_m, dp, ten), (down_m, dp, ten), (sib_m, dp, ten)

    own_rows = ctx.at[pl.ds(pl.multiple_of(ten * TOK, TOK), TOK)]
    other_rows = ctx.at[pl.ds(pl.multiple_of((1 - ten) * TOK, TOK), TOK)]

    locals_ = [
        pltpu.make_async_copy(own_rows, xbuf.at[0, 0, 0], loc.at[0]),
        pltpu.make_async_copy(w, wbuf.at[0, 0], loc.at[1]),
        pltpu.make_async_copy(tgt.at[:, xl], tbuf.at[0], loc.at[2]),
        pltpu.make_async_copy(ids, idbuf, loc.at[3]),
    ]
    moments = [
        pltpu.make_async_copy(m, mbuf, loc.at[4]),
        pltpu.make_async_copy(v, vbuf, loc.at[5]),
    ]
    kept = [
        pltpu.make_async_copy(wbuf.at[0, 0], wall.at[mem], loc.at[6]),
        pltpu.make_async_copy(mcode, mall.at[mem], loc.at[7]),
        pltpu.make_async_copy(vcode, vall.at[mem], loc.at[8]),
    ]
    for copy in locals_ + moments:
        copy.start()

    barrier = pltpu.get_barrier_semaphore()

    neighbours = (right, left, dev_a, dev_b, dev_c, up, down, sib)
    for device in neighbours:
        pl.semaphore_signal(barrier, inc=1, device_id=device, device_id_type=MESH)
    pl.semaphore_wait(barrier, len(neighbours))

    swap = remote(other_rows, xbuf.at[1, 0, 0], in_s.at[0], in_r.at[0], dev_c)
    swap.start()

    def ring(h, s, d):
        dst = xbuf.at[h, lax.rem(s + 1, SLOTS), d if d else s // (SLOTS - 1)]
        return remote(
            xbuf.at[h, s, d],
            dst,
            z_s.at[d, h, s],
            z_r.at[d, h, lax.rem(s + 1, SLOTS)],
            left if d else right,
        )

    def first(h, d, src):
        return remote(
            src, xbuf.at[h, 1, d], z_s.at[d, h, 0], z_r.at[d, h, 1], left if d else right
        )

    for d in (0, 1):
        first(0, d, own_rows).start()
    inputs = [
        remote(w, wbuf.at[0, 1], in_s.at[1], in_r.at[1], dev_a),
        remote(w, wbuf.at[1, 1], in_s.at[2], in_r.at[2], dev_b),
        remote(w, wbuf.at[1, 0], in_s.at[3], in_r.at[3], dev_c),
        remote(tgt.at[:, 1 - xl], tbuf.at[1], in_s.at[4], in_r.at[4], dev_a),
    ]
    for copy in inputs:
        copy.start()

    state = [(w, wall), (mcode, mall), (vcode, vall)]

    def state_first(i, src, dst):
        return [
            remote(src, dst.at[mem], st_s.at[i, 0], st_r.at[i, 0], up),
            remote(src, dst.at[mem], st_s.at[i, 1], st_r.at[i, 1], down),
            remote(src, dst.at[mem], st_s.at[i, 2], st_r.at[i, 2], sib),
        ]

    def state_on(i, dst):
        one, two = dst.at[down_m], dst.at[up_m]
        if i:
            low, high = pl.ds(0, HALF), pl.ds(HALF, CODED - HALF)
            one_low, two_high = one.at[:, low], two.at[:, high]
        else:
            one_low, two_high = one.at[pl.ds(0, HALF)], two.at[pl.ds(HALF, HALF)]
        return [
            remote(one_low, one_low, st_s.at[i, 3], st_r.at[i, 3], up),
            remote(two_high, two_high, st_s.at[i, 4], st_r.at[i, 4], down),
            remote(one, one, st_s.at[i, 5], st_r.at[i, 5], sib),
            remote(two, two, st_s.at[i, 6], st_r.at[i, 6], sib),
        ]

    def state_last(i, dst):
        return remote(dst.at[far_m], dst.at[far_m], st_s.at[i, 7], st_r.at[i, 7], sib)

    for copy in state_first(0, w, wall):
        copy.start()

    eye[...] = (
        lax.broadcasted_iota(jnp.int32, (ROWS, ROWS), 0)
        == lax.broadcasted_iota(jnp.int32, (ROWS, ROWS), 1)
    ).astype(BF16)
    stat[...] = jnp.zeros_like(stat)
    lane = lax.broadcasted_iota(jnp.int32, (1, 2 * TOK), 1)
    low_lanes = lane < TOK

    swap.wait_recv()
    for d in (0, 1):
        first(1, d, xbuf.at[1, 0, 0]).start()
    for copy in moments:
        copy.wait()

    def code_moments(j, _):
        cols = pl.ds(pl.multiple_of(j * CB, CB), CB)
        mcode[j] = encode(mbuf[:, cols])
        vcode[j] = encode(vbuf[:, cols])
        return 0

    lax.fori_loop(0, NB, code_moments, 0)
    for i in (1, 2):
        for copy in state_first(i, *state[i]):
            copy.start()
    for copy in locals_:
        copy.wait()
    for copy in kept:
        copy.start()

    def chunks_of(s):
        one = lax.rem(zz - s + ZN, ZN)
        two = lax.rem(zz + jnp.where(s == 0, SLOTS, s), ZN)
        return one, two

    def project(s):
        one, two = chunks_of(s)
        total = None
        for h in (0, 1):
            part = lax.dot_general(
                wbuf[h].reshape(2 * ROWS, COLS),
                xbuf[h, s].reshape(2 * TOK, COLS),
                (((1,), (1,)), ((), ())),
                preferred_element_type=F32,
            )
            total = part if total is None else total + part
        out = total * SCALING
        yt[s] = out
        goal = jnp.concatenate(
            [
                lax.dot_general(
                    eye[...],
                    jnp.concatenate([tbuf[side, one], tbuf[side, two]], axis=0),
                    (((1,), (1,)), ((), ())),
                    preferred_element_type=F32,
                )
                for side in (0, 1)
            ],
            axis=0,
        )
        gt[s] = goal
        squares = jnp.sum(out * out, axis=0, keepdims=True)
        crosses = jnp.sum(goal * out, axis=0, keepdims=True)
        row_one = jnp.where(low_lanes, squares, pltpu.roll(crosses, TOK, 1))
        row_two = jnp.where(low_lanes, pltpu.roll(squares, TOK, 1), crosses)
        return one, two, row_one, row_two

    def project_early(s, _):
        one, two, row_one, row_two = project(s)
        stat[pl.ds(one, 1), :] = row_one
        stat[pl.ds(two, 1), :] = row_two
        return 0

    def done_by(s):
        return jnp.minimum(jnp.maximum(2 * (s - 3), 0), SLOTS - 1)

    def gather_step(s, _):
        for h in (0, 1):
            for d in (0, 1):
                remote(
                    xbuf.at[h, s, d], xbuf.at[h, s, d], z_s.at[d, h, s], z_r.at[d, h, s], right
                ).wait_recv()
                if d == h:
                    ring(h, s, d).start()
                else:

                    @pl.when(s < SLOTS - 1)
                    def _():
                        ring(h, s, d).start()

        @pl.when(s == 4)
        def _():
            for copy in inputs:
                copy.wait_recv()

        @pl.when(s == SLOTS - 2)
        def _():
            for i, (src, dst) in enumerate(state):
                for copy in state_first(i, src, dst):
                    copy.wait_recv()
                for copy in state_on(i, dst):
                    copy.start()

        lax.fori_loop(done_by(s - 1) + 1, done_by(s) + 1, project_early, 0)
        return 0

    lax.fori_loop(1, SLOTS, gather_step, 0)

    def early_copy(k):
        return remote(stat, early.at[zz], e_s.at[k], e_r.at[zz], at_z(k))

    def late_copy(k):
        return remote(late_out, late.at[zz], l_s.at[k], l_r.at[zz], at_z(k))

    def send_early(k, _):
        early_copy(k).start()
        return 0

    lax.fori_loop(1, SLOTS, send_early, 0)
    lax.fori_loop(SLOTS + 1, ZN, send_early, 0)
    early[zz] = stat[...]

    for h in (0, 1):
        remote(
            xbuf.at[h, 0, 1], xbuf.at[h, 0, 1], z_s.at[h, h, 0], z_r.at[h, h, 0], right
        ).wait_recv()
    early_copy(SLOTS).start()
    _, _, row_one, row_two = project(0)
    late_out[pl.ds(0, 1), :] = row_one
    late_out[pl.ds(1, 1), :] = row_two

    def send_late(k, _):
        late_copy(k).start()
        return 0

    lax.fori_loop(1, ZN, send_late, 0)
    late[zz] = late_out[...]

    def take_early(k, total):
        src = lax.rem(zz + k, ZN)
        remote(stat, early.at[src], e_s.at[k], e_r.at[src], right).wait_recv()
        return total + early[src]

    tot[...] = lax.fori_loop(1, ZN, take_early, stat[...])

    def take_late(k, _):
        src = lax.rem(zz + k, ZN)
        remote(late_out, late.at[src], l_s.at[k], l_r.at[src], right).wait_recv()
        return 0

    lax.fori_loop(1, ZN, take_late, 0)

    def add_late(c, _):
        opposite = lax.rem(c + SLOTS, ZN)
        tot[pl.ds(c, 1), :] = (
            tot[pl.ds(c, 1), :] + late[c, pl.ds(0, 1), :] + late[opposite, pl.ds(1, 1), :]
        )
        return 0

    lax.fori_loop(0, ZN, add_late, 0)

    def window_mask(c):
        row = idbuf[pl.ds(2 * c + xl, 1), :]
        return jnp.where(row != 0, 1.0, 0.0)

    def out_gradient(s, _):
        one, two = chunks_of(s)
        row_one, row_two = tot[pl.ds(one, 1), :], tot[pl.ds(two, 1), :]
        squares = jnp.where(low_lanes, row_one, pltpu.roll(row_two, TOK, 1))
        crosses = jnp.where(low_lanes, pltpu.roll(row_one, TOK, 1), row_two)
        mask_one, mask_two = window_mask(one), window_mask(two)
        first_half = jnp.where(low_lanes, mask_one, pltpu.roll(mask_two, TOK, 1))
        second_half = jnp.where(low_lanes, pltpu.roll(mask_one, TOK, 1), mask_two)
        mask = jnp.where(ten == 0, first_half, second_half)
        inverse = lax.rsqrt(squares / D + norm_eps)
        projection = mask * (inverse * inverse * squares - inverse * crosses) / D
        normed = yt[s] * inverse
        hidden = mask * (normed - gt[s])
        grad_out = inverse * (hidden - normed * projection)
        dyt[:, pl.ds(pl.multiple_of(s * 2 * TOK, 2 * TOK), 2 * TOK)] = grad_out.astype(BF16)
        return 0

    lax.fori_loop(0, SLOTS, out_gradient, 0)

    low, high = pl.ds(0, HALF), pl.ds(HALF, CODED - HALF)

    def hop_one(j):
        return [
            remote(c1.at[0, j], r1.at[0, j], x_s.at[0, j], x_r.at[0, j], dev_a),
            remote(c1.at[1, j], r1.at[1, j], x_s.at[1, j], x_r.at[1, j], dev_b),
        ]

    def hop_two(j):
        return [
            remote(c2.at[0, j], r2.at[0, j], x_s.at[2, j], x_r.at[2, j], dev_a),
            remote(c2.at[1, j], r2.at[1, j], x_s.at[3, j], x_r.at[3, j], dev_b),
        ]

    def y_local(j):
        return pltpu.make_async_copy(rout.at[j], gall.at[mem, j], y_l.at[j])

    def y_first(j):
        return [
            remote(rout.at[j], gall.at[mem, j], y_s.at[0, j], y_r.at[0, j], up),
            remote(rout.at[j], gall.at[mem, j], y_s.at[1, j], y_r.at[1, j], down),
            remote(rout.at[j], gall.at[mem, j], y_s.at[2, j], y_r.at[2, j], sib),
        ]

    def y_on(j):
        one, two = gall.at[down_m, j], gall.at[up_m, j]
        return [
            remote(one.at[low], one.at[low], y_s.at[3, j], y_r.at[3, j], up),
            remote(two.at[high], two.at[high], y_s.at[4, j], y_r.at[4, j], down),
            remote(one, one, y_s.at[5, j], y_r.at[5, j], sib),
            remote(two, two, y_s.at[6, j], y_r.at[6, j], sib),
        ]

    def y_last(j):
        return remote(gall.at[far_m, j], gall.at[far_m, j], y_s.at[7, j], y_r.at[7, j], sib)

    def stage(step, behind, run):
        j = step - behind

        @pl.when(jnp.logical_and(j >= 0, j < NB))
        def _():
            run(j)

    def multiply(j):
        cols = pl.ds(pl.multiple_of(j * CB, CB), CB)
        for h in (1, 0):
            part = SCALING * jnp.dot(
                dyt[...],
                xbuf[h, :, :, :, cols].reshape(2 * SLOTS * TOK, CB),
                preferred_element_type=F32,
            )
            pbuf[j, h, 1] = part[ROWS:]
            if h:
                c1[0, j] = encode(part[:HALF])
                c1[1, j] = encode(part[HALF:ROWS])
                for copy in hop_one(j):
                    copy.start()
            else:
                pbuf[j, h, 0] = part[:ROWS]

    def add_one(j):
        for copy in hop_one(j):
            copy.wait_recv()
        pbuf[j, 1, 1, :HALF] = pbuf[j, 1, 1, :HALF] + decode(r1[0, j])
        pbuf[j, 0, 1, HALF:] = pbuf[j, 0, 1, HALF:] + decode(r1[1, j])
        c2[0, j] = encode(pbuf[j, 0, 1])
        c2[1, j] = encode(pbuf[j, 1, 1])
        for copy in hop_two(j):
            copy.start()

    def add_two(j):
        for copy in hop_two(j):
            copy.wait_recv()
        rout[j] = encode(pbuf[j, 0, 0] + decode(r2[0, j]) + decode(r2[1, j]))
        y_local(j).start()
        for copy in y_first(j):
            copy.start()

    def pass_on(j):
        for copy in y_first(j):
            copy.wait_recv()
        for copy in y_on(j):
            copy.start()

    def pass_last(j):
        for copy in y_on(j):
            copy.wait_recv()
        y_last(j).start()

    def finish(j):
        y_last(j).wait_recv()
        y_local(j).wait()
        for copy in hop_one(j) + hop_two(j) + y_first(j) + y_on(j) + [y_last(j)]:
            copy.wait_send()

    def pipeline_step(step, _):
        runs = (multiply, add_one, add_two, pass_on, pass_last, finish)
        for behind in reversed(range(len(runs))):
            stage(step, LAG * behind, runs[behind])
        return 0

    lax.fori_loop(0, NB + 5 * LAG, pipeline_step, 0)

    for i, (src, dst) in enumerate(state):
        for copy in state_on(i, dst):
            copy.wait_recv()
        state_last(i, dst).start()
    for i, (src, dst) in enumerate(state):
        state_last(i, dst).wait_recv()
        for copy in state_first(i, src, dst) + state_on(i, dst) + [state_last(i, dst)]:
            copy.wait_send()
    for copy in kept:
        copy.wait()
    swap.wait_send()
    for copy in inputs:
        copy.wait_send()
    for d in (0, 1):
        first(0, d, own_rows).wait_send()
        first(1, d, xbuf.at[1, 0, 0]).wait_send()

    def drain_ring(s, _):
        for h in (0, 1):
            for d in (0, 1):
                if d == h:
                    ring(h, s, d).wait_send()
                else:

                    @pl.when(s < SLOTS - 1)
                    def _():
                        ring(h, s, d).wait_send()

        return 0

    lax.fori_loop(1, SLOTS, drain_ring, 0)

    def drain_stats(k, _):
        early_copy(k).wait_send()
        late_copy(k).wait_send()
        return 0

    lax.fori_loop(1, ZN, drain_stats, 0)


def gather_gradients(ctx, w, m, v, tgt, ids):
    anywhere = pl.BlockSpec(memory_space=pl.ANY)
    dma = pltpu.SemaphoreType.DMA
    vmem = pltpu.VMEM
    return pl.pallas_call(
        gradient_kernel,
        out_shape=(
            jax.ShapeDtypeStruct((MEMBERS, NB, CODED, CB), jnp.int16),
            jax.ShapeDtypeStruct((MEMBERS, ROWS, COLS), BF16),
            jax.ShapeDtypeStruct((MEMBERS, NB, CODED, CB), jnp.int16),
            jax.ShapeDtypeStruct((MEMBERS, NB, CODED, CB), jnp.int16),
        ),
        in_specs=[anywhere] * 6,
        out_specs=(anywhere,) * 4,
        scratch_shapes=[
            vmem((2, SLOTS, 2, TOK, COLS), BF16),
            vmem((2, 2, ROWS, COLS), BF16),
            vmem((2, ZN, TOK, ROWS), BF16),
            vmem((ROWS, ROWS), BF16),
            vmem((SLOTS, 2 * ROWS, 2 * TOK), F32),
            vmem((SLOTS, 2 * ROWS, 2 * TOK), F32),
            vmem((2 * ROWS, SLOTS * 2 * TOK), BF16),
            vmem((ZN, 2 * TOK), F32),
            vmem((ZN, ZN, 2 * TOK), F32),
            vmem((2, 2 * TOK), F32),
            vmem((ZN, 2, 2 * TOK), F32),
            vmem((ZN, 2 * TOK), F32),
            vmem((NB, 2, 2, ROWS, CB), F32),
            vmem((2, NB, HALF + PAD, CB), jnp.int16),
            vmem((2, NB, HALF + PAD, CB), jnp.int16),
            vmem((2, NB, CODED, CB), jnp.int16),
            vmem((2, NB, CODED, CB), jnp.int16),
            vmem((NB, CODED, CB), jnp.int16),
            vmem((ROWS, COLS), F32),
            vmem((ROWS, COLS), F32),
            vmem((NB, CODED, CB), jnp.int16),
            vmem((NB, CODED, CB), jnp.int16),
            vmem((2 * ZN, 2 * TOK), jnp.int32),
            dma((9,)),
            dma((5,)),
            dma((5,)),
            dma((2, 2, SLOTS)),
            dma((2, 2, SLOTS)),
            dma((ZN,)),
            dma((ZN,)),
            dma((ZN,)),
            dma((ZN,)),
            dma((3, 8)),
            dma((3, 8)),
            dma((4, NB)),
            dma((4, NB)),
            dma((8, NB)),
            dma((8, NB)),
            dma((NB,)),
        ],
        compiler_params=pltpu.CompilerParams(
            collective_id=0, has_side_effects=True, vmem_limit_bytes=56 * 1024 * 1024
        ),
        cost_estimate=pl.CostEstimate(
            flops=4 * 1024 * HW * 2 * ROWS, bytes_accessed=20_000_000, transcendentals=0
        ),
    )(ctx, w, m, v, tgt, ids)


def update_kernel(
    partner, rates, levels, gall, wall, mall, vall, new_w, new_m, new_v,
    gbuf, wbuf, mbuf, vbuf, wout, mout, vout, in_sem, out_sem,
):
    p = partner[lax.axis_index("member")]

    def cols(j):
        return pl.ds(j * CB, CB)

    def take(j):
        return [
            pltpu.make_async_copy(gall.at[p, j], gbuf.at[j], in_sem.at[0, j]),
            pltpu.make_async_copy(mall.at[p, j], mbuf.at[j], in_sem.at[1, j]),
            pltpu.make_async_copy(vall.at[p, j], vbuf.at[j], in_sem.at[2, j]),
            pltpu.make_async_copy(wall.at[p, :, cols(j)], wbuf.at[j], in_sem.at[3, j]),
        ]

    def give(j):
        return [
            pltpu.make_async_copy(mout.at[j], new_m.at[:, cols(j)], out_sem.at[0, j]),
            pltpu.make_async_copy(vout.at[j], new_v.at[:, cols(j)], out_sem.at[1, j]),
            pltpu.make_async_copy(wout.at[j], new_w.at[:, cols(j)], out_sem.at[2, j]),
        ]

    for j in range(NB):
        for copy in take(j):
            copy.start()
    level = jnp.full((1, CB), levels[p].astype(F32), F32)
    step_size = rates[p] * 2.0 ** ((level - 4.0) / 4.0)
    for j in range(NB):
        for copy in take(j):
            copy.wait()
        gradient = decode(gbuf[j])
        first = beta_one * decode(mbuf[j]) + (1.0 - beta_one) * gradient
        second = beta_two * decode(vbuf[j]) + (1.0 - beta_two) * gradient * gradient
        mout[j] = first
        vout[j] = second
        wout[j] = (
            wbuf[j].astype(F32) - step_size * first / (jnp.sqrt(second) + adam_eps)
        ).astype(BF16)
        for copy in give(j):
            copy.start()
    for j in range(NB):
        for copy in give(j):
            copy.wait()


def update(partner, base_lr, perturb_index, gall, wall, mall, vall):
    smem = pl.BlockSpec(memory_space=pltpu.SMEM)
    anywhere = pl.BlockSpec(memory_space=pl.ANY)
    coded = pltpu.VMEM((NB, CODED, CB), jnp.int16)
    return pl.pallas_call(
        update_kernel,
        out_shape=(
            jax.ShapeDtypeStruct((ROWS, COLS), BF16),
            jax.ShapeDtypeStruct((ROWS, COLS), F32),
            jax.ShapeDtypeStruct((ROWS, COLS), F32),
        ),
        in_specs=[smem] * 3 + [anywhere] * 4,
        out_specs=(anywhere,) * 3,
        scratch_shapes=[
            coded,
            pltpu.VMEM((NB, ROWS, CB), BF16),
            coded,
            coded,
            pltpu.VMEM((NB, ROWS, CB), BF16),
            pltpu.VMEM((NB, ROWS, CB), F32),
            pltpu.VMEM((NB, ROWS, CB), F32),
            pltpu.SemaphoreType.DMA((4, NB)),
            pltpu.SemaphoreType.DMA((3, NB)),
        ],
        compiler_params=pltpu.CompilerParams(vmem_limit_bytes=56 * 1024 * 1024),
    )(partner, base_lr, perturb_index, gall, wall, mall, vall)


def body(
    context,
    out_weight,
    first_moment,
    second_moment,
    target,
    token_ids,
    base_lr,
    perturb_index,
    partner,
):
    gall, wall, mall, vall = gather_gradients(
        context[0, 0],
        out_weight[0],
        first_moment[0],
        second_moment[0],
        target[0].reshape(ZN, 2, TOK, ROWS),
        token_ids[0],
    )
    new_weight, new_first, new_second = update(
        partner.reshape(MEMBERS), base_lr, perturb_index, gall, wall, mall, vall
    )
    return (new_weight[None], new_first[None], new_second[None])


def solution(mesh):
    return jax.shard_map(
        body,
        mesh=mesh,
        in_specs=(
            P("member", "dp", None, "tensor"),
            P("member", "dp", "tensor"),
            P("member", "dp", "tensor"),
            P("member", "dp", "tensor"),
            P("member", None, "tensor", "dp"),
            P("member", None, None),
            P(),
            P(),
            P(None, "dp"),
        ),
        out_specs=(
            P("member", "dp", "tensor"),
            P("member", "dp", "tensor"),
            P("member", "dp", "tensor"),
        ),
        check_vma=False,
    )
```

```python
import math

import jax
import jax.numpy as jnp
from jax import lax
from jax.experimental import pallas as pl
from jax.experimental.pallas import tpu as pltpu
from jax.sharding import PartitionSpec as P

D = 5120
HW = 2560
MEMBERS = 8
ZN = 16
YN = 4
ROWS = 160
COLS = 1280
HALF = 80
TOK = 64
SLOTS = 8
CB = 256
NB = COLS // CB
PAD = 16
CODED = ROWS + PAD
TOP = 32000.0
LAG = 2
SCALING = 1.0 / math.sqrt(HW)

beta_one = 0.9
beta_two = 0.95
norm_eps = 1e-05
adam_eps = 1e-08

MESH = pl.DeviceIdType.MESH
F32 = jnp.float32
BF16 = jnp.bfloat16


def remote(src, dst, send_sem, recv_sem, device):
    return pltpu.make_async_remote_copy(
        src_ref=src,
        dst_ref=dst,
        send_sem=send_sem,
        recv_sem=recv_sem,
        device_id=device,
        device_id_type=MESH,
    )


def encode(values):
    top = jnp.max(jnp.abs(values), axis=0, keepdims=True)
    power = jnp.clip(jnp.ceil(jnp.log2(jnp.maximum(top, 1e-30))), -100.0, 126.0)
    codes = jnp.round(values * (TOP * jnp.exp2(-power)))
    powers = jnp.broadcast_to(power, (PAD, values.shape[1]))
    return jnp.concatenate([codes, powers], axis=0).astype(jnp.int32).astype(jnp.int16)


def decode(coded):
    wide = coded.astype(jnp.int32).astype(F32)
    rows = wide.shape[0] - PAD
    return wide[:rows] * (jnp.exp2(wide[rows : rows + 1]) * (1.0 / TOP))


def gradient_kernel(
    ctx,
    w,
    m,
    v,
    tgt,
    ids,
    gall,
    wall,
    mall,
    vall,
    xbuf,
    wbuf,
    tbuf,
    eye,
    yt,
    gt,
    dyt,
    rows_out,
    rows_in,
    own_out,
    own_in,
    late_out,
    late,
    pbuf,
    c1,
    r1,
    c2,
    r2,
    rout,
    mbuf,
    vbuf,
    mcode,
    vcode,
    idbuf,
    loc,
    in_s,
    in_r,
    z_s,
    z_r,
    e_s,
    e_r,
    o_s,
    o_r,
    l_s,
    l_r,
    st_s,
    st_r,
    x_s,
    x_r,
    y_s,
    y_r,
    y_l,
):
    mem = lax.axis_index("member")
    dp = lax.axis_index("dp")
    ten = lax.axis_index("tensor")
    yy, core = mem // 2, mem % 2
    zz, xl = dp // 2, dp % 2

    def at_z(k):
        return (mem, lax.rem(zz + k, ZN) * 2 + xl, ten)

    def member_at(k):
        return lax.rem(yy + k, YN) * 2 + core

    right, left = at_z(1), at_z(ZN - 1)
    dev_a = (mem, zz * 2 + 1 - xl, ten)
    dev_b = (mem, zz * 2 + 1 - xl, 1 - ten)
    dev_c = (mem, dp, 1 - ten)
    up_m, down_m, far_m = member_at(1), member_at(YN - 1), member_at(2)
    sib_m = yy * 2 + 1 - core
    up, down, sib = (up_m, dp, ten), (down_m, dp, ten), (sib_m, dp, ten)

    own_rows = ctx.at[pl.ds(pl.multiple_of(ten * TOK, TOK), TOK)]
    other_rows = ctx.at[pl.ds(pl.multiple_of((1 - ten) * TOK, TOK), TOK)]

    locals_ = [
        pltpu.make_async_copy(own_rows, xbuf.at[0, 0, 0], loc.at[0]),
        pltpu.make_async_copy(w, wbuf.at[0, 0], loc.at[1]),
        pltpu.make_async_copy(tgt.at[:, xl], tbuf.at[0], loc.at[2]),
        pltpu.make_async_copy(ids, idbuf, loc.at[3]),
    ]
    moments = [
        pltpu.make_async_copy(m, mbuf, loc.at[4]),
        pltpu.make_async_copy(v, vbuf, loc.at[5]),
    ]
    kept = [
        pltpu.make_async_copy(wbuf.at[0, 0], wall.at[mem], loc.at[6]),
        pltpu.make_async_copy(mcode, mall.at[mem], loc.at[7]),
        pltpu.make_async_copy(vcode, vall.at[mem], loc.at[8]),
    ]
    for copy in locals_ + moments:
        copy.start()

    barrier = pltpu.get_barrier_semaphore()

    neighbours = (right, left, dev_a, dev_b, dev_c, up, down, sib)
    for device in neighbours:
        pl.semaphore_signal(barrier, inc=1, device_id=device, device_id_type=MESH)
    pl.semaphore_wait(barrier, len(neighbours))

    swap = remote(other_rows, xbuf.at[1, 0, 0], in_s.at[0], in_r.at[0], dev_c)
    swap.start()

    def ring(h, s, d):
        dst = xbuf.at[h, lax.rem(s + 1, SLOTS), d if d else s // (SLOTS - 1)]
        return remote(
            xbuf.at[h, s, d],
            dst,
            z_s.at[d, h, s],
            z_r.at[d, h, lax.rem(s + 1, SLOTS)],
            left if d else right,
        )

    def first(h, d, src):
        return remote(
            src, xbuf.at[h, 1, d], z_s.at[d, h, 0], z_r.at[d, h, 1], left if d else right
        )

    for d in (0, 1):
        first(0, d, own_rows).start()
    inputs = [
        remote(w, wbuf.at[0, 1], in_s.at[1], in_r.at[1], dev_a),
        remote(w, wbuf.at[1, 1], in_s.at[2], in_r.at[2], dev_b),
        remote(w, wbuf.at[1, 0], in_s.at[3], in_r.at[3], dev_c),
        remote(tgt.at[:, 1 - xl], tbuf.at[1], in_s.at[4], in_r.at[4], dev_a),
    ]

    state = [(w, wall), (mcode, mall), (vcode, vall)]

    def state_first(i, src, dst):
        return [
            remote(src, dst.at[mem], st_s.at[i, 0], st_r.at[i, 0], up),
            remote(src, dst.at[mem], st_s.at[i, 1], st_r.at[i, 1], down),
            remote(src, dst.at[mem], st_s.at[i, 2], st_r.at[i, 2], sib),
        ]

    def state_on(i, dst):
        one, two = dst.at[down_m], dst.at[up_m]
        if i:
            low, high = pl.ds(0, HALF), pl.ds(HALF, CODED - HALF)
            one_low, two_high = one.at[:, low], two.at[:, high]
        else:
            one_low, two_high = one.at[pl.ds(0, HALF)], two.at[pl.ds(HALF, HALF)]
        return [
            remote(one_low, one_low, st_s.at[i, 3], st_r.at[i, 3], up),
            remote(two_high, two_high, st_s.at[i, 4], st_r.at[i, 4], down),
            remote(one, one, st_s.at[i, 5], st_r.at[i, 5], sib),
            remote(two, two, st_s.at[i, 6], st_r.at[i, 6], sib),
        ]

    def state_last(i, dst):
        return remote(dst.at[far_m], dst.at[far_m], st_s.at[i, 7], st_r.at[i, 7], sib)

    for copy in state_first(0, w, wall):
        copy.start()

    eye[...] = (
        lax.broadcasted_iota(jnp.int32, (ROWS, ROWS), 0)
        == lax.broadcasted_iota(jnp.int32, (ROWS, ROWS), 1)
    ).astype(BF16)
    lane = lax.broadcasted_iota(jnp.int32, (1, 2 * TOK), 1)
    low_lanes = lane < TOK

    swap.wait_recv()
    for d in (0, 1):
        first(1, d, xbuf.at[1, 0, 0]).start()
    for copy in inputs:
        copy.start()
    for copy in moments:
        copy.wait()

    def code_moments(j, _):
        cols = pl.ds(pl.multiple_of(j * CB, CB), CB)
        mcode[j] = encode(mbuf[:, cols])
        vcode[j] = encode(vbuf[:, cols])
        return 0

    lax.fori_loop(0, NB, code_moments, 0)
    for i in (1, 2):
        for copy in state_first(i, *state[i]):
            copy.start()
    for copy in locals_:
        copy.wait()
    for copy in kept:
        copy.start()

    def chunks_of(s):
        one = lax.rem(zz - s + ZN, ZN)
        two = lax.rem(zz + jnp.where(s == 0, SLOTS, s), ZN)
        return one, two

    def project(s):
        one, two = chunks_of(s)
        total = None
        for h in (0, 1):
            part = lax.dot_general(
                wbuf[h].reshape(2 * ROWS, COLS),
                xbuf[h, s].reshape(2 * TOK, COLS),
                (((1,), (1,)), ((), ())),
                preferred_element_type=F32,
            )
            total = part if total is None else total + part
        out = total * SCALING
        yt[s] = out
        goal = jnp.concatenate(
            [
                lax.dot_general(
                    eye[...],
                    jnp.concatenate([tbuf[side, one], tbuf[side, two]], axis=0),
                    (((1,), (1,)), ((), ())),
                    preferred_element_type=F32,
                )
                for side in (0, 1)
            ],
            axis=0,
        )
        gt[s] = goal
        squares = jnp.sum(out * out, axis=0, keepdims=True)
        crosses = jnp.sum(goal * out, axis=0, keepdims=True)
        row_one = jnp.where(low_lanes, squares, pltpu.roll(crosses, TOK, 1))
        row_two = jnp.where(low_lanes, pltpu.roll(squares, TOK, 1), crosses)
        return row_one, row_two

    def row_copies(s):
        return [
            remote(
                rows_out.at[2 * s + side],
                rows_in.at[zz],
                e_s.at[2 * s + side],
                e_r.at[zz],
                at_z(s if side else ZN - s),
            )
            for side in (0, 1)
        ]

    def project_early(s, _):
        row_one, row_two = project(s)

        @pl.when(s < SLOTS - 1)
        def _():
            rows_out[2 * s] = row_one
            rows_out[2 * s + 1] = row_two
            for copy in row_copies(s):
                copy.start()

        @pl.when(s == SLOTS - 1)
        def _():
            late_out[pl.ds(2, 1), :] = row_one
            late_out[pl.ds(3, 1), :] = row_two

        return 0

    def done_by(s):
        return jnp.where(s < 5, 0, 2 * (s - 4) + 1)

    def gather_step(s, _):
        for h in (0, 1):
            for d in (0, 1):
                remote(
                    xbuf.at[h, s, d], xbuf.at[h, s, d], z_s.at[d, h, s], z_r.at[d, h, s], right
                ).wait_recv()
                if d == h:
                    ring(h, s, d).start()
                else:

                    @pl.when(s < SLOTS - 1)
                    def _():
                        ring(h, s, d).start()

        @pl.when(s == 5)
        def _():
            for copy in inputs:
                copy.wait_recv()

        @pl.when(s == SLOTS - 2)
        def _():
            for i, (src, dst) in enumerate(state):
                for copy in state_first(i, src, dst):
                    copy.wait_recv()
                for copy in state_on(i, dst):
                    copy.start()

        lax.fori_loop(done_by(s - 1) + 1, done_by(s) + 1, project_early, 0)
        return 0

    lax.fori_loop(1, SLOTS, gather_step, 0)

    def own_copy(k):
        return remote(own_out, own_in.at[zz], o_s.at[k], o_r.at[zz], at_z(k))

    def late_copy(k):
        return remote(late_out, late.at[zz], l_s.at[k], l_r.at[zz], at_z(k))

    def take_row(k, total):
        src = lax.rem(zz + k, ZN)
        remote(own_out, rows_in.at[src], e_s.at[k], e_r.at[src], right).wait_recv()
        return total + rows_in[src]

    total = lax.fori_loop(1, SLOTS - 1, take_row, jnp.zeros((1, 2 * TOK), F32))
    total = lax.fori_loop(SLOTS + 2, ZN, take_row, total)
    own_out[...] = total
    own_in[zz] = total

    def send_own(k, _):
        own_copy(k).start()
        return 0

    lax.fori_loop(1, SLOTS, send_own, 0)
    lax.fori_loop(SLOTS + 1, ZN, send_own, 0)

    for h in (0, 1):
        remote(
            xbuf.at[h, 0, 1], xbuf.at[h, 0, 1], z_s.at[h, h, 0], z_r.at[h, h, 0], right
        ).wait_recv()
    own_copy(SLOTS).start()
    row_one, row_two = project(0)
    late_out[pl.ds(0, 1), :] = row_one
    late_out[pl.ds(1, 1), :] = row_two

    def send_late(k, _):
        late_copy(k).start()
        return 0

    lax.fori_loop(1, ZN, send_late, 0)
    late[zz] = late_out[...]

    def take_sums(k, _):
        src = lax.rem(zz + k, ZN)
        remote(own_out, own_in.at[src], o_s.at[k], o_r.at[src], right).wait_recv()
        remote(late_out, late.at[src], l_s.at[k], l_r.at[src], right).wait_recv()
        return 0

    lax.fori_loop(1, ZN, take_sums, 0)

    def total_row(c):
        total = own_in[c]
        for row, behind in enumerate((0, SLOTS, SLOTS - 1, SLOTS + 1)):
            total = total + late[lax.rem(c + behind, ZN), pl.ds(row, 1), :]
        return total

    def window_mask(c):
        row = idbuf[pl.ds(2 * c + xl, 1), :]
        return jnp.where(row != 0, 1.0, 0.0)

    def out_gradient(s, _):
        one, two = chunks_of(s)
        row_one, row_two = total_row(one), total_row(two)
        squares = jnp.where(low_lanes, row_one, pltpu.roll(row_two, TOK, 1))
        crosses = jnp.where(low_lanes, pltpu.roll(row_one, TOK, 1), row_two)
        mask_one, mask_two = window_mask(one), window_mask(two)
        first_half = jnp.where(low_lanes, mask_one, pltpu.roll(mask_two, TOK, 1))
        second_half = jnp.where(low_lanes, pltpu.roll(mask_one, TOK, 1), mask_two)
        mask = jnp.where(ten == 0, first_half, second_half)
        inverse = lax.rsqrt(squares / D + norm_eps)
        projection = mask * (inverse * inverse * squares - inverse * crosses) / D
        grad_out = yt[s] * (inverse * inverse * (mask - projection)) - gt[s] * (inverse * mask)
        dyt[:, pl.ds(pl.multiple_of(s * 2 * TOK, 2 * TOK), 2 * TOK)] = grad_out.astype(BF16)
        return 0

    lax.fori_loop(0, SLOTS, out_gradient, 0)

    low, high = pl.ds(0, HALF), pl.ds(HALF, CODED - HALF)

    def hop_one(j):
        return [
            remote(c1.at[0, j], r1.at[0, j], x_s.at[0, j], x_r.at[0, j], dev_a),
            remote(c1.at[1, j], r1.at[1, j], x_s.at[1, j], x_r.at[1, j], dev_b),
        ]

    def hop_two(j):
        return [
            remote(c2.at[0, j], r2.at[0, j], x_s.at[2, j], x_r.at[2, j], dev_a),
            remote(c2.at[1, j], r2.at[1, j], x_s.at[3, j], x_r.at[3, j], dev_b),
        ]

    def y_local(j):
        return pltpu.make_async_copy(rout.at[j], gall.at[mem, j], y_l.at[j])

    def y_first(j):
        return [
            remote(rout.at[j], gall.at[mem, j], y_s.at[0, j], y_r.at[0, j], up),
            remote(rout.at[j], gall.at[mem, j], y_s.at[1, j], y_r.at[1, j], down),
            remote(rout.at[j], gall.at[mem, j], y_s.at[2, j], y_r.at[2, j], sib),
        ]

    def y_on(j):
        one, two = gall.at[down_m, j], gall.at[up_m, j]
        return [
            remote(one.at[low], one.at[low], y_s.at[3, j], y_r.at[3, j], up),
            remote(two.at[high], two.at[high], y_s.at[4, j], y_r.at[4, j], down),
            remote(one, one, y_s.at[5, j], y_r.at[5, j], sib),
            remote(two, two, y_s.at[6, j], y_r.at[6, j], sib),
        ]

    def y_last(j):
        return remote(gall.at[far_m, j], gall.at[far_m, j], y_s.at[7, j], y_r.at[7, j], sib)

    def stage(step, behind, run):
        j = step - behind

        @pl.when(jnp.logical_and(j >= 0, j < NB))
        def _():
            run(j)

    def multiply(j):
        cols = pl.ds(pl.multiple_of(j * CB, CB), CB)
        for h in (1, 0):
            part = SCALING * jnp.dot(
                dyt[...],
                xbuf[h, :, :, :, cols].reshape(2 * SLOTS * TOK, CB),
                preferred_element_type=F32,
            )
            pbuf[j, h, 1] = part[ROWS:]
            if h:
                c1[0, j] = encode(part[:HALF])
                c1[1, j] = encode(part[HALF:ROWS])
                for copy in hop_one(j):
                    copy.start()
            else:
                pbuf[j, h, 0] = part[:ROWS]

    def add_one(j):
        for copy in hop_one(j):
            copy.wait_recv()
        pbuf[j, 1, 1, :HALF] = pbuf[j, 1, 1, :HALF] + decode(r1[0, j])
        pbuf[j, 0, 1, HALF:] = pbuf[j, 0, 1, HALF:] + decode(r1[1, j])
        c2[0, j] = encode(pbuf[j, 0, 1])
        c2[1, j] = encode(pbuf[j, 1, 1])
        for copy in hop_two(j):
            copy.start()

    def add_two(j):
        for copy in hop_two(j):
            copy.wait_recv()
        rout[j] = encode(pbuf[j, 0, 0] + decode(r2[0, j]) + decode(r2[1, j]))
        y_local(j).start()
        for copy in y_first(j):
            copy.start()

    def pass_on(j):
        for copy in y_first(j):
            copy.wait_recv()
        for copy in y_on(j):
            copy.start()

    def pass_last(j):
        for copy in y_on(j):
            copy.wait_recv()
        y_last(j).start()

    def finish(j):
        y_last(j).wait_recv()
        y_local(j).wait()
        for copy in hop_one(j) + hop_two(j) + y_first(j) + y_on(j) + [y_last(j)]:
            copy.wait_send()

    def pipeline_step(step, _):
        runs = (multiply, add_one, add_two, pass_on, pass_last, finish)
        for behind in reversed(range(len(runs))):
            stage(step, LAG * behind, runs[behind])
        return 0

    lax.fori_loop(0, NB + 5 * LAG, pipeline_step, 0)

    for i, (src, dst) in enumerate(state):
        for copy in state_on(i, dst):
            copy.wait_recv()
        state_last(i, dst).start()
    for i, (src, dst) in enumerate(state):
        state_last(i, dst).wait_recv()
        for copy in state_first(i, src, dst) + state_on(i, dst) + [state_last(i, dst)]:
            copy.wait_send()
    for copy in kept:
        copy.wait()
    swap.wait_send()
    for copy in inputs:
        copy.wait_send()
    for d in (0, 1):
        first(0, d, own_rows).wait_send()
        first(1, d, xbuf.at[1, 0, 0]).wait_send()

    def drain_ring(s, _):
        for h in (0, 1):
            for d in (0, 1):
                if d == h:
                    ring(h, s, d).wait_send()
                else:

                    @pl.when(s < SLOTS - 1)
                    def _():
                        ring(h, s, d).wait_send()

        return 0

    lax.fori_loop(1, SLOTS, drain_ring, 0)

    def drain_stats(k, _):
        own_copy(k).wait_send()
        late_copy(k).wait_send()
        return 0

    lax.fori_loop(1, ZN, drain_stats, 0)

    def drain_rows(s, _):
        for copy in row_copies(s):
            copy.wait_send()
        return 0

    lax.fori_loop(1, SLOTS - 1, drain_rows, 0)


def gather_gradients(ctx, w, m, v, tgt, ids):
    anywhere = pl.BlockSpec(memory_space=pl.ANY)
    dma = pltpu.SemaphoreType.DMA
    vmem = pltpu.VMEM
    return pl.pallas_call(
        gradient_kernel,
        out_shape=(
            jax.ShapeDtypeStruct((MEMBERS, NB, CODED, CB), jnp.int16),
            jax.ShapeDtypeStruct((MEMBERS, ROWS, COLS), BF16),
            jax.ShapeDtypeStruct((MEMBERS, NB, CODED, CB), jnp.int16),
            jax.ShapeDtypeStruct((MEMBERS, NB, CODED, CB), jnp.int16),
        ),
        in_specs=[anywhere] * 6,
        out_specs=(anywhere,) * 4,
        scratch_shapes=[
            vmem((2, SLOTS, 2, TOK, COLS), BF16),
            vmem((2, 2, ROWS, COLS), BF16),
            vmem((2, ZN, TOK, ROWS), BF16),
            vmem((ROWS, ROWS), BF16),
            vmem((SLOTS, 2 * ROWS, 2 * TOK), F32),
            vmem((SLOTS, 2 * ROWS, 2 * TOK), F32),
            vmem((2 * ROWS, SLOTS * 2 * TOK), BF16),
            vmem((2 * SLOTS, 1, 2 * TOK), F32),
            vmem((ZN, 1, 2 * TOK), F32),
            vmem((1, 2 * TOK), F32),
            vmem((ZN, 1, 2 * TOK), F32),
            vmem((4, 2 * TOK), F32),
            vmem((ZN, 4, 2 * TOK), F32),
            vmem((NB, 2, 2, ROWS, CB), F32),
            vmem((2, NB, HALF + PAD, CB), jnp.int16),
            vmem((2, NB, HALF + PAD, CB), jnp.int16),
            vmem((2, NB, CODED, CB), jnp.int16),
            vmem((2, NB, CODED, CB), jnp.int16),
            vmem((NB, CODED, CB), jnp.int16),
            vmem((ROWS, COLS), F32),
            vmem((ROWS, COLS), F32),
            vmem((NB, CODED, CB), jnp.int16),
            vmem((NB, CODED, CB), jnp.int16),
            vmem((2 * ZN, 2 * TOK), jnp.int32),
            dma((9,)),
            dma((5,)),
            dma((5,)),
            dma((2, 2, SLOTS)),
            dma((2, 2, SLOTS)),
            dma((ZN,)),
            dma((ZN,)),
            dma((ZN,)),
            dma((ZN,)),
            dma((ZN,)),
            dma((ZN,)),
            dma((3, 8)),
            dma((3, 8)),
            dma((4, NB)),
            dma((4, NB)),
            dma((8, NB)),
            dma((8, NB)),
            dma((NB,)),
        ],
        compiler_params=pltpu.CompilerParams(
            collective_id=0, has_side_effects=True, vmem_limit_bytes=56 * 1024 * 1024
        ),
        cost_estimate=pl.CostEstimate(
            flops=4 * 1024 * HW * 2 * ROWS, bytes_accessed=20_000_000, transcendentals=0
        ),
    )(ctx, w, m, v, tgt, ids)


def update_kernel(
    partner, rates, levels, gall, wall, mall, vall, new_w, new_m, new_v,
    gbuf, wbuf, mbuf, vbuf, wout, mout, vout, in_sem, out_sem,
):
    p = partner[lax.axis_index("member")]

    def cols(j):
        return pl.ds(j * CB, CB)

    def take(j):
        return [
            pltpu.make_async_copy(gall.at[p, j], gbuf.at[j], in_sem.at[0, j]),
            pltpu.make_async_copy(mall.at[p, j], mbuf.at[j], in_sem.at[1, j]),
            pltpu.make_async_copy(vall.at[p, j], vbuf.at[j], in_sem.at[2, j]),
            pltpu.make_async_copy(wall.at[p, :, cols(j)], wbuf.at[j], in_sem.at[3, j]),
        ]

    def give(j):
        return [
            pltpu.make_async_copy(mout.at[j], new_m.at[:, cols(j)], out_sem.at[0, j]),
            pltpu.make_async_copy(vout.at[j], new_v.at[:, cols(j)], out_sem.at[1, j]),
            pltpu.make_async_copy(wout.at[j], new_w.at[:, cols(j)], out_sem.at[2, j]),
        ]

    for j in range(NB):
        for copy in take(j):
            copy.start()
    level = jnp.full((1, CB), levels[p].astype(F32), F32)
    step_size = rates[p] * 2.0 ** ((level - 4.0) / 4.0)
    for j in range(NB):
        for copy in take(j):
            copy.wait()
        gradient = decode(gbuf[j])
        first = beta_one * decode(mbuf[j]) + (1.0 - beta_one) * gradient
        second = beta_two * decode(vbuf[j]) + (1.0 - beta_two) * gradient * gradient
        mout[j] = first
        vout[j] = second
        wout[j] = (
            wbuf[j].astype(F32) - step_size * first / (jnp.sqrt(second) + adam_eps)
        ).astype(BF16)
        for copy in give(j):
            copy.start()
    for j in range(NB):
        for copy in give(j):
            copy.wait()


def update(partner, base_lr, perturb_index, gall, wall, mall, vall):
    smem = pl.BlockSpec(memory_space=pltpu.SMEM)
    anywhere = pl.BlockSpec(memory_space=pl.ANY)
    coded = pltpu.VMEM((NB, CODED, CB), jnp.int16)
    return pl.pallas_call(
        update_kernel,
        out_shape=(
            jax.ShapeDtypeStruct((ROWS, COLS), BF16),
            jax.ShapeDtypeStruct((ROWS, COLS), F32),
            jax.ShapeDtypeStruct((ROWS, COLS), F32),
        ),
        in_specs=[smem] * 3 + [anywhere] * 4,
        out_specs=(anywhere,) * 3,
        scratch_shapes=[
            coded,
            pltpu.VMEM((NB, ROWS, CB), BF16),
            coded,
            coded,
            pltpu.VMEM((NB, ROWS, CB), BF16),
            pltpu.VMEM((NB, ROWS, CB), F32),
            pltpu.VMEM((NB, ROWS, CB), F32),
            pltpu.SemaphoreType.DMA((4, NB)),
            pltpu.SemaphoreType.DMA((3, NB)),
        ],
        compiler_params=pltpu.CompilerParams(vmem_limit_bytes=56 * 1024 * 1024),
    )(partner, base_lr, perturb_index, gall, wall, mall, vall)


def body(
    context,
    out_weight,
    first_moment,
    second_moment,
    target,
    token_ids,
    base_lr,
    perturb_index,
    partner,
):
    gall, wall, mall, vall = gather_gradients(
        context[0, 0],
        out_weight[0],
        first_moment[0],
        second_moment[0],
        target[0].reshape(ZN, 2, TOK, ROWS),
        token_ids[0],
    )
    new_weight, new_first, new_second = update(
        partner.reshape(MEMBERS), base_lr, perturb_index, gall, wall, mall, vall
    )
    return (new_weight[None], new_first[None], new_second[None])


def solution(mesh):
    return jax.shard_map(
        body,
        mesh=mesh,
        in_specs=(
            P("member", "dp", None, "tensor"),
            P("member", "dp", "tensor"),
            P("member", "dp", "tensor"),
            P("member", "dp", "tensor"),
            P("member", None, "tensor", "dp"),
            P("member", None, None),
            P(),
            P(),
            P(None, "dp"),
        ),
        out_specs=(
            P("member", "dp", "tensor"),
            P("member", "dp", "tensor"),
            P("member", "dp", "tensor"),
        ),
        check_vma=False,
    )
```

```python
import math

import jax
import jax.numpy as jnp
from jax import lax
from jax.experimental import pallas as pl
from jax.experimental.pallas import tpu as pltpu
from jax.sharding import PartitionSpec as P

D = 5120
HW = 2560
MEMBERS = 8
ZN = 16
YN = 4
ROWS = 160
COLS = 1280
HALF = 80
TOK = 64
SLOTS = 8
CB = 256
NB = COLS // CB
PAD = 16
CODED = ROWS + PAD
TOP = 32000.0
LAG = 2
SCALING = 1.0 / math.sqrt(HW)

beta_one = 0.9
beta_two = 0.95
norm_eps = 1e-05
adam_eps = 1e-08

MESH = pl.DeviceIdType.MESH
F32 = jnp.float32
BF16 = jnp.bfloat16


def remote(src, dst, send_sem, recv_sem, device):
    return pltpu.make_async_remote_copy(
        src_ref=src,
        dst_ref=dst,
        send_sem=send_sem,
        recv_sem=recv_sem,
        device_id=device,
        device_id_type=MESH,
    )


def encode(values):
    top = jnp.max(jnp.abs(values), axis=0, keepdims=True)
    power = jnp.clip(jnp.ceil(jnp.log2(jnp.maximum(top, 1e-30))), -100.0, 126.0)
    codes = jnp.round(values * (TOP * jnp.exp2(-power)))
    powers = jnp.broadcast_to(power, (PAD, values.shape[1]))
    return jnp.concatenate([codes, powers], axis=0).astype(jnp.int32).astype(jnp.int16)


def decode(coded):
    wide = coded.astype(jnp.int32).astype(F32)
    rows = wide.shape[0] - PAD
    return wide[:rows] * (jnp.exp2(wide[rows : rows + 1]) * (1.0 / TOP))


def gradient_kernel(
    ctx,
    w,
    m,
    v,
    tgt,
    ids,
    gall,
    wall,
    mall,
    vall,
    xbuf,
    wbuf,
    tbuf,
    eye,
    yt,
    gt,
    dyt,
    rows_out,
    rows_in,
    own_out,
    own_in,
    late_out,
    late,
    pbuf,
    c1,
    r1,
    c2,
    r2,
    rout,
    mbuf,
    vbuf,
    mcode,
    vcode,
    idbuf,
    loc,
    in_s,
    in_r,
    z_s,
    z_r,
    e_s,
    e_r,
    o_s,
    o_r,
    l_s,
    l_r,
    st_s,
    st_r,
    x_s,
    x_r,
    y_s,
    y_r,
    y_l,
):
    mem = lax.axis_index("member")
    dp = lax.axis_index("dp")
    ten = lax.axis_index("tensor")
    yy, core = mem // 2, mem % 2
    zz, xl = dp // 2, dp % 2

    def at_z(k):
        return (mem, lax.rem(zz + k, ZN) * 2 + xl, ten)

    def member_at(k):
        return lax.rem(yy + k, YN) * 2 + core

    right, left = at_z(1), at_z(ZN - 1)
    dev_a = (mem, zz * 2 + 1 - xl, ten)
    dev_b = (mem, zz * 2 + 1 - xl, 1 - ten)
    dev_c = (mem, dp, 1 - ten)
    up_m, down_m, far_m = member_at(1), member_at(YN - 1), member_at(2)
    sib_m = yy * 2 + 1 - core
    up, down, sib = (up_m, dp, ten), (down_m, dp, ten), (sib_m, dp, ten)

    own_rows = ctx.at[pl.ds(pl.multiple_of(ten * TOK, TOK), TOK)]
    other_rows = ctx.at[pl.ds(pl.multiple_of((1 - ten) * TOK, TOK), TOK)]

    locals_ = [
        pltpu.make_async_copy(own_rows, xbuf.at[0, 0, 0], loc.at[0]),
        pltpu.make_async_copy(w, wbuf.at[0, 0], loc.at[1]),
        pltpu.make_async_copy(tgt.at[:, xl], tbuf.at[0], loc.at[2]),
        pltpu.make_async_copy(ids, idbuf, loc.at[3]),
    ]
    moments = [
        pltpu.make_async_copy(m, mbuf, loc.at[4]),
        pltpu.make_async_copy(v, vbuf, loc.at[5]),
    ]
    kept = [
        pltpu.make_async_copy(wbuf.at[0, 0], wall.at[mem], loc.at[6]),
        pltpu.make_async_copy(mcode, mall.at[mem], loc.at[7]),
        pltpu.make_async_copy(vcode, vall.at[mem], loc.at[8]),
    ]
    for copy in locals_ + moments:
        copy.start()

    barrier = pltpu.get_barrier_semaphore()

    neighbours = (right, left, dev_a, dev_b, dev_c, up, down, sib)
    for device in neighbours:
        pl.semaphore_signal(barrier, inc=1, device_id=device, device_id_type=MESH)
    pl.semaphore_wait(barrier, len(neighbours))

    swap = remote(other_rows, xbuf.at[1, 0, 0], in_s.at[0], in_r.at[0], dev_c)
    swap.start()

    def ring(h, s, d):
        dst = xbuf.at[h, lax.rem(s + 1, SLOTS), d if d else s // (SLOTS - 1)]
        return remote(
            xbuf.at[h, s, d],
            dst,
            z_s.at[d, h, s],
            z_r.at[d, h, lax.rem(s + 1, SLOTS)],
            left if d else right,
        )

    def first(h, d, src):
        return remote(
            src, xbuf.at[h, 1, d], z_s.at[d, h, 0], z_r.at[d, h, 1], left if d else right
        )

    for d in (0, 1):
        first(0, d, own_rows).start()
    inputs = [
        remote(w, wbuf.at[0, 1], in_s.at[1], in_r.at[1], dev_a),
        remote(w, wbuf.at[1, 1], in_s.at[2], in_r.at[2], dev_b),
        remote(w, wbuf.at[1, 0], in_s.at[3], in_r.at[3], dev_c),
        remote(tgt.at[:, 1 - xl], tbuf.at[1], in_s.at[4], in_r.at[4], dev_a),
    ]

    state = [(w, wall), (mcode, mall), (vcode, vall)]

    def state_first(i, src, dst):
        return [
            remote(src, dst.at[mem], st_s.at[i, 0], st_r.at[i, 0], up),
            remote(src, dst.at[mem], st_s.at[i, 1], st_r.at[i, 1], down),
            remote(src, dst.at[mem], st_s.at[i, 2], st_r.at[i, 2], sib),
        ]

    def state_on(i, dst):
        one, two = dst.at[down_m], dst.at[up_m]
        if i:
            low, high = pl.ds(0, HALF), pl.ds(HALF, CODED - HALF)
            one_low, two_high = one.at[:, low], two.at[:, high]
        else:
            one_low, two_high = one.at[pl.ds(0, HALF)], two.at[pl.ds(HALF, HALF)]
        return [
            remote(one_low, one_low, st_s.at[i, 3], st_r.at[i, 3], up),
            remote(two_high, two_high, st_s.at[i, 4], st_r.at[i, 4], down),
            remote(one, one, st_s.at[i, 5], st_r.at[i, 5], sib),
            remote(two, two, st_s.at[i, 6], st_r.at[i, 6], sib),
        ]

    def state_last(i, dst):
        return remote(dst.at[far_m], dst.at[far_m], st_s.at[i, 7], st_r.at[i, 7], sib)

    for copy in state_first(0, w, wall):
        copy.start()

    eye[...] = (
        lax.broadcasted_iota(jnp.int32, (ROWS, ROWS), 0)
        == lax.broadcasted_iota(jnp.int32, (ROWS, ROWS), 1)
    ).astype(BF16)
    lane = lax.broadcasted_iota(jnp.int32, (1, 2 * TOK), 1)
    low_lanes = lane < TOK

    swap.wait_recv()
    for d in (0, 1):
        first(1, d, xbuf.at[1, 0, 0]).start()
    for copy in inputs:
        copy.start()
    for copy in moments:
        copy.wait()

    def code_moments(j, _):
        cols = pl.ds(pl.multiple_of(j * CB, CB), CB)
        mcode[j] = encode(mbuf[:, cols])
        vcode[j] = encode(vbuf[:, cols])
        return 0

    lax.fori_loop(0, NB, code_moments, 0)
    for i in (1, 2):
        for copy in state_first(i, *state[i]):
            copy.start()
    for copy in locals_:
        copy.wait()
    for copy in kept:
        copy.start()

    def chunks_of(s):
        one = lax.rem(zz - s + ZN, ZN)
        two = lax.rem(zz + jnp.where(s == 0, SLOTS, s), ZN)
        return one, two

    def project(s):
        one, two = chunks_of(s)
        total = None
        for h in (0, 1):
            part = lax.dot_general(
                wbuf[h].reshape(2 * ROWS, COLS),
                xbuf[h, s].reshape(2 * TOK, COLS),
                (((1,), (1,)), ((), ())),
                preferred_element_type=F32,
            )
            total = part if total is None else total + part
        out = total * SCALING
        yt[s] = out
        goal = jnp.concatenate(
            [
                lax.dot_general(
                    eye[...],
                    jnp.concatenate([tbuf[side, one], tbuf[side, two]], axis=0),
                    (((1,), (1,)), ((), ())),
                    preferred_element_type=F32,
                )
                for side in (0, 1)
            ],
            axis=0,
        )
        gt[s] = goal
        squares = jnp.sum(out * out, axis=0, keepdims=True)
        crosses = jnp.sum(goal * out, axis=0, keepdims=True)
        row_one = jnp.where(low_lanes, squares, pltpu.roll(crosses, TOK, 1))
        row_two = jnp.where(low_lanes, pltpu.roll(squares, TOK, 1), crosses)
        return row_one, row_two

    def row_copies(s):
        return [
            remote(
                rows_out.at[2 * s + side],
                rows_in.at[zz],
                e_s.at[2 * s + side],
                e_r.at[zz],
                at_z(s if side else ZN - s),
            )
            for side in (0, 1)
        ]

    def project_early(s, _):
        row_one, row_two = project(s)

        @pl.when(s < SLOTS - 1)
        def _():
            rows_out[2 * s] = row_one
            rows_out[2 * s + 1] = row_two
            for copy in row_copies(s):
                copy.start()

        @pl.when(s == SLOTS - 1)
        def _():
            late_out[pl.ds(2, 1), :] = row_one
            late_out[pl.ds(3, 1), :] = row_two

        return 0

    def done_by(s):
        return jnp.where(s < 5, 0, 2 * (s - 4) + 1)

    def gather_step(s, _):
        for h in (0, 1):
            for d in (0, 1):
                remote(
                    xbuf.at[h, s, d], xbuf.at[h, s, d], z_s.at[d, h, s], z_r.at[d, h, s], right
                ).wait_recv()
                if d == h:
                    ring(h, s, d).start()
                else:

                    @pl.when(s < SLOTS - 1)
                    def _():
                        ring(h, s, d).start()

        @pl.when(s == 5)
        def _():
            for copy in inputs:
                copy.wait_recv()

        @pl.when(s == SLOTS - 2)
        def _():
            for i, (src, dst) in enumerate(state):
                for copy in state_first(i, src, dst):
                    copy.wait_recv()
                for copy in state_on(i, dst):
                    copy.start()

        lax.fori_loop(done_by(s - 1) + 1, done_by(s) + 1, project_early, 0)
        return 0

    lax.fori_loop(1, SLOTS, gather_step, 0)

    def own_copy(k):
        return remote(own_out, own_in.at[zz], o_s.at[k], o_r.at[zz], at_z(k))

    def late_copy(k):
        return remote(late_out, late.at[zz], l_s.at[k], l_r.at[zz], at_z(k))

    def take_row(k, total):
        src = lax.rem(zz + k, ZN)
        remote(own_out, rows_in.at[src], e_s.at[k], e_r.at[src], right).wait_recv()
        return total + rows_in[src]

    total = lax.fori_loop(1, SLOTS - 1, take_row, jnp.zeros((1, 2 * TOK), F32))
    total = lax.fori_loop(SLOTS + 2, ZN, take_row, total)
    own_out[...] = total
    own_in[zz] = total

    def send_own(k, _):
        own_copy(k).start()
        return 0

    lax.fori_loop(1, SLOTS, send_own, 0)
    lax.fori_loop(SLOTS + 1, ZN, send_own, 0)

    for h in (0, 1):
        remote(
            xbuf.at[h, 0, 1], xbuf.at[h, 0, 1], z_s.at[h, h, 0], z_r.at[h, h, 0], right
        ).wait_recv()
    own_copy(SLOTS).start()
    row_one, row_two = project(0)
    late_out[pl.ds(0, 1), :] = row_one
    late_out[pl.ds(1, 1), :] = row_two

    def send_late(k, _):
        late_copy(k).start()
        return 0

    lax.fori_loop(1, ZN, send_late, 0)
    late[zz] = late_out[...]

    for i, (src, dst) in enumerate(state):
        for copy in state_on(i, dst):
            copy.wait_recv()
        state_last(i, dst).start()
    for copy in kept:
        copy.wait()
    swap.wait_send()
    for copy in inputs:
        copy.wait_send()
    for d in (0, 1):
        first(0, d, own_rows).wait_send()
        first(1, d, xbuf.at[1, 0, 0]).wait_send()

    def drain_ring(s, _):
        for h in (0, 1):
            for d in (0, 1):
                if d == h:
                    ring(h, s, d).wait_send()
                else:

                    @pl.when(s < SLOTS - 1)
                    def _():
                        ring(h, s, d).wait_send()

        return 0

    lax.fori_loop(1, SLOTS, drain_ring, 0)

    def drain_rows(s, _):
        for copy in row_copies(s):
            copy.wait_send()
        return 0

    lax.fori_loop(1, SLOTS - 1, drain_rows, 0)

    def take_sums(k, _):
        src = lax.rem(zz + k, ZN)
        remote(own_out, own_in.at[src], o_s.at[k], o_r.at[src], right).wait_recv()
        remote(late_out, late.at[src], l_s.at[k], l_r.at[src], right).wait_recv()
        return 0

    lax.fori_loop(1, ZN, take_sums, 0)

    def total_row(c):
        total = own_in[c]
        for row, behind in enumerate((0, SLOTS, SLOTS - 1, SLOTS + 1)):
            total = total + late[lax.rem(c + behind, ZN), pl.ds(row, 1), :]
        return total

    def window_mask(c):
        row = idbuf[pl.ds(2 * c + xl, 1), :]
        return jnp.where(row != 0, 1.0, 0.0)

    def out_gradient(s, _):
        one, two = chunks_of(s)
        row_one, row_two = total_row(one), total_row(two)
        squares = jnp.where(low_lanes, row_one, pltpu.roll(row_two, TOK, 1))
        crosses = jnp.where(low_lanes, pltpu.roll(row_one, TOK, 1), row_two)
        mask_one, mask_two = window_mask(one), window_mask(two)
        first_half = jnp.where(low_lanes, mask_one, pltpu.roll(mask_two, TOK, 1))
        second_half = jnp.where(low_lanes, pltpu.roll(mask_one, TOK, 1), mask_two)
        mask = jnp.where(ten == 0, first_half, second_half)
        inverse = lax.rsqrt(squares / D + norm_eps)
        projection = mask * (inverse * inverse * squares - inverse * crosses) / D
        grad_out = yt[s] * (inverse * inverse * (mask - projection)) - gt[s] * (inverse * mask)
        dyt[:, pl.ds(pl.multiple_of(s * 2 * TOK, 2 * TOK), 2 * TOK)] = grad_out.astype(BF16)
        return 0

    lax.fori_loop(0, SLOTS, out_gradient, 0)

    low, high = pl.ds(0, HALF), pl.ds(HALF, CODED - HALF)

    def hop_one(j):
        return [
            remote(c1.at[0, j], r1.at[0, j], x_s.at[0, j], x_r.at[0, j], dev_a),
            remote(c1.at[1, j], r1.at[1, j], x_s.at[1, j], x_r.at[1, j], dev_b),
        ]

    def hop_two(j):
        return [
            remote(c2.at[0, j], r2.at[0, j], x_s.at[2, j], x_r.at[2, j], dev_a),
            remote(c2.at[1, j], r2.at[1, j], x_s.at[3, j], x_r.at[3, j], dev_b),
        ]

    def y_local(j):
        return pltpu.make_async_copy(rout.at[j], gall.at[mem, j], y_l.at[j])

    def y_first(j):
        return [
            remote(rout.at[j], gall.at[mem, j], y_s.at[0, j], y_r.at[0, j], up),
            remote(rout.at[j], gall.at[mem, j], y_s.at[1, j], y_r.at[1, j], down),
            remote(rout.at[j], gall.at[mem, j], y_s.at[2, j], y_r.at[2, j], sib),
        ]

    def y_on(j):
        one, two = gall.at[down_m, j], gall.at[up_m, j]
        return [
            remote(one.at[low], one.at[low], y_s.at[3, j], y_r.at[3, j], up),
            remote(two.at[high], two.at[high], y_s.at[4, j], y_r.at[4, j], down),
            remote(one, one, y_s.at[5, j], y_r.at[5, j], sib),
            remote(two, two, y_s.at[6, j], y_r.at[6, j], sib),
        ]

    def y_last(j):
        return remote(gall.at[far_m, j], gall.at[far_m, j], y_s.at[7, j], y_r.at[7, j], sib)

    def stage(step, behind, run):
        j = step - behind

        @pl.when(jnp.logical_and(j >= 0, j < NB))
        def _():
            run(j)

    def multiply(j):
        cols = pl.ds(pl.multiple_of(j * CB, CB), CB)
        for h in (1, 0):
            part = SCALING * jnp.dot(
                dyt[...],
                xbuf[h, :, :, :, cols].reshape(2 * SLOTS * TOK, CB),
                preferred_element_type=F32,
            )
            pbuf[j, h, 1] = part[ROWS:]
            if h:
                c1[0, j] = encode(part[:HALF])
                c1[1, j] = encode(part[HALF:ROWS])
                for copy in hop_one(j):
                    copy.start()
            else:
                pbuf[j, h, 0] = part[:ROWS]

    def add_one(j):
        for copy in hop_one(j):
            copy.wait_recv()
        pbuf[j, 1, 1, :HALF] = pbuf[j, 1, 1, :HALF] + decode(r1[0, j])
        pbuf[j, 0, 1, HALF:] = pbuf[j, 0, 1, HALF:] + decode(r1[1, j])
        c2[0, j] = encode(pbuf[j, 0, 1])
        c2[1, j] = encode(pbuf[j, 1, 1])
        for copy in hop_two(j):
            copy.start()

    def add_two(j):
        for copy in hop_two(j):
            copy.wait_recv()
        rout[j] = encode(pbuf[j, 0, 0] + decode(r2[0, j]) + decode(r2[1, j]))
        y_local(j).start()
        for copy in y_first(j):
            copy.start()

    def pass_on(j):
        for copy in y_first(j):
            copy.wait_recv()
        for copy in y_on(j):
            copy.start()

    def pass_last(j):
        for copy in y_on(j):
            copy.wait_recv()
        y_last(j).start()

    def finish(j):
        y_last(j).wait_recv()
        y_local(j).wait()
        for copy in hop_one(j) + hop_two(j) + y_first(j) + y_on(j) + [y_last(j)]:
            copy.wait_send()

    def drain_stats(k, _):
        own_copy(k).wait_send()
        late_copy(k).wait_send()
        return 0

    def pipeline_step(step, _):
        runs = (multiply, add_one, add_two, pass_on, pass_last, finish)
        for behind in reversed(range(len(runs))):
            stage(step, LAG * behind, runs[behind])

        @pl.when(step == NB)
        def _():
            lax.fori_loop(1, ZN, drain_stats, 0)
            for i, (src, dst) in enumerate(state):
                state_last(i, dst).wait_recv()
                for copy in state_first(i, src, dst) + state_on(i, dst) + [state_last(i, dst)]:
                    copy.wait_send()

        return 0

    lax.fori_loop(0, NB + 5 * LAG, pipeline_step, 0)


def gather_gradients(ctx, w, m, v, tgt, ids):
    anywhere = pl.BlockSpec(memory_space=pl.ANY)
    dma = pltpu.SemaphoreType.DMA
    vmem = pltpu.VMEM
    return pl.pallas_call(
        gradient_kernel,
        out_shape=(
            jax.ShapeDtypeStruct((MEMBERS, NB, CODED, CB), jnp.int16),
            jax.ShapeDtypeStruct((MEMBERS, ROWS, COLS), BF16),
            jax.ShapeDtypeStruct((MEMBERS, NB, CODED, CB), jnp.int16),
            jax.ShapeDtypeStruct((MEMBERS, NB, CODED, CB), jnp.int16),
        ),
        in_specs=[anywhere] * 6,
        out_specs=(anywhere,) * 4,
        scratch_shapes=[
            vmem((2, SLOTS, 2, TOK, COLS), BF16),
            vmem((2, 2, ROWS, COLS), BF16),
            vmem((2, ZN, TOK, ROWS), BF16),
            vmem((ROWS, ROWS), BF16),
            vmem((SLOTS, 2 * ROWS, 2 * TOK), F32),
            vmem((SLOTS, 2 * ROWS, 2 * TOK), F32),
            vmem((2 * ROWS, SLOTS * 2 * TOK), BF16),
            vmem((2 * SLOTS, 1, 2 * TOK), F32),
            vmem((ZN, 1, 2 * TOK), F32),
            vmem((1, 2 * TOK), F32),
            vmem((ZN, 1, 2 * TOK), F32),
            vmem((4, 2 * TOK), F32),
            vmem((ZN, 4, 2 * TOK), F32),
            vmem((NB, 2, 2, ROWS, CB), F32),
            vmem((2, NB, HALF + PAD, CB), jnp.int16),
            vmem((2, NB, HALF + PAD, CB), jnp.int16),
            vmem((2, NB, CODED, CB), jnp.int16),
            vmem((2, NB, CODED, CB), jnp.int16),
            vmem((NB, CODED, CB), jnp.int16),
            vmem((ROWS, COLS), F32),
            vmem((ROWS, COLS), F32),
            vmem((NB, CODED, CB), jnp.int16),
            vmem((NB, CODED, CB), jnp.int16),
            vmem((2 * ZN, 2 * TOK), jnp.int32),
            dma((9,)),
            dma((5,)),
            dma((5,)),
            dma((2, 2, SLOTS)),
            dma((2, 2, SLOTS)),
            dma((ZN,)),
            dma((ZN,)),
            dma((ZN,)),
            dma((ZN,)),
            dma((ZN,)),
            dma((ZN,)),
            dma((3, 8)),
            dma((3, 8)),
            dma((4, NB)),
            dma((4, NB)),
            dma((8, NB)),
            dma((8, NB)),
            dma((NB,)),
        ],
        compiler_params=pltpu.CompilerParams(
            collective_id=0, has_side_effects=True, vmem_limit_bytes=56 * 1024 * 1024
        ),
        cost_estimate=pl.CostEstimate(
            flops=4 * 1024 * HW * 2 * ROWS, bytes_accessed=20_000_000, transcendentals=0
        ),
    )(ctx, w, m, v, tgt, ids)


def update_kernel(
    partner, rates, levels, gall, wall, mall, vall, new_w, new_m, new_v,
    gbuf, wbuf, mbuf, vbuf, wout, mout, vout, in_sem, out_sem,
):
    p = partner[lax.axis_index("member")]

    def cols(j):
        return pl.ds(j * CB, CB)

    def take(j):
        return [
            pltpu.make_async_copy(gall.at[p, j], gbuf.at[j], in_sem.at[0, j]),
            pltpu.make_async_copy(mall.at[p, j], mbuf.at[j], in_sem.at[1, j]),
            pltpu.make_async_copy(vall.at[p, j], vbuf.at[j], in_sem.at[2, j]),
            pltpu.make_async_copy(wall.at[p, :, cols(j)], wbuf.at[j], in_sem.at[3, j]),
        ]

    def give(j):
        return [
            pltpu.make_async_copy(mout.at[j], new_m.at[:, cols(j)], out_sem.at[0, j]),
            pltpu.make_async_copy(vout.at[j], new_v.at[:, cols(j)], out_sem.at[1, j]),
            pltpu.make_async_copy(wout.at[j], new_w.at[:, cols(j)], out_sem.at[2, j]),
        ]

    for j in range(NB):
        for copy in take(j):
            copy.start()
    level = jnp.full((1, CB), levels[p].astype(F32), F32)
    step_size = rates[p] * 2.0 ** ((level - 4.0) / 4.0)
    for j in range(NB):
        for copy in take(j):
            copy.wait()
        gradient = decode(gbuf[j])
        first = beta_one * decode(mbuf[j]) + (1.0 - beta_one) * gradient
        second = beta_two * decode(vbuf[j]) + (1.0 - beta_two) * gradient * gradient
        mout[j] = first
        vout[j] = second
        wout[j] = (
            wbuf[j].astype(F32) - step_size * first / (jnp.sqrt(second) + adam_eps)
        ).astype(BF16)
        for copy in give(j):
            copy.start()
    for j in range(NB):
        for copy in give(j):
            copy.wait()


def update(partner, base_lr, perturb_index, gall, wall, mall, vall):
    smem = pl.BlockSpec(memory_space=pltpu.SMEM)
    anywhere = pl.BlockSpec(memory_space=pl.ANY)
    coded = pltpu.VMEM((NB, CODED, CB), jnp.int16)
    return pl.pallas_call(
        update_kernel,
        out_shape=(
            jax.ShapeDtypeStruct((ROWS, COLS), BF16),
            jax.ShapeDtypeStruct((ROWS, COLS), F32),
            jax.ShapeDtypeStruct((ROWS, COLS), F32),
        ),
        in_specs=[smem] * 3 + [anywhere] * 4,
        out_specs=(anywhere,) * 3,
        scratch_shapes=[
            coded,
            pltpu.VMEM((NB, ROWS, CB), BF16),
            coded,
            coded,
            pltpu.VMEM((NB, ROWS, CB), BF16),
            pltpu.VMEM((NB, ROWS, CB), F32),
            pltpu.VMEM((NB, ROWS, CB), F32),
            pltpu.SemaphoreType.DMA((4, NB)),
            pltpu.SemaphoreType.DMA((3, NB)),
        ],
        compiler_params=pltpu.CompilerParams(vmem_limit_bytes=56 * 1024 * 1024),
    )(partner, base_lr, perturb_index, gall, wall, mall, vall)


def body(
    context,
    out_weight,
    first_moment,
    second_moment,
    target,
    token_ids,
    base_lr,
    perturb_index,
    partner,
):
    gall, wall, mall, vall = gather_gradients(
        context[0, 0],
        out_weight[0],
        first_moment[0],
        second_moment[0],
        target[0].reshape(ZN, 2, TOK, ROWS),
        token_ids[0],
    )
    new_weight, new_first, new_second = update(
        partner.reshape(MEMBERS), base_lr, perturb_index, gall, wall, mall, vall
    )
    return (new_weight[None], new_first[None], new_second[None])


def solution(mesh):
    return jax.shard_map(
        body,
        mesh=mesh,
        in_specs=(
            P("member", "dp", None, "tensor"),
            P("member", "dp", "tensor"),
            P("member", "dp", "tensor"),
            P("member", "dp", "tensor"),
            P("member", None, "tensor", "dp"),
            P("member", None, None),
            P(),
            P(),
            P(None, "dp"),
        ),
        out_specs=(
            P("member", "dp", "tensor"),
            P("member", "dp", "tensor"),
            P("member", "dp", "tensor"),
        ),
        check_vma=False,
    )
```

```python
import math

import jax
import jax.numpy as jnp
from jax import lax
from jax.experimental import pallas as pl
from jax.experimental.pallas import tpu as pltpu
from jax.sharding import PartitionSpec as P

D = 5120
HW = 2560
MEMBERS = 8
ZN = 16
YN = 4
ROWS = 160
COLS = 1280
HALF = 80
TOK = 64
SLOTS = 8
CB = 128
NP = COLS // CB
NB = 6
PART = 32
PAD = 16
CODED = ROWS + PAD
TOP = 32000.0
LAG = 2
SCALING = 1.0 / math.sqrt(HW)

beta_one = 0.9
beta_two = 0.95
norm_eps = 1e-05
adam_eps = 1e-08

MESH = pl.DeviceIdType.MESH
F32 = jnp.float32
BF16 = jnp.bfloat16


def remote(src, dst, send_sem, recv_sem, device):
    return pltpu.make_async_remote_copy(
        src_ref=src,
        dst_ref=dst,
        send_sem=send_sem,
        recv_sem=recv_sem,
        device_id=device,
        device_id_type=MESH,
    )


def encode(values):
    top = jnp.max(jnp.abs(values), axis=0, keepdims=True)
    power = jnp.clip(jnp.ceil(jnp.log2(jnp.maximum(top, 1e-30))), -100.0, 126.0)
    codes = jnp.round(values * (TOP * jnp.exp2(-power)))
    powers = jnp.broadcast_to(power, (PAD, values.shape[1]))
    return jnp.concatenate([codes, powers], axis=0).astype(jnp.int32).astype(jnp.int16)


def decode(coded):
    wide = coded.astype(jnp.int32).astype(F32)
    rows = wide.shape[0] - PAD
    return wide[:rows] * (jnp.exp2(wide[rows : rows + 1]) * (1.0 / TOP))


def gradient_kernel(
    ctx,
    w,
    m,
    v,
    tgt,
    ids,
    gall,
    wall,
    mall,
    vall,
    xbuf,
    wbuf,
    tbuf,
    eye,
    yt,
    gt,
    dyt,
    rows_out,
    rows_in,
    own_out,
    own_in,
    late_out,
    late,
    pbuf,
    c1,
    r1,
    c2,
    r2,
    rout,
    mbuf,
    vbuf,
    mcode,
    vcode,
    idbuf,
    loc,
    in_s,
    in_r,
    z_s,
    z_r,
    e_s,
    e_r,
    o_s,
    o_r,
    l_s,
    l_r,
    st_s,
    st_r,
    x_s,
    x_r,
    y_s,
    y_r,
    y_l,
):
    mem = lax.axis_index("member")
    dp = lax.axis_index("dp")
    ten = lax.axis_index("tensor")
    yy, core = mem // 2, mem % 2
    zz, xl = dp // 2, dp % 2

    def at_z(k):
        return (mem, lax.rem(zz + k, ZN) * 2 + xl, ten)

    def member_at(k):
        return lax.rem(yy + k, YN) * 2 + core

    right, left = at_z(1), at_z(ZN - 1)
    dev_a = (mem, zz * 2 + 1 - xl, ten)
    dev_b = (mem, zz * 2 + 1 - xl, 1 - ten)
    dev_c = (mem, dp, 1 - ten)
    up_m, down_m, far_m = member_at(1), member_at(YN - 1), member_at(2)
    sib_m = yy * 2 + 1 - core
    up, down, sib = (up_m, dp, ten), (down_m, dp, ten), (sib_m, dp, ten)

    own_rows = ctx.at[pl.ds(pl.multiple_of(ten * TOK, TOK), TOK)]
    other_rows = ctx.at[pl.ds(pl.multiple_of((1 - ten) * TOK, TOK), TOK)]

    locals_ = [
        pltpu.make_async_copy(own_rows, xbuf.at[0, 0, 0], loc.at[0]),
        pltpu.make_async_copy(w, wbuf.at[0, 0], loc.at[1]),
        pltpu.make_async_copy(tgt.at[:, xl], tbuf.at[0], loc.at[2]),
        pltpu.make_async_copy(ids, idbuf, loc.at[3]),
    ]
    moments = [
        pltpu.make_async_copy(m, mbuf, loc.at[4]),
        pltpu.make_async_copy(v, vbuf, loc.at[5]),
    ]
    kept = [
        pltpu.make_async_copy(wbuf.at[0, 0], wall.at[mem], loc.at[6]),
        pltpu.make_async_copy(mcode, mall.at[mem], loc.at[7]),
        pltpu.make_async_copy(vcode, vall.at[mem], loc.at[8]),
    ]
    for copy in locals_ + moments:
        copy.start()

    barrier = pltpu.get_barrier_semaphore()

    neighbours = (right, left, dev_a, dev_b, dev_c, up, down, sib)
    for device in neighbours:
        pl.semaphore_signal(barrier, inc=1, device_id=device, device_id_type=MESH)
    pl.semaphore_wait(barrier, len(neighbours))

    swaps = [
        remote(
            other_rows.at[pl.ds(part * PART, PART)],
            xbuf.at[1, 0, 0, pl.ds(part * PART, PART)],
            in_s.at[4 + part],
            in_r.at[4 + part],
            dev_c,
        )
        for part in range(TOK // PART)
    ]
    for copy in swaps:
        copy.start()

    messages = [(h, part) for h in (0, 1) for part in range(TOK // PART)]

    def rows_of(part):
        return pl.ds(part * PART, PART)

    def ring(h, part, s, d):
        dst = xbuf.at[h, lax.rem(s + 1, SLOTS), d if d else s // (SLOTS - 1), rows_of(part)]
        return remote(
            xbuf.at[h, s, d, rows_of(part)],
            dst,
            z_s.at[d, h, part, s],
            z_r.at[d, h, part, lax.rem(s + 1, SLOTS)],
            left if d else right,
        )

    def arrived(h, part, s, d):
        dst = xbuf.at[h, s, d, rows_of(part)]
        remote(dst, dst, z_s.at[d, h, part, s], z_r.at[d, h, part, s], right).wait_recv()

    def first(h, part, d, src):
        return remote(
            src.at[rows_of(part)],
            xbuf.at[h, 1, d, rows_of(part)],
            z_s.at[d, h, part, 0],
            z_r.at[d, h, part, 1],
            left if d else right,
        )

    for part in range(TOK // PART):
        for d in (0, 1):
            first(0, part, d, own_rows).start()
    inputs = [
        remote(w, wbuf.at[0, 1], in_s.at[1], in_r.at[1], dev_a),
        remote(w, wbuf.at[1, 1], in_s.at[2], in_r.at[2], dev_b),
        remote(w, wbuf.at[1, 0], in_s.at[3], in_r.at[3], dev_c),
        remote(tgt.at[:, 1 - xl], tbuf.at[1], in_s.at[0], in_r.at[0], dev_a),
    ]

    state = [(w, wall), (mcode, mall), (vcode, vall)]

    def state_first(i, src, dst):
        return [
            remote(src, dst.at[mem], st_s.at[i, 0], st_r.at[i, 0], up),
            remote(src, dst.at[mem], st_s.at[i, 1], st_r.at[i, 1], down),
            remote(src, dst.at[mem], st_s.at[i, 2], st_r.at[i, 2], sib),
        ]

    def state_on(i, dst):
        one, two = dst.at[down_m], dst.at[up_m]
        if i:
            low, high = pl.ds(0, HALF), pl.ds(HALF, CODED - HALF)
            one_low, two_high = one.at[:, low], two.at[:, high]
        else:
            one_low, two_high = one.at[pl.ds(0, HALF)], two.at[pl.ds(HALF, HALF)]
        return [
            remote(one_low, one_low, st_s.at[i, 3], st_r.at[i, 3], up),
            remote(two_high, two_high, st_s.at[i, 4], st_r.at[i, 4], down),
            remote(one, one, st_s.at[i, 5], st_r.at[i, 5], sib),
            remote(two, two, st_s.at[i, 6], st_r.at[i, 6], sib),
        ]

    def state_last(i, dst):
        return remote(dst.at[far_m], dst.at[far_m], st_s.at[i, 7], st_r.at[i, 7], sib)

    for copy in state_first(0, w, wall):
        copy.start()

    eye[...] = (
        lax.broadcasted_iota(jnp.int32, (ROWS, ROWS), 0)
        == lax.broadcasted_iota(jnp.int32, (ROWS, ROWS), 1)
    ).astype(BF16)
    lane = lax.broadcasted_iota(jnp.int32, (1, 2 * TOK), 1)
    low_lanes = lane < TOK

    for part, swap in enumerate(swaps):
        swap.wait_recv()
        for d in (0, 1):
            first(1, part, d, xbuf.at[1, 0, 0]).start()
    for copy in inputs:
        copy.start()
    for copy in moments:
        copy.wait()

    def code_moments(j, _):
        cols = pl.ds(pl.multiple_of(j * CB, CB), CB)
        mcode[j] = encode(mbuf[:, cols])
        vcode[j] = encode(vbuf[:, cols])
        return 0

    lax.fori_loop(0, NP, code_moments, 0)
    for i in (1, 2):
        for copy in state_first(i, *state[i]):
            copy.start()
    for copy in locals_:
        copy.wait()
    for copy in kept:
        copy.start()

    def chunks_of(s):
        one = lax.rem(zz - s + ZN, ZN)
        two = lax.rem(zz + jnp.where(s == 0, SLOTS, s), ZN)
        return one, two

    def project(s):
        one, two = chunks_of(s)
        total = None
        for h in (0, 1):
            part = lax.dot_general(
                wbuf[h].reshape(2 * ROWS, COLS),
                xbuf[h, s].reshape(2 * TOK, COLS),
                (((1,), (1,)), ((), ())),
                preferred_element_type=F32,
            )
            total = part if total is None else total + part
        out = total * SCALING
        yt[s] = out
        goal = jnp.concatenate(
            [
                lax.dot_general(
                    eye[...],
                    jnp.concatenate([tbuf[side, one], tbuf[side, two]], axis=0),
                    (((1,), (1,)), ((), ())),
                    preferred_element_type=F32,
                )
                for side in (0, 1)
            ],
            axis=0,
        )
        gt[s] = goal
        squares = jnp.sum(out * out, axis=0, keepdims=True)
        crosses = jnp.sum(goal * out, axis=0, keepdims=True)
        row_one = jnp.where(low_lanes, squares, pltpu.roll(crosses, TOK, 1))
        row_two = jnp.where(low_lanes, pltpu.roll(squares, TOK, 1), crosses)
        return row_one, row_two

    def row_copies(s):
        return [
            remote(
                rows_out.at[2 * s + side],
                rows_in.at[zz],
                e_s.at[2 * s + side],
                e_r.at[zz],
                at_z(s if side else ZN - s),
            )
            for side in (0, 1)
        ]

    def project_early(s, _):
        row_one, row_two = project(s)

        @pl.when(s < SLOTS - 1)
        def _():
            rows_out[2 * s] = row_one
            rows_out[2 * s + 1] = row_two
            for copy in row_copies(s):
                copy.start()

        @pl.when(s == SLOTS - 1)
        def _():
            late_out[pl.ds(2, 1), :] = row_one
            late_out[pl.ds(3, 1), :] = row_two

        return 0

    def done_by(s):
        return jnp.where(s < 5, 0, 2 * (s - 4) + 1)

    def gather_step(s, _):
        for h, part in messages:
            for d in (0, 1):
                arrived(h, part, s, d)
                if d == h:
                    ring(h, part, s, d).start()
                else:

                    @pl.when(s < SLOTS - 1)
                    def _():
                        ring(h, part, s, d).start()

        @pl.when(s == 5)
        def _():
            for copy in inputs:
                copy.wait_recv()

        @pl.when(s == SLOTS - 2)
        def _():
            for i, (src, dst) in enumerate(state):
                for copy in state_first(i, src, dst):
                    copy.wait_recv()
                for copy in state_on(i, dst):
                    copy.start()

        lax.fori_loop(done_by(s - 1) + 1, done_by(s) + 1, project_early, 0)
        return 0

    lax.fori_loop(1, SLOTS, gather_step, 0)

    def own_copy(k):
        return remote(own_out, own_in.at[zz], o_s.at[k], o_r.at[zz], at_z(k))

    def late_copy(k):
        return remote(late_out, late.at[zz], l_s.at[k], l_r.at[zz], at_z(k))

    def take_row(k, total):
        src = lax.rem(zz + k, ZN)
        remote(own_out, rows_in.at[src], e_s.at[k], e_r.at[src], right).wait_recv()
        return total + rows_in[src]

    total = lax.fori_loop(1, SLOTS - 1, take_row, jnp.zeros((1, 2 * TOK), F32))
    total = lax.fori_loop(SLOTS + 2, ZN, take_row, total)
    own_out[...] = total
    own_in[zz] = total

    def send_own(k, _):
        own_copy(k).start()
        return 0

    lax.fori_loop(1, SLOTS, send_own, 0)
    lax.fori_loop(SLOTS + 1, ZN, send_own, 0)

    for h, part in messages:
        dst = xbuf.at[h, 0, 1, rows_of(part)]
        remote(dst, dst, z_s.at[h, h, part, 0], z_r.at[h, h, part, 0], right).wait_recv()
    own_copy(SLOTS).start()
    row_one, row_two = project(0)
    late_out[pl.ds(0, 1), :] = row_one
    late_out[pl.ds(1, 1), :] = row_two

    def send_late(k, _):
        late_copy(k).start()
        return 0

    lax.fori_loop(1, ZN, send_late, 0)
    late[zz] = late_out[...]

    for i, (src, dst) in enumerate(state):
        for copy in state_on(i, dst):
            copy.wait_recv()
        state_last(i, dst).start()
    for copy in kept:
        copy.wait()
    for copy in inputs + swaps:
        copy.wait_send()
    for part in range(TOK // PART):
        for d in (0, 1):
            first(0, part, d, own_rows).wait_send()
            first(1, part, d, xbuf.at[1, 0, 0]).wait_send()

    def drain_ring(s, _):
        for h, part in messages:
            for d in (0, 1):
                if d == h:
                    ring(h, part, s, d).wait_send()
                else:

                    @pl.when(s < SLOTS - 1)
                    def _():
                        ring(h, part, s, d).wait_send()

        return 0

    lax.fori_loop(1, SLOTS, drain_ring, 0)

    def drain_rows(s, _):
        for copy in row_copies(s):
            copy.wait_send()
        return 0

    lax.fori_loop(1, SLOTS - 1, drain_rows, 0)

    def take_sums(k, _):
        src = lax.rem(zz + k, ZN)
        remote(own_out, own_in.at[src], o_s.at[k], o_r.at[src], right).wait_recv()
        remote(late_out, late.at[src], l_s.at[k], l_r.at[src], right).wait_recv()
        return 0

    lax.fori_loop(1, ZN, take_sums, 0)

    def total_row(c):
        total = own_in[c]
        for row, behind in enumerate((0, SLOTS, SLOTS - 1, SLOTS + 1)):
            total = total + late[lax.rem(c + behind, ZN), pl.ds(row, 1), :]
        return total

    def window_mask(c):
        row = idbuf[pl.ds(2 * c + xl, 1), :]
        return jnp.where(row != 0, 1.0, 0.0)

    def out_gradient(s, _):
        one, two = chunks_of(s)
        row_one, row_two = total_row(one), total_row(two)
        squares = jnp.where(low_lanes, row_one, pltpu.roll(row_two, TOK, 1))
        crosses = jnp.where(low_lanes, pltpu.roll(row_one, TOK, 1), row_two)
        mask_one, mask_two = window_mask(one), window_mask(two)
        first_half = jnp.where(low_lanes, mask_one, pltpu.roll(mask_two, TOK, 1))
        second_half = jnp.where(low_lanes, pltpu.roll(mask_one, TOK, 1), mask_two)
        mask = jnp.where(ten == 0, first_half, second_half)
        inverse = lax.rsqrt(squares / D + norm_eps)
        projection = mask * (inverse * inverse * squares - inverse * crosses) / D
        grad_out = yt[s] * (inverse * inverse * (mask - projection)) - gt[s] * (inverse * mask)
        dyt[:, pl.ds(pl.multiple_of(s * 2 * TOK, 2 * TOK), 2 * TOK)] = grad_out.astype(BF16)
        return 0

    lax.fori_loop(0, SLOTS, out_gradient, 0)

    low, high = pl.ds(0, HALF), pl.ds(HALF, CODED - HALF)

    def pieces(j, n):
        return pl.ds(jnp.maximum(2 * j - 1, 0), n)

    def hop_one(j, n):
        at = pieces(j, n)
        return [
            remote(c1.at[0, at], r1.at[0, at], x_s.at[0, j], x_r.at[0, j], dev_a),
            remote(c1.at[1, at], r1.at[1, at], x_s.at[1, j], x_r.at[1, j], dev_b),
        ]

    def hop_two(j, n):
        at = pieces(j, n)
        return [
            remote(c2.at[0, at], r2.at[0, at], x_s.at[2, j], x_r.at[2, j], dev_a),
            remote(c2.at[1, at], r2.at[1, at], x_s.at[3, j], x_r.at[3, j], dev_b),
        ]

    def y_local(j, n):
        at = pieces(j, n)
        return pltpu.make_async_copy(rout.at[at], gall.at[mem, at], y_l.at[j])

    def y_first(j, n):
        at = pieces(j, n)
        return [
            remote(rout.at[at], gall.at[mem, at], y_s.at[0, j], y_r.at[0, j], up),
            remote(rout.at[at], gall.at[mem, at], y_s.at[1, j], y_r.at[1, j], down),
            remote(rout.at[at], gall.at[mem, at], y_s.at[2, j], y_r.at[2, j], sib),
        ]

    def y_on(j, n):
        at = pieces(j, n)
        one, two = gall.at[down_m, at], gall.at[up_m, at]
        return [
            remote(one.at[:, low], one.at[:, low], y_s.at[3, j], y_r.at[3, j], up),
            remote(two.at[:, high], two.at[:, high], y_s.at[4, j], y_r.at[4, j], down),
            remote(one, one, y_s.at[5, j], y_r.at[5, j], sib),
            remote(two, two, y_s.at[6, j], y_r.at[6, j], sib),
        ]

    def y_last(j, n):
        far = gall.at[far_m, pieces(j, n)]
        return remote(far, far, y_s.at[7, j], y_r.at[7, j], sib)

    def stage(step, behind, run):
        j = step - behind

        @pl.when(jnp.logical_or(j == 0, j == NB - 1))
        def _():
            run(j, 1)

        @pl.when(jnp.logical_and(j > 0, j < NB - 1))
        def _():
            run(j, 2)

    def multiply(j, n):
        at = jnp.maximum(2 * j - 1, 0)
        cols = pl.ds(pl.multiple_of(at * CB, CB), n * CB)
        for h in (1, 0):
            block = SCALING * jnp.dot(
                dyt[...],
                xbuf[h, :, :, :, cols].reshape(2 * SLOTS * TOK, n * CB),
                preferred_element_type=F32,
            )
            for i in range(n):
                part = block[:, i * CB : (i + 1) * CB]
                pbuf[at + i, h, 1] = part[ROWS:]
                if h:
                    c1[0, at + i] = encode(part[:HALF])
                    c1[1, at + i] = encode(part[HALF:ROWS])
                else:
                    pbuf[at + i, h, 0] = part[:ROWS]
            if h:
                for copy in hop_one(j, n):
                    copy.start()

    def add_one(j, n):
        for copy in hop_one(j, n):
            copy.wait_recv()
        for i in range(n):
            k = jnp.maximum(2 * j - 1, 0) + i
            pbuf[k, 1, 1, :HALF] = pbuf[k, 1, 1, :HALF] + decode(r1[0, k])
            pbuf[k, 0, 1, HALF:] = pbuf[k, 0, 1, HALF:] + decode(r1[1, k])
            c2[0, k] = encode(pbuf[k, 0, 1])
            c2[1, k] = encode(pbuf[k, 1, 1])
        for copy in hop_two(j, n):
            copy.start()

    def add_two(j, n):
        for copy in hop_two(j, n):
            copy.wait_recv()
        for i in range(n):
            k = jnp.maximum(2 * j - 1, 0) + i
            rout[k] = encode(pbuf[k, 0, 0] + decode(r2[0, k]) + decode(r2[1, k]))
        y_local(j, n).start()
        for copy in y_first(j, n):
            copy.start()

    def pass_on(j, n):
        for copy in y_first(j, n):
            copy.wait_recv()
        for copy in y_on(j, n):
            copy.start()

    def pass_last(j, n):
        for copy in y_on(j, n):
            copy.wait_recv()
        y_last(j, n).start()

    def finish(j, n):
        y_last(j, n).wait_recv()
        y_local(j, n).wait()
        for copy in (
            hop_one(j, n) + hop_two(j, n) + y_first(j, n) + y_on(j, n) + [y_last(j, n)]
        ):
            copy.wait_send()

    def drain_stats(k, _):
        own_copy(k).wait_send()
        late_copy(k).wait_send()
        return 0

    def pipeline_step(step, _):
        runs = (multiply, add_one, add_two, pass_on, pass_last, finish)
        for behind in reversed(range(len(runs))):
            stage(step, LAG * behind, runs[behind])

        @pl.when(step == NB)
        def _():
            lax.fori_loop(1, ZN, drain_stats, 0)
            for i, (src, dst) in enumerate(state):
                state_last(i, dst).wait_recv()
                for copy in state_first(i, src, dst) + state_on(i, dst) + [state_last(i, dst)]:
                    copy.wait_send()

        return 0

    lax.fori_loop(0, NB + 5 * LAG, pipeline_step, 0)


def gather_gradients(ctx, w, m, v, tgt, ids):
    anywhere = pl.BlockSpec(memory_space=pl.ANY)
    dma = pltpu.SemaphoreType.DMA
    vmem = pltpu.VMEM
    return pl.pallas_call(
        gradient_kernel,
        out_shape=(
            jax.ShapeDtypeStruct((MEMBERS, NP, CODED, CB), jnp.int16),
            jax.ShapeDtypeStruct((MEMBERS, ROWS, COLS), BF16),
            jax.ShapeDtypeStruct((MEMBERS, NP, CODED, CB), jnp.int16),
            jax.ShapeDtypeStruct((MEMBERS, NP, CODED, CB), jnp.int16),
        ),
        in_specs=[anywhere] * 6,
        out_specs=(anywhere,) * 4,
        scratch_shapes=[
            vmem((2, SLOTS, 2, TOK, COLS), BF16),
            vmem((2, 2, ROWS, COLS), BF16),
            vmem((2, ZN, TOK, ROWS), BF16),
            vmem((ROWS, ROWS), BF16),
            vmem((SLOTS, 2 * ROWS, 2 * TOK), F32),
            vmem((SLOTS, 2 * ROWS, 2 * TOK), F32),
            vmem((2 * ROWS, SLOTS * 2 * TOK), BF16),
            vmem((2 * SLOTS, 1, 2 * TOK), F32),
            vmem((ZN, 1, 2 * TOK), F32),
            vmem((1, 2 * TOK), F32),
            vmem((ZN, 1, 2 * TOK), F32),
            vmem((4, 2 * TOK), F32),
            vmem((ZN, 4, 2 * TOK), F32),
            vmem((NP, 2, 2, ROWS, CB), F32),
            vmem((2, NP, HALF + PAD, CB), jnp.int16),
            vmem((2, NP, HALF + PAD, CB), jnp.int16),
            vmem((2, NP, CODED, CB), jnp.int16),
            vmem((2, NP, CODED, CB), jnp.int16),
            vmem((NP, CODED, CB), jnp.int16),
            vmem((ROWS, COLS), F32),
            vmem((ROWS, COLS), F32),
            vmem((NP, CODED, CB), jnp.int16),
            vmem((NP, CODED, CB), jnp.int16),
            vmem((2 * ZN, 2 * TOK), jnp.int32),
            dma((9,)),
            dma((6,)),
            dma((6,)),
            dma((2, 2, TOK // PART, SLOTS)),
            dma((2, 2, TOK // PART, SLOTS)),
            dma((ZN,)),
            dma((ZN,)),
            dma((ZN,)),
            dma((ZN,)),
            dma((ZN,)),
            dma((ZN,)),
            dma((3, 8)),
            dma((3, 8)),
            dma((4, NB)),
            dma((4, NB)),
            dma((8, NB)),
            dma((8, NB)),
            dma((NB,)),
        ],
        compiler_params=pltpu.CompilerParams(
            collective_id=0, has_side_effects=True, vmem_limit_bytes=56 * 1024 * 1024
        ),
        cost_estimate=pl.CostEstimate(
            flops=4 * 1024 * HW * 2 * ROWS, bytes_accessed=20_000_000, transcendentals=0
        ),
    )(ctx, w, m, v, tgt, ids)


def update_kernel(
    partner, rates, levels, gall, wall, mall, vall, new_w, new_m, new_v,
    gbuf, wbuf, mbuf, vbuf, wout, mout, vout, in_sem, out_sem,
):
    p = partner[lax.axis_index("member")]

    def cols(j):
        return pl.ds(j * 2 * CB, 2 * CB)

    def pair(j):
        return pl.ds(2 * j, 2)

    def take(j):
        return [
            pltpu.make_async_copy(gall.at[p, pair(j)], gbuf.at[pair(j)], in_sem.at[0, j]),
            pltpu.make_async_copy(mall.at[p, pair(j)], mbuf.at[pair(j)], in_sem.at[1, j]),
            pltpu.make_async_copy(vall.at[p, pair(j)], vbuf.at[pair(j)], in_sem.at[2, j]),
            pltpu.make_async_copy(wall.at[p, :, cols(j)], wbuf.at[j], in_sem.at[3, j]),
        ]

    def give(j):
        return [
            pltpu.make_async_copy(mout.at[j], new_m.at[:, cols(j)], out_sem.at[0, j]),
            pltpu.make_async_copy(vout.at[j], new_v.at[:, cols(j)], out_sem.at[1, j]),
            pltpu.make_async_copy(wout.at[j], new_w.at[:, cols(j)], out_sem.at[2, j]),
        ]

    for j in range(NP // 2):
        for copy in take(j):
            copy.start()
    level = jnp.full((1, CB), levels[p].astype(F32), F32)
    step_size = rates[p] * 2.0 ** ((level - 4.0) / 4.0)
    for j in range(NP // 2):
        for copy in take(j):
            copy.wait()
        for i in range(2):
            k, at = 2 * j + i, slice(i * CB, (i + 1) * CB)
            gradient = decode(gbuf[k])
            first = beta_one * decode(mbuf[k]) + (1.0 - beta_one) * gradient
            second = beta_two * decode(vbuf[k]) + (1.0 - beta_two) * gradient * gradient
            mout[j, :, at] = first
            vout[j, :, at] = second
            wout[j, :, at] = (
                wbuf[j, :, at].astype(F32) - step_size * first / (jnp.sqrt(second) + adam_eps)
            ).astype(BF16)
        for copy in give(j):
            copy.start()
    for j in range(NP // 2):
        for copy in give(j):
            copy.wait()


def update(partner, base_lr, perturb_index, gall, wall, mall, vall):
    smem = pl.BlockSpec(memory_space=pltpu.SMEM)
    anywhere = pl.BlockSpec(memory_space=pl.ANY)
    coded = pltpu.VMEM((NP, CODED, CB), jnp.int16)
    return pl.pallas_call(
        update_kernel,
        out_shape=(
            jax.ShapeDtypeStruct((ROWS, COLS), BF16),
            jax.ShapeDtypeStruct((ROWS, COLS), F32),
            jax.ShapeDtypeStruct((ROWS, COLS), F32),
        ),
        in_specs=[smem] * 3 + [anywhere] * 4,
        out_specs=(anywhere,) * 3,
        scratch_shapes=[
            coded,
            pltpu.VMEM((NP // 2, ROWS, 2 * CB), BF16),
            coded,
            coded,
            pltpu.VMEM((NP // 2, ROWS, 2 * CB), BF16),
            pltpu.VMEM((NP // 2, ROWS, 2 * CB), F32),
            pltpu.VMEM((NP // 2, ROWS, 2 * CB), F32),
            pltpu.SemaphoreType.DMA((4, NP // 2)),
            pltpu.SemaphoreType.DMA((3, NP // 2)),
        ],
        compiler_params=pltpu.CompilerParams(vmem_limit_bytes=56 * 1024 * 1024),
    )(partner, base_lr, perturb_index, gall, wall, mall, vall)


def body(
    context,
    out_weight,
    first_moment,
    second_moment,
    target,
    token_ids,
    base_lr,
    perturb_index,
    partner,
):
    gall, wall, mall, vall = gather_gradients(
        context[0, 0],
        out_weight[0],
        first_moment[0],
        second_moment[0],
        target[0].reshape(ZN, 2, TOK, ROWS),
        token_ids[0],
    )
    new_weight, new_first, new_second = update(
        partner.reshape(MEMBERS), base_lr, perturb_index, gall, wall, mall, vall
    )
    return (new_weight[None], new_first[None], new_second[None])


def solution(mesh):
    return jax.shard_map(
        body,
        mesh=mesh,
        in_specs=(
            P("member", "dp", None, "tensor"),
            P("member", "dp", "tensor"),
            P("member", "dp", "tensor"),
            P("member", "dp", "tensor"),
            P("member", None, "tensor", "dp"),
            P("member", None, None),
            P(),
            P(),
            P(None, "dp"),
        ),
        out_specs=(
            P("member", "dp", "tensor"),
            P("member", "dp", "tensor"),
            P("member", "dp", "tensor"),
        ),
        check_vma=False,
    )
```

```python
import math

import jax
import jax.numpy as jnp
from jax import lax
from jax.experimental import pallas as pl
from jax.experimental.pallas import tpu as pltpu
from jax.sharding import PartitionSpec as P

D = 5120
HW = 2560
MEMBERS = 8
ZN = 16
YN = 4
ROWS = 160
COLS = 1280
HALF = 80
TOK = 64
SLOTS = 8
CB = 256
NB = COLS // CB
PAD = 16
CODED = ROWS + PAD
TOP = 32000.0
SPLIT = 3
LAG = 2
SCALING = 1.0 / math.sqrt(HW)

beta_one = 0.9
beta_two = 0.95
norm_eps = 1e-05
adam_eps = 1e-08

MESH = pl.DeviceIdType.MESH
F32 = jnp.float32
BF16 = jnp.bfloat16


def remote(src, dst, send_sem, recv_sem, device):
    return pltpu.make_async_remote_copy(
        src_ref=src,
        dst_ref=dst,
        send_sem=send_sem,
        recv_sem=recv_sem,
        device_id=device,
        device_id_type=MESH,
    )


def encode(values):
    top = jnp.max(jnp.abs(values), axis=0, keepdims=True)
    power = jnp.clip(jnp.ceil(jnp.log2(jnp.maximum(top, 1e-30))), -100.0, 126.0)
    codes = jnp.round(values * (TOP * jnp.exp2(-power)))
    powers = jnp.broadcast_to(power, (PAD, values.shape[1]))
    return jnp.concatenate([codes, powers], axis=0).astype(jnp.int32).astype(jnp.int16)


def decode(coded):
    wide = coded.astype(jnp.int32).astype(F32)
    rows = wide.shape[0] - PAD
    return wide[:rows] * (jnp.exp2(wide[rows : rows + 1]) * (1.0 / TOP))


def gradient_kernel(
    ctx,
    w,
    m,
    v,
    tgt,
    ids,
    gall,
    wall,
    mall,
    vall,
    xbuf,
    wbuf,
    tbuf,
    eye,
    yt,
    gt,
    dyt,
    rows_out,
    rows_in,
    own_out,
    own_in,
    late_out,
    late,
    pbuf,
    c1,
    r1,
    c2,
    r2,
    rout,
    mbuf,
    vbuf,
    mcode,
    vcode,
    idbuf,
    loc,
    in_s,
    in_r,
    z_s,
    z_r,
    e_s,
    e_r,
    o_s,
    o_r,
    l_s,
    l_r,
    st_s,
    st_r,
    x_s,
    x_r,
    y_s,
    y_r,
    y_l,
):
    mem = lax.axis_index("member")
    dp = lax.axis_index("dp")
    ten = lax.axis_index("tensor")
    yy, core = mem // 2, mem % 2
    zz, xl = dp // 2, dp % 2

    def at_z(k):
        return (mem, lax.rem(zz + k, ZN) * 2 + xl, ten)

    def member_at(k):
        return lax.rem(yy + k, YN) * 2 + core

    right, left = at_z(1), at_z(ZN - 1)
    dev_a = (mem, zz * 2 + 1 - xl, ten)
    dev_b = (mem, zz * 2 + 1 - xl, 1 - ten)
    dev_c = (mem, dp, 1 - ten)
    up_m, down_m, far_m = member_at(1), member_at(YN - 1), member_at(2)
    sib_m = yy * 2 + 1 - core
    up, down, sib = (up_m, dp, ten), (down_m, dp, ten), (sib_m, dp, ten)

    own_rows = ctx.at[pl.ds(pl.multiple_of(ten * TOK, TOK), TOK)]
    other_rows = ctx.at[pl.ds(pl.multiple_of((1 - ten) * TOK, TOK), TOK)]

    locals_ = [
        pltpu.make_async_copy(own_rows, xbuf.at[0, 0, 0], loc.at[0]),
        pltpu.make_async_copy(w, wbuf.at[0, 0], loc.at[1]),
        pltpu.make_async_copy(tgt.at[:, xl], tbuf.at[0], loc.at[2]),
        pltpu.make_async_copy(ids, idbuf, loc.at[3]),
    ]
    moments = [
        pltpu.make_async_copy(m, mbuf, loc.at[4]),
        pltpu.make_async_copy(v, vbuf, loc.at[5]),
    ]
    kept = [
        pltpu.make_async_copy(wbuf.at[0, 0], wall.at[mem], loc.at[6]),
        pltpu.make_async_copy(mcode, mall.at[mem], loc.at[7]),
        pltpu.make_async_copy(vcode, vall.at[mem], loc.at[8]),
    ]
    for copy in locals_ + moments:
        copy.start()

    barrier = pltpu.get_barrier_semaphore()

    neighbours = (right, left, dev_a, dev_b, dev_c, up, down, sib)
    for device in neighbours:
        pl.semaphore_signal(barrier, inc=1, device_id=device, device_id_type=MESH)
    pl.semaphore_wait(barrier, len(neighbours))

    swap = remote(other_rows, xbuf.at[1, 0, 0], in_s.at[0], in_r.at[0], dev_c)
    swap.start()

    def ring(h, s, d):
        dst = xbuf.at[h, lax.rem(s + 1, SLOTS), d if d else s // (SLOTS - 1)]
        return remote(
            xbuf.at[h, s, d],
            dst,
            z_s.at[d, h, s],
            z_r.at[d, h, lax.rem(s + 1, SLOTS)],
            left if d else right,
        )

    def first(h, d, src):
        return remote(
            src, xbuf.at[h, 1, d], z_s.at[d, h, 0], z_r.at[d, h, 1], left if d else right
        )

    for d in (0, 1):
        first(0, d, own_rows).start()
    inputs = [
        remote(w, wbuf.at[0, 1], in_s.at[1], in_r.at[1], dev_a),
        remote(w, wbuf.at[1, 1], in_s.at[2], in_r.at[2], dev_b),
        remote(w, wbuf.at[1, 0], in_s.at[3], in_r.at[3], dev_c),
        remote(tgt.at[:, 1 - xl], tbuf.at[1], in_s.at[4], in_r.at[4], dev_a),
    ]

    state = [(w, wall), (mcode, mall), (vcode, vall)]

    def state_first(i, src, dst):
        return [
            remote(src, dst.at[mem], st_s.at[i, 0], st_r.at[i, 0], up),
            remote(src, dst.at[mem], st_s.at[i, 1], st_r.at[i, 1], down),
            remote(src, dst.at[mem], st_s.at[i, 2], st_r.at[i, 2], sib),
        ]

    def state_on(i, dst):
        one, two = dst.at[down_m], dst.at[up_m]
        if i:
            low, high = pl.ds(0, HALF), pl.ds(HALF, CODED - HALF)
            one_low, two_high = one.at[:, low], two.at[:, high]
        else:
            one_low, two_high = one.at[pl.ds(0, HALF)], two.at[pl.ds(HALF, HALF)]
        return [
            remote(one_low, one_low, st_s.at[i, 3], st_r.at[i, 3], up),
            remote(two_high, two_high, st_s.at[i, 4], st_r.at[i, 4], down),
            remote(one, one, st_s.at[i, 5], st_r.at[i, 5], sib),
            remote(two, two, st_s.at[i, 6], st_r.at[i, 6], sib),
        ]

    def state_last(i, dst):
        return remote(dst.at[far_m], dst.at[far_m], st_s.at[i, 7], st_r.at[i, 7], sib)

    for copy in state_first(0, w, wall):
        copy.start()

    eye[...] = (
        lax.broadcasted_iota(jnp.int32, (ROWS, ROWS), 0)
        == lax.broadcasted_iota(jnp.int32, (ROWS, ROWS), 1)
    ).astype(BF16)
    lane = lax.broadcasted_iota(jnp.int32, (1, 2 * TOK), 1)
    low_lanes = lane < TOK

    swap.wait_recv()
    for d in (0, 1):
        first(1, d, xbuf.at[1, 0, 0]).start()
    for copy in inputs:
        copy.start()
    for copy in moments:
        copy.wait()

    def code_moments(j, _):
        cols = pl.ds(pl.multiple_of(j * CB, CB), CB)
        mcode[j] = encode(mbuf[:, cols])
        vcode[j] = encode(vbuf[:, cols])
        return 0

    lax.fori_loop(0, NB, code_moments, 0)
    for i in (1, 2):
        for copy in state_first(i, *state[i]):
            copy.start()
    for copy in locals_:
        copy.wait()
    for copy in kept:
        copy.start()

    def chunks_of(s):
        one = lax.rem(zz - s + ZN, ZN)
        two = lax.rem(zz + jnp.where(s == 0, SLOTS, s), ZN)
        return one, two

    def project(s):
        one, two = chunks_of(s)
        total = None
        for h in (0, 1):
            part = lax.dot_general(
                wbuf[h].reshape(2 * ROWS, COLS),
                xbuf[h, s].reshape(2 * TOK, COLS),
                (((1,), (1,)), ((), ())),
                preferred_element_type=F32,
            )
            total = part if total is None else total + part
        out = total * SCALING
        yt[s] = out
        goal = jnp.concatenate(
            [
                lax.dot_general(
                    eye[...],
                    jnp.concatenate([tbuf[side, one], tbuf[side, two]], axis=0),
                    (((1,), (1,)), ((), ())),
                    preferred_element_type=F32,
                )
                for side in (0, 1)
            ],
            axis=0,
        )
        gt[s] = goal
        squares = jnp.sum(out * out, axis=0, keepdims=True)
        crosses = jnp.sum(goal * out, axis=0, keepdims=True)
        row_one = jnp.where(low_lanes, squares, pltpu.roll(crosses, TOK, 1))
        row_two = jnp.where(low_lanes, pltpu.roll(squares, TOK, 1), crosses)
        return row_one, row_two

    def row_copies(s):
        return [
            remote(
                rows_out.at[2 * s + side],
                rows_in.at[zz],
                e_s.at[2 * s + side],
                e_r.at[zz],
                at_z(s if side else ZN - s),
            )
            for side in (0, 1)
        ]

    def project_early(s, _):
        row_one, row_two = project(s)

        @pl.when(s < SLOTS - 1)
        def _():
            rows_out[2 * s] = row_one
            rows_out[2 * s + 1] = row_two
            for copy in row_copies(s):
                copy.start()

        @pl.when(s == SLOTS - 1)
        def _():
            late_out[pl.ds(2, 1), :] = row_one
            late_out[pl.ds(3, 1), :] = row_two

        return 0

    def done_by(s):
        return jnp.where(s < 5, 0, 2 * (s - 4) + 1)

    def gather_step(s, _):
        for h in (0, 1):
            for d in (0, 1):
                remote(
                    xbuf.at[h, s, d], xbuf.at[h, s, d], z_s.at[d, h, s], z_r.at[d, h, s], right
                ).wait_recv()
                if d == h:
                    ring(h, s, d).start()
                else:

                    @pl.when(s < SLOTS - 1)
                    def _():
                        ring(h, s, d).start()

        @pl.when(s == 5)
        def _():
            for copy in inputs:
                copy.wait_recv()

        @pl.when(s == SLOTS - 2)
        def _():
            for i, (src, dst) in enumerate(state):
                for copy in state_first(i, src, dst):
                    copy.wait_recv()
                for copy in state_on(i, dst):
                    copy.start()

        lax.fori_loop(done_by(s - 1) + 1, done_by(s) + 1, project_early, 0)
        return 0

    lax.fori_loop(1, SLOTS, gather_step, 0)

    def own_copy(k):
        return remote(own_out, own_in.at[zz], o_s.at[k], o_r.at[zz], at_z(k))

    def late_copy(k):
        return remote(late_out, late.at[zz], l_s.at[k], l_r.at[zz], at_z(k))

    def take_row(k, total):
        src = lax.rem(zz + k, ZN)
        remote(own_out, rows_in.at[src], e_s.at[k], e_r.at[src], right).wait_recv()
        return total + rows_in[src]

    total = lax.fori_loop(1, SLOTS - 1, take_row, jnp.zeros((1, 2 * TOK), F32))
    total = lax.fori_loop(SLOTS + 2, ZN, take_row, total)
    own_out[...] = total
    own_in[zz] = total

    def send_own(k, _):
        own_copy(k).start()
        return 0

    lax.fori_loop(1, SLOTS, send_own, 0)
    lax.fori_loop(SLOTS + 1, ZN, send_own, 0)

    for h in (0, 1):
        remote(
            xbuf.at[h, 0, 1], xbuf.at[h, 0, 1], z_s.at[h, h, 0], z_r.at[h, h, 0], right
        ).wait_recv()
    own_copy(SLOTS).start()
    row_one, row_two = project(0)
    late_out[pl.ds(0, 1), :] = row_one
    late_out[pl.ds(1, 1), :] = row_two

    def send_late(i, _):
        away = (i + 1) // 2
        late_copy(SLOTS + away * (1 - 2 * lax.rem(i, 2))).start()
        return 0

    lax.fori_loop(0, ZN - 1, send_late, 0)
    late[zz] = late_out[...]

    for i, (src, dst) in enumerate(state):
        for copy in state_on(i, dst):
            copy.wait_recv()
        state_last(i, dst).start()
    for copy in kept:
        copy.wait()
    swap.wait_send()
    for copy in inputs:
        copy.wait_send()
    for d in (0, 1):
        first(0, d, own_rows).wait_send()
        first(1, d, xbuf.at[1, 0, 0]).wait_send()

    def drain_ring(s, _):
        for h in (0, 1):
            for d in (0, 1):
                if d == h:
                    ring(h, s, d).wait_send()
                else:

                    @pl.when(s < SLOTS - 1)
                    def _():
                        ring(h, s, d).wait_send()

        return 0

    lax.fori_loop(1, SLOTS, drain_ring, 0)

    def drain_rows(s, _):
        for copy in row_copies(s):
            copy.wait_send()
        return 0

    lax.fori_loop(1, SLOTS - 1, drain_rows, 0)

    def take_sums(k, _):
        src = lax.rem(zz + k, ZN)
        remote(own_out, own_in.at[src], o_s.at[k], o_r.at[src], right).wait_recv()
        remote(late_out, late.at[src], l_s.at[k], l_r.at[src], right).wait_recv()
        return 0

    lax.fori_loop(1, ZN, take_sums, 0)

    def total_row(c):
        total = own_in[c]
        for row, behind in enumerate((0, SLOTS, SLOTS - 1, SLOTS + 1)):
            total = total + late[lax.rem(c + behind, ZN), pl.ds(row, 1), :]
        return total

    def window_mask(c):
        row = idbuf[pl.ds(2 * c + xl, 1), :]
        return jnp.where(row != 0, 1.0, 0.0)

    def out_gradient(s, _):
        one, two = chunks_of(s)
        row_one, row_two = total_row(one), total_row(two)
        squares = jnp.where(low_lanes, row_one, pltpu.roll(row_two, TOK, 1))
        crosses = jnp.where(low_lanes, pltpu.roll(row_one, TOK, 1), row_two)
        mask_one, mask_two = window_mask(one), window_mask(two)
        first_half = jnp.where(low_lanes, mask_one, pltpu.roll(mask_two, TOK, 1))
        second_half = jnp.where(low_lanes, pltpu.roll(mask_one, TOK, 1), mask_two)
        mask = jnp.where(ten == 0, first_half, second_half)
        inverse = lax.rsqrt(squares / D + norm_eps)
        projection = mask * (inverse * inverse * squares - inverse * crosses) / D
        grad_out = yt[s] * (inverse * inverse * (mask - projection)) - gt[s] * (inverse * mask)
        dyt[:, pl.ds(pl.multiple_of(s * 2 * TOK, 2 * TOK), 2 * TOK)] = grad_out.astype(BF16)
        return 0

    lax.fori_loop(0, SLOTS, out_gradient, 0)

    low, high = pl.ds(0, HALF), pl.ds(HALF, CODED - HALF)

    def hop_one(j):
        return [
            remote(c1.at[0, j], r1.at[0, j], x_s.at[0, j], x_r.at[0, j], dev_a),
            remote(c1.at[1, j], r1.at[1, j], x_s.at[1, j], x_r.at[1, j], dev_b),
        ]

    def hop_two(j):
        return [
            remote(c2.at[0, j], r2.at[0, j], x_s.at[2, j], x_r.at[2, j], dev_a),
            remote(c2.at[1, j], r2.at[1, j], x_s.at[3, j], x_r.at[3, j], dev_b),
        ]

    def y_local(j):
        return pltpu.make_async_copy(rout.at[j], gall.at[mem, j], y_l.at[j])

    def y_first(j):
        return [
            remote(rout.at[j], gall.at[mem, j], y_s.at[0, j], y_r.at[0, j], up),
            remote(rout.at[j], gall.at[mem, j], y_s.at[1, j], y_r.at[1, j], down),
            remote(rout.at[j], gall.at[mem, j], y_s.at[2, j], y_r.at[2, j], sib),
        ]

    def y_on(j):
        one, two = gall.at[down_m, j], gall.at[up_m, j]
        return [
            remote(one.at[low], one.at[low], y_s.at[3, j], y_r.at[3, j], up),
            remote(two.at[high], two.at[high], y_s.at[4, j], y_r.at[4, j], down),
            remote(one, one, y_s.at[5, j], y_r.at[5, j], sib),
            remote(two, two, y_s.at[6, j], y_r.at[6, j], sib),
        ]

    def y_last(j):
        return remote(gall.at[far_m, j], gall.at[far_m, j], y_s.at[7, j], y_r.at[7, j], sib)

    def stage(step, behind, run):
        j = step - behind

        @pl.when(jnp.logical_and(j >= 0, j < NB))
        def _():
            run(j)

    def multiply(j):
        cols = pl.ds(pl.multiple_of(j * CB, CB), CB)
        for h in (1, 0):
            part = SCALING * jnp.dot(
                dyt[...],
                xbuf[h, :, :, :, cols].reshape(2 * SLOTS * TOK, CB),
                preferred_element_type=F32,
            )
            pbuf[j, h, 1] = part[ROWS:]
            if h:
                c1[0, j] = encode(part[:HALF])
                c1[1, j] = encode(part[HALF:ROWS])
                for copy in hop_one(j):
                    copy.start()
            else:
                pbuf[j, h, 0] = part[:ROWS]

    def add_one(j):
        for copy in hop_one(j):
            copy.wait_recv()
        pbuf[j, 1, 1, :HALF] = pbuf[j, 1, 1, :HALF] + decode(r1[0, j])
        pbuf[j, 0, 1, HALF:] = pbuf[j, 0, 1, HALF:] + decode(r1[1, j])
        c2[0, j] = encode(pbuf[j, 0, 1])
        c2[1, j] = encode(pbuf[j, 1, 1])
        for copy in hop_two(j):
            copy.start()

    def add_two(j):
        for copy in hop_two(j):
            copy.wait_recv()
        rout[j] = encode(pbuf[j, 0, 0] + decode(r2[0, j]) + decode(r2[1, j]))
        y_local(j).start()
        for copy in y_first(j):
            copy.start()

    def pass_on(j):
        for copy in y_first(j):
            copy.wait_recv()
        for copy in y_on(j):
            copy.start()

    def pass_last(j):
        for copy in y_on(j):
            copy.wait_recv()
        y_last(j).start()

    def finish(j):
        y_last(j).wait_recv()
        y_local(j).wait()
        for copy in hop_one(j) + hop_two(j) + y_first(j) + y_on(j) + [y_last(j)]:
            copy.wait_send()

    def drain_stats(k, _):
        own_copy(k).wait_send()
        late_copy(k).wait_send()
        return 0

    def pipeline_step(step, _):
        runs = (multiply, add_one, add_two, pass_on, pass_last, finish)
        for behind in reversed(range(len(runs))):
            stage(step, LAG * behind, runs[behind])

        @pl.when(step == NB)
        def _():
            lax.fori_loop(1, ZN, drain_stats, 0)
            for i, (src, dst) in enumerate(state):
                state_last(i, dst).wait_recv()
                for copy in state_first(i, src, dst) + state_on(i, dst) + [state_last(i, dst)]:
                    copy.wait_send()

        return 0

    lax.fori_loop(0, NB + 5 * LAG, pipeline_step, 0)


def gather_gradients(ctx, w, m, v, tgt, ids):
    anywhere = pl.BlockSpec(memory_space=pl.ANY)
    dma = pltpu.SemaphoreType.DMA
    vmem = pltpu.VMEM
    return pl.pallas_call(
        gradient_kernel,
        out_shape=(
            jax.ShapeDtypeStruct((MEMBERS, NB, CODED, CB), jnp.int16),
            jax.ShapeDtypeStruct((MEMBERS, ROWS, COLS), BF16),
            jax.ShapeDtypeStruct((MEMBERS, NB, CODED, CB), jnp.int16),
            jax.ShapeDtypeStruct((MEMBERS, NB, CODED, CB), jnp.int16),
        ),
        in_specs=[anywhere] * 6,
        out_specs=(anywhere,) * 4,
        scratch_shapes=[
            vmem((2, SLOTS, 2, TOK, COLS), BF16),
            vmem((2, 2, ROWS, COLS), BF16),
            vmem((2, ZN, TOK, ROWS), BF16),
            vmem((ROWS, ROWS), BF16),
            vmem((SLOTS, 2 * ROWS, 2 * TOK), F32),
            vmem((SLOTS, 2 * ROWS, 2 * TOK), F32),
            vmem((2 * ROWS, SLOTS * 2 * TOK), BF16),
            vmem((2 * SLOTS, 1, 2 * TOK), F32),
            vmem((ZN, 1, 2 * TOK), F32),
            vmem((1, 2 * TOK), F32),
            vmem((ZN, 1, 2 * TOK), F32),
            vmem((4, 2 * TOK), F32),
            vmem((ZN, 4, 2 * TOK), F32),
            vmem((NB, 2, 2, ROWS, CB), F32),
            vmem((2, NB, HALF + PAD, CB), jnp.int16),
            vmem((2, NB, HALF + PAD, CB), jnp.int16),
            vmem((2, NB, CODED, CB), jnp.int16),
            vmem((2, NB, CODED, CB), jnp.int16),
            vmem((NB, CODED, CB), jnp.int16),
            vmem((ROWS, COLS), F32),
            vmem((ROWS, COLS), F32),
            vmem((NB, CODED, CB), jnp.int16),
            vmem((NB, CODED, CB), jnp.int16),
            vmem((2 * ZN, 2 * TOK), jnp.int32),
            dma((9,)),
            dma((5,)),
            dma((5,)),
            dma((2, 2, SLOTS)),
            dma((2, 2, SLOTS)),
            dma((ZN,)),
            dma((ZN,)),
            dma((ZN,)),
            dma((ZN,)),
            dma((ZN,)),
            dma((ZN,)),
            dma((3, 8)),
            dma((3, 8)),
            dma((4, NB)),
            dma((4, NB)),
            dma((8, NB)),
            dma((8, NB)),
            dma((NB,)),
        ],
        compiler_params=pltpu.CompilerParams(
            collective_id=0, has_side_effects=True, vmem_limit_bytes=56 * 1024 * 1024
        ),
        cost_estimate=pl.CostEstimate(
            flops=4 * 1024 * HW * 2 * ROWS, bytes_accessed=20_000_000, transcendentals=0
        ),
    )(ctx, w, m, v, tgt, ids)


def update_kernel(
    partner, rates, levels, gall, wall, mall, vall, new_w, new_m, new_v,
    gbuf, wbuf, mbuf, vbuf, wout, mout, vout, in_sem, out_sem,
):
    p = partner[lax.axis_index("member")]

    spans = [(0, SPLIT), (SPLIT, NB)]

    def take(part):
        low, high = spans[part]
        blocks, cols = pl.ds(low, high - low), pl.ds(low * CB, (high - low) * CB)
        return [
            pltpu.make_async_copy(gall.at[p, blocks], gbuf.at[blocks], in_sem.at[0, part]),
            pltpu.make_async_copy(mall.at[p, blocks], mbuf.at[blocks], in_sem.at[1, part]),
            pltpu.make_async_copy(vall.at[p, blocks], vbuf.at[blocks], in_sem.at[2, part]),
            pltpu.make_async_copy(wall.at[p, :, cols], wbuf.at[:, cols], in_sem.at[3, part]),
        ]

    def give(part):
        low, high = spans[part]
        cols = pl.ds(low * CB, (high - low) * CB)
        return [
            pltpu.make_async_copy(mout.at[:, cols], new_m.at[:, cols], out_sem.at[0, part]),
            pltpu.make_async_copy(vout.at[:, cols], new_v.at[:, cols], out_sem.at[1, part]),
            pltpu.make_async_copy(wout.at[:, cols], new_w.at[:, cols], out_sem.at[2, part]),
        ]

    for part in (0, 1):
        for copy in take(part):
            copy.start()
    level = jnp.full((1, CB), levels[p].astype(F32), F32)
    step_size = rates[p] * 2.0 ** ((level - 4.0) / 4.0)
    for part in (0, 1):
        for copy in take(part):
            copy.wait()
        for j in range(*spans[part]):
            cols = slice(j * CB, (j + 1) * CB)
            gradient = decode(gbuf[j])
            first = beta_one * decode(mbuf[j]) + (1.0 - beta_one) * gradient
            second = beta_two * decode(vbuf[j]) + (1.0 - beta_two) * gradient * gradient
            mout[:, cols] = first
            vout[:, cols] = second
            wout[:, cols] = (
                wbuf[:, cols].astype(F32) - step_size * first / (jnp.sqrt(second) + adam_eps)
            ).astype(BF16)
        for copy in give(part):
            copy.start()
    for part in (0, 1):
        for copy in give(part):
            copy.wait()


def update(partner, base_lr, perturb_index, gall, wall, mall, vall):
    smem = pl.BlockSpec(memory_space=pltpu.SMEM)
    anywhere = pl.BlockSpec(memory_space=pl.ANY)
    coded = pltpu.VMEM((NB, CODED, CB), jnp.int16)
    return pl.pallas_call(
        update_kernel,
        out_shape=(
            jax.ShapeDtypeStruct((ROWS, COLS), BF16),
            jax.ShapeDtypeStruct((ROWS, COLS), F32),
            jax.ShapeDtypeStruct((ROWS, COLS), F32),
        ),
        in_specs=[smem] * 3 + [anywhere] * 4,
        out_specs=(anywhere,) * 3,
        scratch_shapes=[
            coded,
            pltpu.VMEM((ROWS, COLS), BF16),
            coded,
            coded,
            pltpu.VMEM((ROWS, COLS), BF16),
            pltpu.VMEM((ROWS, COLS), F32),
            pltpu.VMEM((ROWS, COLS), F32),
            pltpu.SemaphoreType.DMA((4, 2)),
            pltpu.SemaphoreType.DMA((3, 2)),
        ],
        compiler_params=pltpu.CompilerParams(vmem_limit_bytes=56 * 1024 * 1024),
    )(partner, base_lr, perturb_index, gall, wall, mall, vall)


def body(
    context,
    out_weight,
    first_moment,
    second_moment,
    target,
    token_ids,
    base_lr,
    perturb_index,
    partner,
):
    gall, wall, mall, vall = gather_gradients(
        context[0, 0],
        out_weight[0],
        first_moment[0],
        second_moment[0],
        target[0].reshape(ZN, 2, TOK, ROWS),
        token_ids[0],
    )
    new_weight, new_first, new_second = update(
        partner.reshape(MEMBERS), base_lr, perturb_index, gall, wall, mall, vall
    )
    return (new_weight[None], new_first[None], new_second[None])


def solution(mesh):
    return jax.shard_map(
        body,
        mesh=mesh,
        in_specs=(
            P("member", "dp", None, "tensor"),
            P("member", "dp", "tensor"),
            P("member", "dp", "tensor"),
            P("member", "dp", "tensor"),
            P("member", None, "tensor", "dp"),
            P("member", None, None),
            P(),
            P(),
            P(None, "dp"),
        ),
        out_specs=(
            P("member", "dp", "tensor"),
            P("member", "dp", "tensor"),
            P("member", "dp", "tensor"),
        ),
        check_vma=False,
    )
```

```python
import math

import jax
import jax.numpy as jnp
from jax import lax
from jax.experimental import pallas as pl
from jax.experimental.pallas import tpu as pltpu
from jax.sharding import PartitionSpec as P

D = 5120
HW = 2560
MEMBERS = 8
ZN = 16
YN = 4
ROWS = 160
COLS = 1280
HALF = 80
TOK = 64
SLOTS = 8
CB = 256
NB = COLS // CB
PAD = 16
CODED = ROWS + PAD
TOP = 32000.0
SPLIT = 3
LAG = 2
SCALING = 1.0 / math.sqrt(HW)

beta_one = 0.9
beta_two = 0.95
norm_eps = 1e-05
adam_eps = 1e-08

MESH = pl.DeviceIdType.MESH
F32 = jnp.float32
BF16 = jnp.bfloat16


def remote(src, dst, send_sem, recv_sem, device):
    return pltpu.make_async_remote_copy(
        src_ref=src,
        dst_ref=dst,
        send_sem=send_sem,
        recv_sem=recv_sem,
        device_id=device,
        device_id_type=MESH,
    )


def encode(values):
    top = jnp.max(jnp.abs(values), axis=0, keepdims=True)
    power = jnp.clip(jnp.ceil(jnp.log2(jnp.maximum(top, 1e-30))), -100.0, 126.0)
    codes = jnp.round(values * (TOP * jnp.exp2(-power)))
    powers = jnp.broadcast_to(power, (PAD, values.shape[1]))
    return jnp.concatenate([codes, powers], axis=0).astype(jnp.int32).astype(jnp.int16)


def decode(coded):
    wide = coded.astype(jnp.int32).astype(F32)
    rows = wide.shape[0] - PAD
    return wide[:rows] * (jnp.exp2(wide[rows : rows + 1]) * (1.0 / TOP))


def gradient_kernel(
    ctx,
    w,
    m,
    v,
    tgt,
    ids,
    gall,
    wall,
    mall,
    vall,
    xbuf,
    wbuf,
    tbuf,
    eye,
    yt,
    gt,
    dyt,
    rows_out,
    rows_in,
    own_out,
    own_in,
    late_out,
    late,
    pbuf,
    c1,
    r1,
    c2,
    r2,
    rout,
    mbuf,
    vbuf,
    mcode,
    vcode,
    idbuf,
    loc,
    in_s,
    in_r,
    z_s,
    z_r,
    e_s,
    e_r,
    o_s,
    o_r,
    l_s,
    l_r,
    st_s,
    st_r,
    x_s,
    x_r,
    y_s,
    y_r,
    y_l,
):
    mem = lax.axis_index("member")
    dp = lax.axis_index("dp")
    ten = lax.axis_index("tensor")
    yy, core = mem // 2, mem % 2
    zz, xl = dp // 2, dp % 2

    def at_z(k):
        return (mem, lax.rem(zz + k, ZN) * 2 + xl, ten)

    def member_at(k):
        return lax.rem(yy + k, YN) * 2 + core

    right, left = at_z(1), at_z(ZN - 1)
    dev_a = (mem, zz * 2 + 1 - xl, ten)
    dev_b = (mem, zz * 2 + 1 - xl, 1 - ten)
    dev_c = (mem, dp, 1 - ten)
    up_m, down_m, far_m = member_at(1), member_at(YN - 1), member_at(2)
    sib_m = yy * 2 + 1 - core
    up, down, sib = (up_m, dp, ten), (down_m, dp, ten), (sib_m, dp, ten)

    own_rows = ctx.at[pl.ds(pl.multiple_of(ten * TOK, TOK), TOK)]
    other_rows = ctx.at[pl.ds(pl.multiple_of((1 - ten) * TOK, TOK), TOK)]

    locals_ = [
        pltpu.make_async_copy(own_rows, xbuf.at[0, 0, 0], loc.at[0]),
        pltpu.make_async_copy(w, wbuf.at[0, 0], loc.at[1]),
        pltpu.make_async_copy(tgt.at[:, xl], tbuf.at[0], loc.at[2]),
        pltpu.make_async_copy(ids, idbuf, loc.at[3]),
    ]
    moments = [
        pltpu.make_async_copy(m, mbuf, loc.at[4]),
        pltpu.make_async_copy(v, vbuf, loc.at[5]),
    ]
    kept = [
        pltpu.make_async_copy(wbuf.at[0, 0], wall.at[mem], loc.at[6]),
        pltpu.make_async_copy(mcode, mall.at[mem], loc.at[7]),
        pltpu.make_async_copy(vcode, vall.at[mem], loc.at[8]),
    ]
    for copy in locals_ + moments:
        copy.start()

    barrier = pltpu.get_barrier_semaphore()

    neighbours = (right, left, dev_a, dev_b, dev_c, up, down, sib)
    for device in neighbours:
        pl.semaphore_signal(barrier, inc=1, device_id=device, device_id_type=MESH)
    pl.semaphore_wait(barrier, len(neighbours))

    swap = remote(other_rows, xbuf.at[1, 0, 0], in_s.at[0], in_r.at[0], dev_c)
    swap.start()

    def ring(h, s, d):
        dst = xbuf.at[h, lax.rem(s + 1, SLOTS), d if d else s // (SLOTS - 1)]
        return remote(
            xbuf.at[h, s, d],
            dst,
            z_s.at[d, h, s],
            z_r.at[d, h, lax.rem(s + 1, SLOTS)],
            left if d else right,
        )

    def first(h, d, src):
        return remote(
            src, xbuf.at[h, 1, d], z_s.at[d, h, 0], z_r.at[d, h, 1], left if d else right
        )

    for d in (0, 1):
        first(0, d, own_rows).start()
    inputs = [
        remote(w, wbuf.at[0, 1], in_s.at[1], in_r.at[1], dev_a),
        remote(w, wbuf.at[1, 1], in_s.at[2], in_r.at[2], dev_b),
        remote(w, wbuf.at[1, 0], in_s.at[3], in_r.at[3], dev_c),
        remote(tgt.at[:, 1 - xl], tbuf.at[1], in_s.at[4], in_r.at[4], dev_a),
    ]
    for copy in inputs:
        copy.start()

    state = [(w, wall), (mcode, mall), (vcode, vall)]

    def state_first(i, src, dst):
        return [
            remote(src, dst.at[mem], st_s.at[i, 0], st_r.at[i, 0], up),
            remote(src, dst.at[mem], st_s.at[i, 1], st_r.at[i, 1], down),
            remote(src, dst.at[mem], st_s.at[i, 2], st_r.at[i, 2], sib),
        ]

    def state_on(i, dst):
        one, two = dst.at[down_m], dst.at[up_m]
        if i:
            low, high = pl.ds(0, HALF), pl.ds(HALF, CODED - HALF)
            one_low, two_high = one.at[:, low], two.at[:, high]
        else:
            one_low, two_high = one.at[pl.ds(0, HALF)], two.at[pl.ds(HALF, HALF)]
        return [
            remote(one_low, one_low, st_s.at[i, 3], st_r.at[i, 3], up),
            remote(two_high, two_high, st_s.at[i, 4], st_r.at[i, 4], down),
            remote(one, one, st_s.at[i, 5], st_r.at[i, 5], sib),
            remote(two, two, st_s.at[i, 6], st_r.at[i, 6], sib),
        ]

    def state_last(i, dst):
        return remote(dst.at[far_m], dst.at[far_m], st_s.at[i, 7], st_r.at[i, 7], sib)

    for copy in state_first(0, w, wall):
        copy.start()

    eye[...] = (
        lax.broadcasted_iota(jnp.int32, (ROWS, ROWS), 0)
        == lax.broadcasted_iota(jnp.int32, (ROWS, ROWS), 1)
    ).astype(BF16)
    lane = lax.broadcasted_iota(jnp.int32, (1, 2 * TOK), 1)
    low_lanes = lane < TOK

    swap.wait_recv()
    for d in (0, 1):
        first(1, d, xbuf.at[1, 0, 0]).start()
    for copy in moments:
        copy.wait()

    def code_moments(j, _):
        cols = pl.ds(pl.multiple_of(j * CB, CB), CB)
        mcode[j] = encode(mbuf[:, cols])
        vcode[j] = encode(vbuf[:, cols])
        return 0

    lax.fori_loop(0, NB, code_moments, 0)
    for i in (1, 2):
        for copy in state_first(i, *state[i]):
            copy.start()
    for copy in locals_:
        copy.wait()
    for copy in kept:
        copy.start()

    def chunks_of(s):
        one = lax.rem(zz - s + ZN, ZN)
        two = lax.rem(zz + jnp.where(s == 0, SLOTS, s), ZN)
        return one, two

    def project(s):
        one, two = chunks_of(s)
        total = None
        for h in (0, 1):
            part = lax.dot_general(
                wbuf[h].reshape(2 * ROWS, COLS),
                xbuf[h, s].reshape(2 * TOK, COLS),
                (((1,), (1,)), ((), ())),
                preferred_element_type=F32,
            )
            total = part if total is None else total + part
        out = total * SCALING
        yt[s] = out
        goal = jnp.concatenate(
            [
                lax.dot_general(
                    eye[...],
                    jnp.concatenate([tbuf[side, one], tbuf[side, two]], axis=0),
                    (((1,), (1,)), ((), ())),
                    preferred_element_type=F32,
                )
                for side in (0, 1)
            ],
            axis=0,
        )
        gt[s] = goal
        squares = jnp.sum(out * out, axis=0, keepdims=True)
        crosses = jnp.sum(goal * out, axis=0, keepdims=True)
        row_one = jnp.where(low_lanes, squares, pltpu.roll(crosses, TOK, 1))
        row_two = jnp.where(low_lanes, pltpu.roll(squares, TOK, 1), crosses)
        return row_one, row_two

    def row_copies(s):
        return [
            remote(
                rows_out.at[2 * s + side],
                rows_in.at[zz],
                e_s.at[2 * s + side],
                e_r.at[zz],
                at_z(s if side else ZN - s),
            )
            for side in (0, 1)
        ]

    def project_early(s, _):
        row_one, row_two = project(s)

        @pl.when(s < SLOTS - 1)
        def _():
            rows_out[2 * s] = row_one
            rows_out[2 * s + 1] = row_two
            for copy in row_copies(s):
                copy.start()

        @pl.when(s == SLOTS - 1)
        def _():
            late_out[pl.ds(2, 1), :] = row_one
            late_out[pl.ds(3, 1), :] = row_two

        return 0

    def done_by(s):
        return jnp.where(s < 5, 0, 2 * (s - 4) + 1)

    def gather_step(s, _):
        for h in (0, 1):
            for d in (0, 1):
                remote(
                    xbuf.at[h, s, d], xbuf.at[h, s, d], z_s.at[d, h, s], z_r.at[d, h, s], right
                ).wait_recv()
                if d == h:
                    ring(h, s, d).start()
                else:

                    @pl.when(s < SLOTS - 1)
                    def _():
                        ring(h, s, d).start()

        @pl.when(s == 5)
        def _():
            for copy in inputs:
                copy.wait_recv()

        @pl.when(s == SLOTS - 2)
        def _():
            for i, (src, dst) in enumerate(state):
                for copy in state_first(i, src, dst):
                    copy.wait_recv()
                for copy in state_on(i, dst):
                    copy.start()

        lax.fori_loop(done_by(s - 1) + 1, done_by(s) + 1, project_early, 0)
        return 0

    lax.fori_loop(1, SLOTS, gather_step, 0)

    def own_copy(k):
        return remote(own_out, own_in.at[zz], o_s.at[k], o_r.at[zz], at_z(k))

    def late_copy(k):
        return remote(late_out, late.at[zz], l_s.at[k], l_r.at[zz], at_z(k))

    def take_row(k, total):
        src = lax.rem(zz + k, ZN)
        remote(own_out, rows_in.at[src], e_s.at[k], e_r.at[src], right).wait_recv()
        return total + rows_in[src]

    total = lax.fori_loop(1, SLOTS - 1, take_row, jnp.zeros((1, 2 * TOK), F32))
    total = lax.fori_loop(SLOTS + 2, ZN, take_row, total)
    own_out[...] = total
    own_in[zz] = total

    def send_own(k, _):
        own_copy(k).start()
        return 0

    lax.fori_loop(1, SLOTS, send_own, 0)
    lax.fori_loop(SLOTS + 1, ZN, send_own, 0)

    for h in (0, 1):
        remote(
            xbuf.at[h, 0, 1], xbuf.at[h, 0, 1], z_s.at[h, h, 0], z_r.at[h, h, 0], right
        ).wait_recv()
    own_copy(SLOTS).start()
    row_one, row_two = project(0)
    late_out[pl.ds(0, 1), :] = row_one
    late_out[pl.ds(1, 1), :] = row_two

    def send_late(i, _):
        away = (i + 1) // 2
        late_copy(SLOTS + away * (1 - 2 * lax.rem(i, 2))).start()
        return 0

    lax.fori_loop(0, ZN - 1, send_late, 0)
    late[zz] = late_out[...]

    for i, (src, dst) in enumerate(state):
        for copy in state_on(i, dst):
            copy.wait_recv()
        state_last(i, dst).start()
    for copy in kept:
        copy.wait()
    swap.wait_send()
    for copy in inputs:
        copy.wait_send()
    for d in (0, 1):
        first(0, d, own_rows).wait_send()
        first(1, d, xbuf.at[1, 0, 0]).wait_send()

    def drain_ring(s, _):
        for h in (0, 1):
            for d in (0, 1):
                if d == h:
                    ring(h, s, d).wait_send()
                else:

                    @pl.when(s < SLOTS - 1)
                    def _():
                        ring(h, s, d).wait_send()

        return 0

    lax.fori_loop(1, SLOTS, drain_ring, 0)

    def drain_rows(s, _):
        for copy in row_copies(s):
            copy.wait_send()
        return 0

    lax.fori_loop(1, SLOTS - 1, drain_rows, 0)

    def take_sums(k, _):
        src = lax.rem(zz + k, ZN)
        remote(own_out, own_in.at[src], o_s.at[k], o_r.at[src], right).wait_recv()
        remote(late_out, late.at[src], l_s.at[k], l_r.at[src], right).wait_recv()
        return 0

    lax.fori_loop(1, ZN, take_sums, 0)

    def total_row(c):
        total = own_in[c]
        for row, behind in enumerate((0, SLOTS, SLOTS - 1, SLOTS + 1)):
            total = total + late[lax.rem(c + behind, ZN), pl.ds(row, 1), :]
        return total

    def window_mask(c):
        row = idbuf[pl.ds(2 * c + xl, 1), :]
        return jnp.where(row != 0, 1.0, 0.0)

    def out_gradient(s, _):
        one, two = chunks_of(s)
        row_one, row_two = total_row(one), total_row(two)
        squares = jnp.where(low_lanes, row_one, pltpu.roll(row_two, TOK, 1))
        crosses = jnp.where(low_lanes, pltpu.roll(row_one, TOK, 1), row_two)
        mask_one, mask_two = window_mask(one), window_mask(two)
        first_half = jnp.where(low_lanes, mask_one, pltpu.roll(mask_two, TOK, 1))
        second_half = jnp.where(low_lanes, pltpu.roll(mask_one, TOK, 1), mask_two)
        mask = jnp.where(ten == 0, first_half, second_half)
        inverse = lax.rsqrt(squares / D + norm_eps)
        projection = mask * (inverse * inverse * squares - inverse * crosses) / D
        grad_out = yt[s] * (inverse * inverse * (mask - projection)) - gt[s] * (inverse * mask)
        dyt[:, pl.ds(pl.multiple_of(s * 2 * TOK, 2 * TOK), 2 * TOK)] = grad_out.astype(BF16)
        return 0

    lax.fori_loop(0, SLOTS, out_gradient, 0)

    low, high = pl.ds(0, HALF), pl.ds(HALF, CODED - HALF)

    def hop_one(j):
        return [
            remote(c1.at[0, j], r1.at[0, j], x_s.at[0, j], x_r.at[0, j], dev_a),
            remote(c1.at[1, j], r1.at[1, j], x_s.at[1, j], x_r.at[1, j], dev_b),
        ]

    def hop_two(j):
        return [
            remote(c2.at[0, j], r2.at[0, j], x_s.at[2, j], x_r.at[2, j], dev_a),
            remote(c2.at[1, j], r2.at[1, j], x_s.at[3, j], x_r.at[3, j], dev_b),
        ]

    def y_local(j):
        return pltpu.make_async_copy(rout.at[j], gall.at[mem, j], y_l.at[j])

    def y_first(j):
        return [
            remote(rout.at[j], gall.at[mem, j], y_s.at[0, j], y_r.at[0, j], up),
            remote(rout.at[j], gall.at[mem, j], y_s.at[1, j], y_r.at[1, j], down),
            remote(rout.at[j], gall.at[mem, j], y_s.at[2, j], y_r.at[2, j], sib),
        ]

    def y_on(j):
        one, two = gall.at[down_m, j], gall.at[up_m, j]
        return [
            remote(one.at[low], one.at[low], y_s.at[3, j], y_r.at[3, j], up),
            remote(two.at[high], two.at[high], y_s.at[4, j], y_r.at[4, j], down),
            remote(one, one, y_s.at[5, j], y_r.at[5, j], sib),
            remote(two, two, y_s.at[6, j], y_r.at[6, j], sib),
        ]

    def y_last(j):
        return remote(gall.at[far_m, j], gall.at[far_m, j], y_s.at[7, j], y_r.at[7, j], sib)

    def stage(step, behind, run):
        j = step - behind

        @pl.when(jnp.logical_and(j >= 0, j < NB))
        def _():
            run(j)

    def multiply(j):
        cols = pl.ds(pl.multiple_of(j * CB, CB), CB)
        for h in (1, 0):
            part = SCALING * jnp.dot(
                dyt[...],
                xbuf[h, :, :, :, cols].reshape(2 * SLOTS * TOK, CB),
                preferred_element_type=F32,
            )
            pbuf[j, h, 1] = part[ROWS:]
            if h:
                c1[0, j] = encode(part[:HALF])
                c1[1, j] = encode(part[HALF:ROWS])
                for copy in hop_one(j):
                    copy.start()
            else:
                pbuf[j, h, 0] = part[:ROWS]

    def add_one(j):
        for copy in hop_one(j):
            copy.wait_recv()
        pbuf[j, 1, 1, :HALF] = pbuf[j, 1, 1, :HALF] + decode(r1[0, j])
        pbuf[j, 0, 1, HALF:] = pbuf[j, 0, 1, HALF:] + decode(r1[1, j])
        c2[0, j] = encode(pbuf[j, 0, 1])
        c2[1, j] = encode(pbuf[j, 1, 1])
        for copy in hop_two(j):
            copy.start()

    def add_two(j):
        for copy in hop_two(j):
            copy.wait_recv()
        rout[j] = encode(pbuf[j, 0, 0] + decode(r2[0, j]) + decode(r2[1, j]))
        y_local(j).start()
        for copy in y_first(j):
            copy.start()

    def pass_on(j):
        for copy in y_first(j):
            copy.wait_recv()
        for copy in y_on(j):
            copy.start()

    def pass_last(j):
        for copy in y_on(j):
            copy.wait_recv()
        y_last(j).start()

    def finish(j):
        y_last(j).wait_recv()
        y_local(j).wait()
        for copy in hop_one(j) + hop_two(j) + y_first(j) + y_on(j) + [y_last(j)]:
            copy.wait_send()

    def drain_stats(k, _):
        own_copy(k).wait_send()
        late_copy(k).wait_send()
        return 0

    def pipeline_step(step, _):
        runs = (multiply, add_one, add_two, pass_on, pass_last, finish)
        for behind in reversed(range(len(runs))):
            stage(step, LAG * behind, runs[behind])

        @pl.when(step == NB)
        def _():
            lax.fori_loop(1, ZN, drain_stats, 0)
            for i, (src, dst) in enumerate(state):
                state_last(i, dst).wait_recv()
                for copy in state_first(i, src, dst) + state_on(i, dst) + [state_last(i, dst)]:
                    copy.wait_send()

        return 0

    lax.fori_loop(0, NB + 5 * LAG, pipeline_step, 0)


def gather_gradients(ctx, w, m, v, tgt, ids):
    anywhere = pl.BlockSpec(memory_space=pl.ANY)
    dma = pltpu.SemaphoreType.DMA
    vmem = pltpu.VMEM
    return pl.pallas_call(
        gradient_kernel,
        out_shape=(
            jax.ShapeDtypeStruct((MEMBERS, NB, CODED, CB), jnp.int16),
            jax.ShapeDtypeStruct((MEMBERS, ROWS, COLS), BF16),
            jax.ShapeDtypeStruct((MEMBERS, NB, CODED, CB), jnp.int16),
            jax.ShapeDtypeStruct((MEMBERS, NB, CODED, CB), jnp.int16),
        ),
        in_specs=[anywhere] * 6,
        out_specs=(anywhere,) * 4,
        scratch_shapes=[
            vmem((2, SLOTS, 2, TOK, COLS), BF16),
            vmem((2, 2, ROWS, COLS), BF16),
            vmem((2, ZN, TOK, ROWS), BF16),
            vmem((ROWS, ROWS), BF16),
            vmem((SLOTS, 2 * ROWS, 2 * TOK), F32),
            vmem((SLOTS, 2 * ROWS, 2 * TOK), F32),
            vmem((2 * ROWS, SLOTS * 2 * TOK), BF16),
            vmem((2 * SLOTS, 1, 2 * TOK), F32),
            vmem((ZN, 1, 2 * TOK), F32),
            vmem((1, 2 * TOK), F32),
            vmem((ZN, 1, 2 * TOK), F32),
            vmem((4, 2 * TOK), F32),
            vmem((ZN, 4, 2 * TOK), F32),
            vmem((NB, 2, 2, ROWS, CB), F32),
            vmem((2, NB, HALF + PAD, CB), jnp.int16),
            vmem((2, NB, HALF + PAD, CB), jnp.int16),
            vmem((2, NB, CODED, CB), jnp.int16),
            vmem((2, NB, CODED, CB), jnp.int16),
            vmem((NB, CODED, CB), jnp.int16),
            vmem((ROWS, COLS), F32),
            vmem((ROWS, COLS), F32),
            vmem((NB, CODED, CB), jnp.int16),
            vmem((NB, CODED, CB), jnp.int16),
            vmem((2 * ZN, 2 * TOK), jnp.int32),
            dma((9,)),
            dma((5,)),
            dma((5,)),
            dma((2, 2, SLOTS)),
            dma((2, 2, SLOTS)),
            dma((ZN,)),
            dma((ZN,)),
            dma((ZN,)),
            dma((ZN,)),
            dma((ZN,)),
            dma((ZN,)),
            dma((3, 8)),
            dma((3, 8)),
            dma((4, NB)),
            dma((4, NB)),
            dma((8, NB)),
            dma((8, NB)),
            dma((NB,)),
        ],
        compiler_params=pltpu.CompilerParams(
            collective_id=0, has_side_effects=True, vmem_limit_bytes=56 * 1024 * 1024
        ),
        cost_estimate=pl.CostEstimate(
            flops=4 * 1024 * HW * 2 * ROWS, bytes_accessed=20_000_000, transcendentals=0
        ),
    )(ctx, w, m, v, tgt, ids)


def update_kernel(
    partner, rates, levels, gall, wall, mall, vall, new_w, new_m, new_v,
    gbuf, wbuf, mbuf, vbuf, wout, mout, vout, in_sem, out_sem,
):
    p = partner[lax.axis_index("member")]

    spans = [(0, SPLIT), (SPLIT, NB)]

    def take(part):
        low, high = spans[part]
        blocks, cols = pl.ds(low, high - low), pl.ds(low * CB, (high - low) * CB)
        return [
            pltpu.make_async_copy(gall.at[p, blocks], gbuf.at[blocks], in_sem.at[0, part]),
            pltpu.make_async_copy(mall.at[p, blocks], mbuf.at[blocks], in_sem.at[1, part]),
            pltpu.make_async_copy(vall.at[p, blocks], vbuf.at[blocks], in_sem.at[2, part]),
            pltpu.make_async_copy(wall.at[p, :, cols], wbuf.at[:, cols], in_sem.at[3, part]),
        ]

    def give(part):
        low, high = spans[part]
        cols = pl.ds(low * CB, (high - low) * CB)
        return [
            pltpu.make_async_copy(mout.at[:, cols], new_m.at[:, cols], out_sem.at[0, part]),
            pltpu.make_async_copy(vout.at[:, cols], new_v.at[:, cols], out_sem.at[1, part]),
            pltpu.make_async_copy(wout.at[:, cols], new_w.at[:, cols], out_sem.at[2, part]),
        ]

    for part in (0, 1):
        for copy in take(part):
            copy.start()
    level = jnp.full((1, CB), levels[p].astype(F32), F32)
    step_size = rates[p] * 2.0 ** ((level - 4.0) / 4.0)
    for part in (0, 1):
        for copy in take(part):
            copy.wait()
        for j in range(*spans[part]):
            cols = slice(j * CB, (j + 1) * CB)
            gradient = decode(gbuf[j])
            first = beta_one * decode(mbuf[j]) + (1.0 - beta_one) * gradient
            second = beta_two * decode(vbuf[j]) + (1.0 - beta_two) * gradient * gradient
            mout[:, cols] = first
            vout[:, cols] = second
            wout[:, cols] = (
                wbuf[:, cols].astype(F32) - step_size * first / (jnp.sqrt(second) + adam_eps)
            ).astype(BF16)
        for copy in give(part):
            copy.start()
    for part in (0, 1):
        for copy in give(part):
            copy.wait()


def update(partner, base_lr, perturb_index, gall, wall, mall, vall):
    smem = pl.BlockSpec(memory_space=pltpu.SMEM)
    anywhere = pl.BlockSpec(memory_space=pl.ANY)
    coded = pltpu.VMEM((NB, CODED, CB), jnp.int16)
    return pl.pallas_call(
        update_kernel,
        out_shape=(
            jax.ShapeDtypeStruct((ROWS, COLS), BF16),
            jax.ShapeDtypeStruct((ROWS, COLS), F32),
            jax.ShapeDtypeStruct((ROWS, COLS), F32),
        ),
        in_specs=[smem] * 3 + [anywhere] * 4,
        out_specs=(anywhere,) * 3,
        scratch_shapes=[
            coded,
            pltpu.VMEM((ROWS, COLS), BF16),
            coded,
            coded,
            pltpu.VMEM((ROWS, COLS), BF16),
            pltpu.VMEM((ROWS, COLS), F32),
            pltpu.VMEM((ROWS, COLS), F32),
            pltpu.SemaphoreType.DMA((4, 2)),
            pltpu.SemaphoreType.DMA((3, 2)),
        ],
        compiler_params=pltpu.CompilerParams(vmem_limit_bytes=56 * 1024 * 1024),
    )(partner, base_lr, perturb_index, gall, wall, mall, vall)


def body(
    context,
    out_weight,
    first_moment,
    second_moment,
    target,
    token_ids,
    base_lr,
    perturb_index,
    partner,
):
    gall, wall, mall, vall = gather_gradients(
        context[0, 0],
        out_weight[0],
        first_moment[0],
        second_moment[0],
        target[0].reshape(ZN, 2, TOK, ROWS),
        token_ids[0],
    )
    new_weight, new_first, new_second = update(
        partner.reshape(MEMBERS), base_lr, perturb_index, gall, wall, mall, vall
    )
    return (new_weight[None], new_first[None], new_second[None])


def solution(mesh):
    return jax.shard_map(
        body,
        mesh=mesh,
        in_specs=(
            P("member", "dp", None, "tensor"),
            P("member", "dp", "tensor"),
            P("member", "dp", "tensor"),
            P("member", "dp", "tensor"),
            P("member", None, "tensor", "dp"),
            P("member", None, None),
            P(),
            P(),
            P(None, "dp"),
        ),
        out_specs=(
            P("member", "dp", "tensor"),
            P("member", "dp", "tensor"),
            P("member", "dp", "tensor"),
        ),
        check_vma=False,
    )
```
